32 devices in a mesh: groups: 2 (over y), mem: 4 (over x, core), heads: 4 (over z).
Axes of the slice: x: 2, y: 2, z: 4, core: 2. Of those that a mesh axis runs over, the one named last changes fastest.
Arguments:
- hidden: bfloat16 [32, 8192], P(('groups', 'heads')), parts along dimension 0, may hold values from -6 to 6
- norm_gain: bfloat16 [8192], P('mem'), may hold values from 0.5 to 1.5
- q_weight: bfloat16 [8192, 8192], P('mem', 'heads'), may hold values from -0.0625 to 0.0625
- k_weight: bfloat16 [8192, 1024], P('mem', 'heads'), may hold values from -1 to 1, as said below
- v_weight: bfloat16 [8192, 1024], P('mem', 'heads'), may hold values from -1 to 1, as said below
- o_weight: bfloat16 [8192, 8192], P('heads', 'mem'), may hold values from -0.0625 to 0.0625
- k_cache: bfloat16 [384, 8, 128, 128], P(('groups', 'mem'), 'heads'), parts along dimension 0, may hold values from -40 to 40, as said below
- v_cache: bfloat16 [384, 8, 128, 128], P(('groups', 'mem'), 'heads'), parts along dimension 0, may hold values from -6 to 6, as said below
- page_table: int32 [16, 24], P('groups'), parts along dimension 0, may hold values from 0 to 191, as said below
- attend_list: int32 [16, 8], P('groups'), parts along dimension 0, may hold values from 0 to 23, as said below
- lengths: int32 [16], P('groups'), parts along dimension 0, may hold values from 1409 to 3072, as said below
Outputs:
- layer_out: bfloat16 [32, 8192], P(('groups', 'heads'), 'mem'), parts along dimension 0
The draws below stay inside these ranges and needn't reach their ends.
There are 2 independent parts, one for each index of `groups`. The reference program is written for one: setup_inputs(seed, part) draws one part's arguments, and reference() takes and returns one part's arrays. A program takes and returns all parts, laid end to end along the dimension named above; an argument that names none is the same for every part. Nothing has to cross between parts.
Inputs may be any that keep to these rules, and one draw needn't show every extreme that they name: `page_table`: A permutation of the pool slots 0 to 191 laid out as 8 rows of 24. The blocks named by attend_list lie at most 32 in any one range of slots m * 48 to (m + 1) * 48 - 1, and exactly 32 in some such range. `attend_list`: each row names 8 distinct blocks, all below ceil(lengths[r] / 128), among them its last block ceil(lengths[r] / 128) - 1. `lengths`: some row holds 3072 steps. `k_cache`: each key-value head is stored 1 times, the copies equal. `v_cache`: each key-value head is stored 1 times, the copies equal. `k_weight`: the 1 column blocks of each key-value head are equal. `v_weight`: the 1 column blocks of each key-value head are equal.
All inputs are finite; a program needn't handle non-finite values.
Results may differ from the reference program's by a relative error of at most 0.007.
The reference program's roundings to bfloat16 on the way count: a program that leaves them out, or rounds other values in their place, can miss the bound.
Values may be sent and summed in bfloat16 or wider, within the bound.
No kernel may reach another device: no remote copies, remote signals or barrier semaphores. Data moves between devices by JAX's collectives and lax.ppermute only.
A program may use at most 64 MiB of HBM per device.

```python
import jax
import jax.numpy as jnp
from jax import lax

D = 8192
HQ = 64
KVH = 8
HD = 128
BS = 128
STEPS = 2
ROWS = 8
BLK_DEV = 48
NBLK = 192
HBLK = 24
SEL = 8
CAP = 32
KVC = 8
REP = 1
TOKENS = 16


def layout_tables(key):
    base_key = jax.random.fold_in(key, 7)
    key_blocks, key_longest, key_tail, key_pick, key_rank, key_slots, key_pairs = jax.random.split(base_key, 7)
    row_ids = jnp.arange(ROWS, dtype=jnp.int32)
    lowest = max(SEL, HBLK // 2)
    block_count = jax.random.randint(key_blocks, (ROWS,), lowest, HBLK + 1).astype(jnp.int32)
    longest = jax.random.randint(key_longest, (), 0, ROWS)
    block_count = jnp.where(row_ids == longest, HBLK, block_count)
    tail_steps = jax.random.randint(key_tail, (ROWS,), 1, BS + 1).astype(jnp.int32)
    tail_steps = jnp.where(row_ids == longest, BS, tail_steps)
    row_lengths = (block_count - 1) * BS + tail_steps
    block_ids = jnp.arange(HBLK, dtype=jnp.int32)
    pick_score = jax.random.randint(key_pick, (ROWS, HBLK), 0, 1 << 20).astype(jnp.int32) * HBLK + block_ids[None, :]
    pick_score = jnp.where(block_ids[None, :] < block_count[:, None] - 1, pick_score, (1 << 20) * HBLK + HBLK + block_ids[None, :])
    pick_score = jnp.where(block_ids[None, :] == block_count[:, None] - 1, -1, pick_score)
    chosen_blocks = jnp.argsort(pick_score, axis=1)[:, :SEL].astype(jnp.int32)
    attended = jnp.any(chosen_blocks[:, :, None] == block_ids[None, None, :], axis=1).reshape(-1)
    owners = NBLK // BLK_DEV
    listed = ROWS * SEL
    spread = (listed - CAP) // (owners - 1)
    extra = listed - CAP - spread * (owners - 1)
    owner_rank = jax.random.permutation(key_rank, owners).astype(jnp.int32)
    owner_load = jnp.where(owner_rank == 0, CAP, spread + (owner_rank <= extra).astype(jnp.int32))
    slot_ids = jnp.arange(BLK_DEV, dtype=jnp.int32)
    inner_order = jnp.argsort(jax.random.randint(key_slots, (owners, BLK_DEV), 0, 1 << 20).astype(jnp.int32) * BLK_DEV + slot_ids[None, :], axis=1).astype(jnp.int32)
    owner_ids = jnp.arange(owners, dtype=jnp.int32)[:, None]
    slot_values = (owner_ids * BLK_DEV + inner_order).reshape(-1)
    slot_used = (slot_ids[None, :] < owner_load[:, None]).reshape(-1)
    slot_order = jnp.argsort(jnp.where(slot_used, 0, NBLK) + jnp.arange(NBLK, dtype=jnp.int32))
    pair_rank = jax.random.permutation(key_pairs, NBLK).astype(jnp.int32)
    pair_order = jnp.argsort(jnp.where(attended, 0, NBLK) + pair_rank)
    table = jnp.zeros((NBLK,), jnp.int32).at[pair_order].set(slot_values[slot_order])
    return (table.reshape(ROWS, HBLK), chosen_blocks, row_lengths.astype(jnp.int32))


def draw_page_table(key, part):
    return layout_tables(key)[0]


def draw_attend_list(key, part):
    return layout_tables(key)[1]


def draw_lengths(key, part):
    return layout_tables(key)[2]


def draw_k_cache(key, part):
    key_base = jax.random.fold_in(jax.random.fold_in(key, 11), 0)
    values = jnp.clip(jax.random.normal(key_base, (NBLK, KVH, BS, HD), jnp.float32), -6.0, 6.0)
    return jnp.repeat(values, REP, axis=1).astype(jnp.bfloat16)


def draw_v_cache(key, part):
    values = jnp.clip(jax.random.normal(jax.random.fold_in(key, 13), (NBLK, KVH, BS, HD), jnp.float32), -6.0, 6.0)
    return jnp.repeat(values, REP, axis=1).astype(jnp.bfloat16)


def duplicated_weight(key, salt, factor):
    values = jnp.clip(jax.random.normal(jax.random.fold_in(key, salt), (D, KVH, 1, HD), jnp.float32), -4.0, 4.0) * (factor * D ** (-0.5))
    return jnp.broadcast_to(values, (D, KVH, REP, HD)).reshape(D, KVC * HD).astype(jnp.bfloat16)


def draw_k_weight(key, part):
    return duplicated_weight(key, 17, 4.0)


def draw_v_weight(key, part):
    return duplicated_weight(key, 19, 3.0)


def shard_levels(stream_key, shape, shards, least, top_value):
    factor_of = 1.0
    for dim, parts in shards:
        heights = jax.random.uniform(jax.random.fold_in(jax.random.fold_in(stream_key, 6), dim), (parts,), jnp.float32, least / len(shards), top_value / len(shards))
        factor_of = factor_of * jnp.repeat(jnp.exp(heights), shape[dim] // parts).reshape((-1,) + (1,) * (len(shape) - 1 - dim))
    return factor_of


def bell_draw(stream_key, dims, width, limit, cuts=(), held_as=jnp.bfloat16):
    drawn = width * jax.random.normal(stream_key, dims, jnp.float32)
    if cuts:
        drawn = drawn * shard_levels(stream_key, dims, cuts, -0.22, 0.18)
    return jnp.clip(drawn, -limit, limit).astype(held_as)


def setup_inputs(seed: int = 0, part: int = 0) -> dict:
    key_of = jax.random.split(jax.random.key(seed), 12)
    part_keys = jax.random.split(jax.random.fold_in(key_of[11], part), 12)
    hidden = bell_draw(part_keys[0], (TOKENS, D), 1.0, 6.0, ((0, 4),))
    norm_gain = jnp.clip(1.0 + 0.1 * jax.random.normal(key_of[1], (D,), jnp.float32), 0.5, 1.5).astype(jnp.bfloat16)
    q_weight = bell_draw(key_of[2], (D, HQ * HD), D ** -0.5, 0.0625, ((0, 4), (1, 4)))
    k_weight = draw_k_weight(jax.random.fold_in(key_of[11], 71), part)
    v_weight = draw_v_weight(jax.random.fold_in(key_of[11], 71), part)
    o_weight = bell_draw(key_of[5], (HQ * HD, D), (HQ * HD) ** -0.5, 0.0625, ((0, 4), (1, 4)))
    k_cache = draw_k_cache(jax.random.fold_in(jax.random.fold_in(key_of[11], part), 71), part)
    v_cache = draw_v_cache(jax.random.fold_in(jax.random.fold_in(key_of[11], part), 71), part)
    page_table = draw_page_table(jax.random.fold_in(jax.random.fold_in(key_of[11], part), 71), part)
    attend_list = draw_attend_list(jax.random.fold_in(jax.random.fold_in(key_of[11], part), 71), part)
    lengths = draw_lengths(jax.random.fold_in(jax.random.fold_in(key_of[11], part), 71), part)
    return dict(hidden=hidden, norm_gain=norm_gain, q_weight=q_weight, k_weight=k_weight, v_weight=v_weight, o_weight=o_weight, k_cache=k_cache, v_cache=v_cache, page_table=page_table, attend_list=attend_list, lengths=lengths)


def reference(hidden, norm_gain, q_weight, k_weight, v_weight, o_weight, k_cache, v_cache, page_table, attend_list, lengths):
    hidden_f = hidden.astype(jnp.float32)
    mean_sq = lax.optimization_barrier(jnp.mean(hidden_f * hidden_f, axis=-1, keepdims=True))
    normed = (hidden_f * lax.rsqrt(mean_sq + 1e-05) * norm_gain.astype(jnp.float32)).astype(jnp.bfloat16)
    group_size = HQ // KVH
    queries = jnp.dot(normed, q_weight, preferred_element_type=jnp.float32).astype(jnp.bfloat16)
    queries = queries.reshape(ROWS, STEPS, KVH, group_size, HD)
    key_base = k_weight.reshape(D, KVH, REP, HD)[:, :, 0, :].reshape(D, KVH * HD)
    value_base = v_weight.reshape(D, KVH, REP, HD)[:, :, 0, :].reshape(D, KVH * HD)
    new_keys = jnp.dot(normed, key_base, preferred_element_type=jnp.float32).astype(jnp.bfloat16).reshape(ROWS, STEPS, KVH, HD)
    new_values = jnp.dot(normed, value_base, preferred_element_type=jnp.float32).astype(jnp.bfloat16).reshape(ROWS, STEPS, KVH, HD)
    cache_keys = k_cache[:, ::REP]
    cache_values = v_cache[:, ::REP]
    scale_factor = HD ** (-0.5)
    highest = lax.Precision.HIGHEST

    def one_row(operands):
        row_query, row_keys, row_values, table_row, list_row, row_length = operands
        slots = jnp.take(table_row, list_row).astype(jnp.int32)
        block_keys = jnp.take(cache_keys, slots, axis=0).astype(jnp.float32)
        block_values = jnp.take(cache_values, slots, axis=0).astype(jnp.float32)
        positions = list_row[:, None] * BS + jnp.arange(BS, dtype=jnp.int32)[None, :]
        valid = positions < row_length
        query_f = row_query.astype(jnp.float32)
        cache_scores = jnp.einsum('sgpd,ngkd->sgpnk', query_f, block_keys, precision=highest) * scale_factor
        cache_scores = jnp.where(valid[None, None, None], cache_scores, -jnp.inf)
        cache_scores = cache_scores.reshape(STEPS, KVH, group_size, SEL * BS)
        fresh_scores = jnp.einsum('sgpd,tgd->sgpt', query_f, row_keys.astype(jnp.float32), precision=highest) * scale_factor
        causal = jnp.arange(STEPS, dtype=jnp.int32)[None, :] <= jnp.arange(STEPS, dtype=jnp.int32)[:, None]
        fresh_scores = jnp.where(causal[:, None, None, :], fresh_scores, -jnp.inf)
        all_scores = jnp.concatenate([cache_scores, fresh_scores], axis=-1)
        row_peak = lax.optimization_barrier(jnp.max(all_scores, axis=-1, keepdims=True))
        weights = jnp.exp(all_scores - row_peak)
        weight_sum = lax.optimization_barrier(jnp.sum(weights, axis=-1, keepdims=True))
        all_values = jnp.concatenate([block_values.transpose(1, 0, 2, 3).reshape(KVH, SEL * BS, HD), row_values.astype(jnp.float32).transpose(1, 0, 2)], axis=1)
        mixed = jnp.einsum('sgpk,gkd->sgpd', weights, all_values, precision=highest)
        return (mixed / weight_sum).astype(jnp.bfloat16).reshape(STEPS, HQ * HD)
    attended = lax.map(one_row, (queries, new_keys, new_values, page_table, attend_list, lengths))
    attended = attended.reshape(ROWS * STEPS, HQ * HD)
    return jnp.dot(attended, o_weight, preferred_element_type=jnp.float32).astype(jnp.bfloat16)
```

```python
import functools

import jax
import jax.numpy as jnp
from jax import lax
from jax.experimental import pallas as pl
from jax.experimental.pallas import tpu as pltpu
from jax.sharding import PartitionSpec as P

NEG_FILL = -1e30
EPSILON = 1e-05
LANES = 128
MIB = 1 << 20
IN_VMEM = pl.BlockSpec(memory_space=pltpu.VMEM)
IN_SMEM = pl.BlockSpec(memory_space=pltpu.SMEM)


def swap(array, axis, distance):
    count = lax.axis_size(axis)
    return lax.ppermute(array, axis, [(i, i ^ distance) for i in range(count)])


def kernel_call(body, name, outs, ins, vmem_mib, flops, scratch=()):
    return pl.pallas_call(
        body,
        out_shape=outs,
        in_specs=ins,
        out_specs=jax.tree.map(lambda _: IN_VMEM, outs),
        scratch_shapes=list(scratch),
        name=name,
        compiler_params=pltpu.CompilerParams(vmem_limit_bytes=vmem_mib * MIB),
        cost_estimate=pl.CostEstimate(flops=int(flops), bytes_accessed=MIB, transcendentals=0),
    )


def norm_body(hidden_ref, gain_ref, out_ref):
    cols = gain_ref.shape[1]
    start = pl.multiple_of(lax.axis_index("mem") * cols, cols)
    hidden = hidden_ref[...].astype(jnp.float32)
    mean_sq = jnp.mean(hidden * hidden, axis=-1, keepdims=True)
    own = hidden_ref[:, pl.ds(start, cols)].astype(jnp.float32)
    normed = own * lax.rsqrt(mean_sq + EPSILON) * gain_ref[...].astype(jnp.float32)
    out_ref[...] = normed.astype(jnp.bfloat16)


def project_body(parts, tile, *refs):
    chunks, (q_ref, k_ref, v_ref, out_ref) = refs[:parts], refs[parts:]
    rows = jnp.concatenate([c[...].astype(jnp.float32) for c in chunks], axis=0)
    rows = rows.astype(jnp.bfloat16)
    at = 0
    for weight in (q_ref, k_ref, v_ref):
        width = min(tile, weight.shape[1])
        for col in range(0, weight.shape[1], width):
            out_ref[:, at : at + width] = jnp.dot(
                rows, weight[:, col : col + width], preferred_element_type=jnp.float32
            )
            at += width


def output_body(tile, rows_ref, weight_ref, *out_refs):
    rows = rows_ref[...]
    chunk = out_refs[0].shape[0]
    for col in range(0, weight_ref.shape[1], tile):
        product = jnp.dot(
            rows, weight_ref[:, col : col + tile], preferred_element_type=jnp.float32
        )
        for i, out_ref in enumerate(out_refs):
            out_ref[:, col : col + tile] = product[i * chunk : (i + 1) * chunk]


def split_dot(weights, values):
    high = weights.astype(jnp.bfloat16)
    low = (weights - high.astype(jnp.float32)).astype(jnp.bfloat16)
    both = jnp.dot(
        jnp.concatenate([high, low], axis=0), values, preferred_element_type=jnp.float32
    )
    return both[: weights.shape[0]] + both[weights.shape[0] :]


def group_lanes(query_count):
    lane = lax.broadcasted_iota(jnp.int32, (query_count, LANES), 1)
    row = lax.broadcasted_iota(jnp.int32, (query_count, LANES), 0)
    return lane - row


def pack_columns(columns, query_count):
    per_row = LANES // query_count
    offset = group_lanes(query_count)
    rows = []
    for first in range(0, len(columns), per_row):
        row = jnp.zeros((query_count, LANES), jnp.float32)
        for i, column in enumerate(columns[first : first + per_row]):
            row = jnp.where(offset == i * query_count, column, row)
        rows.append(jnp.sum(row, axis=0, keepdims=True))
    return rows


def unpack_column(row, place, query_count):
    spread = jnp.broadcast_to(row, (query_count, LANES))
    picked = jnp.where(group_lanes(query_count) == place * query_count, spread, 0.0)
    return jnp.sum(picked, axis=1, keepdims=True)


def attend_body(
    chunk,
    steps,
    scale,
    table_ref,
    list_ref,
    lengths_ref,
    query_ref,
    new_key_ref,
    new_value_ref,
    key_ref,
    value_ref,
    out_ref,
    slot_ref,
    row_ref,
    valid_ref,
    score_ref,
    peak_ref,
    total_ref,
    accum_ref,
):
    mem = lax.axis_index("mem")
    head_shard = lax.axis_index("heads")
    row_count, kv_heads, query_count, head_dim = query_ref.shape
    pool, block = key_ref.shape[0], key_ref.shape[2]
    selected = list_ref.shape[1]
    capacity = score_ref.shape[0]

    def place_of(row):
        first = row * steps
        return (lax.bitwise_xor(first // chunk, head_shard) * chunk + first % chunk) // steps

    def add_pair(row, i, count):
        index = list_ref[row, i]
        slot = table_ref[row, index] - mem * pool
        slot_ref[count] = slot
        row_ref[count] = place_of(row)
        valid_ref[count] = lengths_ref[row] - index * block
        return count + ((slot >= 0) & (slot < pool)).astype(jnp.int32)

    count = jnp.int32(0)
    for row in range(row_count):
        for i in range(selected):
            count = add_pair(row, i, count)

    def block_of(c):
        live = c < count
        slot = jnp.where(live, slot_ref[c], 0)
        row = jnp.where(live, row_ref[c], row_count)
        valid = jnp.where(live, valid_ref[c], 0)
        return slot, row, valid

    lane = lax.broadcasted_iota(jnp.int32, (query_count, LANES), 1)
    peak_ref[...] = jnp.full(peak_ref.shape, NEG_FILL, jnp.float32)
    total_ref[...] = jnp.zeros(total_ref.shape, jnp.float32)
    accum_ref[...] = jnp.zeros(accum_ref.shape, jnp.float32)
    contract_last = (((1,), (1,)), ((), ()))
    for c in range(capacity):
        slot, row, valid = block_of(c)
        read_row = jnp.minimum(row, row_count - 1)
        for g in range(kv_heads):
            score = lax.dot_general(
                query_ref[read_row, g],
                key_ref[slot, g],
                contract_last,
                preferred_element_type=jnp.float32,
            )
            score = jnp.where(lane < valid, score * scale, NEG_FILL)
            score_ref[c, g] = score
            peak_ref[row, g] = jnp.maximum(peak_ref[row, g], score)

    tokens = new_key_ref.shape[1]
    shape = (row_count * query_count, tokens)
    per_kv = query_count // steps
    query_row = lax.broadcasted_iota(jnp.int32, shape, 0)
    query_place = query_row // query_count * steps + query_row % query_count // per_kv
    key_place = lax.broadcasted_iota(jnp.int32, shape, 1)

    def token_of(place):
        return lax.bitwise_xor(place // chunk, head_shard) * chunk + place % chunk

    query_token, key_token = token_of(query_place), token_of(key_place)
    seen = (
        (query_token // steps == key_token // steps)
        & (key_token <= query_token)
        & (query_token // steps % lax.axis_size("mem") == mem)
    )
    peaks = [None] * (row_count * kv_heads)
    totals = [None] * (row_count * kv_heads)
    for g in range(kv_heads):
        score = lax.dot_general(
            query_ref[:, g].reshape(row_count * query_count, head_dim),
            new_key_ref[g],
            contract_last,
            preferred_element_type=jnp.float32,
        )
        score = jnp.where(seen, score * scale, NEG_FILL)
        old = jnp.max(
            peak_ref[:row_count, g].reshape(row_count * query_count, LANES), axis=1, keepdims=True
        )
        peak = jnp.maximum(old, jnp.max(score, axis=1, keepdims=True))
        weights = jnp.where(seen, jnp.exp(score - peak), 0.0)
        accum = split_dot(weights, new_value_ref[g]).reshape(row_count, query_count, head_dim)
        total = jnp.sum(weights, axis=1, keepdims=True)
        wide = jnp.broadcast_to(peak, (row_count * query_count, LANES))
        wide = wide.reshape(row_count, query_count, LANES)
        peak_ref[:row_count, g] = wide
        accum_ref[:row_count, g] = accum
        total = jnp.broadcast_to(total, (row_count * query_count, LANES))
        total = total.reshape(row_count, query_count, LANES)
        for row in range(row_count):
            peaks[row * kv_heads + g] = wide[row]
            totals[row * kv_heads + g] = total[row]

    for c in range(capacity):
        slot, row, valid = block_of(c)
        for g in range(kv_heads):
            weights = jnp.exp(score_ref[c, g] - peak_ref[row, g])
            weights = jnp.where(lane < valid, weights, 0.0)
            total_ref[row, g] += weights
            accum_ref[row, g] += split_dot(weights, value_ref[slot, g])

    for row in range(row_count):
        for g in range(kv_heads):
            group = row * kv_heads + g
            totals[group] = totals[group] + jnp.sum(total_ref[row, g], axis=1, keepdims=True)
    groups = row_count * kv_heads
    height = groups * query_count
    out_ref[:height] = accum_ref[:row_count].reshape(height, head_dim)
    packed = pack_columns(peaks, query_count) + pack_columns(totals, query_count)
    spare = out_ref.shape[0] - height - len(packed)
    packed.append(jnp.zeros((spare, LANES), jnp.float32))
    out_ref[height:] = jnp.concatenate(packed, axis=0)


def combine_body(query_count, last, own_ref, other_ref, out_ref):
    per_row = LANES // query_count
    height = own_ref.shape[0] - 8
    groups = height // query_count
    rows = -(-groups // per_row)
    own_peak, other_peak = own_ref[height : height + rows], other_ref[height : height + rows]
    peak = jnp.maximum(own_peak, other_peak)
    own_factor, other_factor = jnp.exp(own_peak - peak), jnp.exp(other_peak - peak)
    total = (
        own_ref[height + rows : height + 2 * rows] * own_factor
        + other_ref[height + rows : height + 2 * rows] * other_factor
    )
    if last:
        own_factor, other_factor = own_factor / total, other_factor / total
    else:
        spare = jnp.zeros((8 - 2 * rows, LANES), jnp.float32)
        out_ref[height:] = jnp.concatenate([peak, total, spare], axis=0)
    for group in range(groups):
        row, place = divmod(group, per_row)
        at = slice(group * query_count, (group + 1) * query_count)
        merged = own_ref[at] * unpack_column(
            own_factor[row : row + 1], place, query_count
        ) + other_ref[at] * unpack_column(other_factor[row : row + 1], place, query_count)
        out_ref[at] = merged.astype(out_ref.dtype)


def shards(
    hidden,
    norm_gain,
    q_weight,
    k_weight,
    v_weight,
    o_weight,
    k_cache,
    v_cache,
    page_table,
    attend_list,
    lengths,
):
    mem_count, head_count = lax.axis_size("mem"), lax.axis_size("heads")
    chunk = hidden.shape[0]
    feature_cols = norm_gain.shape[0]
    query_cols, value_cols = q_weight.shape[1], k_weight.shape[1]
    _, kv_heads, block, head_dim = k_cache.shape
    row_count, selected = attend_list.shape
    token_count = chunk * head_count
    steps = token_count // row_count
    per_kv = query_cols // head_dim // kv_heads
    query_count = steps * per_kv
    capacity = 2 * row_count * selected // mem_count
    f32, bf16 = jnp.float32, jnp.bfloat16

    normed = kernel_call(
        norm_body,
        "norm",
        jax.ShapeDtypeStruct((chunk, feature_cols), bf16),
        [IN_VMEM] * 2,
        2,
        1e10,
    )(hidden, norm_gain.reshape(1, feature_cols))
    pieces = [normed] + [swap(normed, "heads", d) for d in range(1, head_count)]

    width = query_cols + 2 * value_cols
    summed = kernel_call(
        functools.partial(project_body, head_count, 512),
        "project",
        jax.ShapeDtypeStruct((token_count, width), f32),
        [IN_VMEM] * (head_count + 3),
        8,
        2 * token_count * feature_cols * width,
    )(*pieces, q_weight, k_weight, v_weight)
    distance = 1
    while distance < mem_count:
        summed = summed + swap(summed, "mem", distance)
        distance *= 2

    queries = summed[:, :query_cols].astype(bf16)
    queries = queries.reshape(row_count, steps, kv_heads, per_kv, head_dim)
    queries = queries.transpose(0, 2, 1, 3, 4).reshape(row_count, kv_heads, query_count, head_dim)
    fresh = summed[:, query_cols:].astype(bf16).reshape(token_count, 2, kv_heads, head_dim)
    fresh = fresh.transpose(1, 2, 0, 3)

    height = row_count * kv_heads * query_count
    partial = kernel_call(
        functools.partial(attend_body, chunk, steps, head_dim ** (-0.5)),
        "attend",
        jax.ShapeDtypeStruct((height + 8, LANES), f32),
        [IN_SMEM] * 3 + [IN_VMEM] * 5,
        8,
        1e10,
        [pltpu.SMEM((capacity + 1,), jnp.int32)] * 3
        + [pltpu.VMEM((capacity, kv_heads, query_count, LANES), f32)]
        + [pltpu.VMEM((row_count + 1, kv_heads, query_count, LANES), f32)] * 3,
    )(page_table, attend_list, lengths, queries, fresh[0], fresh[1], k_cache, v_cache)

    distance = 1
    while distance < mem_count:
        last = 2 * distance == mem_count
        partial = kernel_call(
            functools.partial(combine_body, query_count, last),
            "combine",
            jax.ShapeDtypeStruct((height, LANES), bf16)
            if last
            else jax.ShapeDtypeStruct(partial.shape, f32),
            [IN_VMEM] * 2,
            4,
            1e7,
        )(partial, swap(partial, "mem", distance))
        distance *= 2

    attended = partial.reshape(row_count, kv_heads, steps, per_kv, head_dim)
    attended = attended.transpose(0, 2, 1, 3, 4).reshape(token_count, query_cols)
    projected = kernel_call(
        functools.partial(output_body, 512),
        "output",
        [jax.ShapeDtypeStruct((chunk, o_weight.shape[1]), f32)] * head_count,
        [IN_VMEM] * 2,
        8,
        2 * token_count * query_cols * o_weight.shape[1],
    )(attended, o_weight)
    total = projected[0]
    for d in range(1, head_count):
        total = total + swap(projected[d], "heads", d)
    return total.astype(bf16)


def solution(mesh):
    in_specs = (
        P(("groups", "heads"), None),
        P("mem"),
        P("mem", "heads"),
        P("mem", "heads"),
        P("mem", "heads"),
        P("heads", "mem"),
        P(("groups", "mem"), "heads", None, None),
        P(("groups", "mem"), "heads", None, None),
        P("groups", None),
        P("groups", None),
        P("groups"),
    )
    out_specs = P(("groups", "heads"), "mem")
    return jax.shard_map(shards, mesh=mesh, in_specs=in_specs, out_specs=out_specs, check_vma=False)
```

```python
import functools

import jax
import jax.numpy as jnp
from jax import lax
from jax.experimental import pallas as pl
from jax.experimental.pallas import tpu as pltpu
from jax.sharding import PartitionSpec as P

NEG_FILL = -1e30
EPSILON = 1e-05
LANES = 128
MIB = 1 << 20
IN_VMEM = pl.BlockSpec(memory_space=pltpu.VMEM)
IN_SMEM = pl.BlockSpec(memory_space=pltpu.SMEM)


def swap(array, axis, distance):
    count = lax.axis_size(axis)
    return lax.ppermute(array, axis, [(i, i ^ distance) for i in range(count)])


def kernel_call(body, name, outs, ins, vmem_mib, flops, scratch=(), out_space=IN_VMEM):
    return pl.pallas_call(
        body,
        out_shape=outs,
        in_specs=ins,
        out_specs=jax.tree.map(lambda _: out_space, outs),
        scratch_shapes=list(scratch),
        name=name,
        compiler_params=pltpu.CompilerParams(vmem_limit_bytes=vmem_mib * MIB),
        cost_estimate=pl.CostEstimate(flops=int(flops), bytes_accessed=1024, transcendentals=0),
    )


def norm_body(hidden_hbm, gain_hbm, out_ref, hidden_ref, gain_ref, sems):
    copies = [
        pltpu.make_async_copy(hidden_hbm, hidden_ref, sems.at[0]),
        pltpu.make_async_copy(gain_hbm, gain_ref, sems.at[1]),
    ]
    for copy in copies:
        copy.start()
    for copy in copies:
        copy.wait()
    cols = gain_ref.shape[0]
    start = pl.multiple_of(lax.axis_index("mem") * cols, cols)
    hidden = hidden_ref[...].astype(jnp.float32)
    mean_sq = jnp.mean(hidden * hidden, axis=-1, keepdims=True)
    own = hidden_ref[:, pl.ds(start, cols)].astype(jnp.float32)
    gain = gain_ref[...].astype(jnp.float32).reshape(1, cols)
    normed = own * lax.rsqrt(mean_sq + EPSILON) * gain
    out_ref[...] = normed.astype(jnp.bfloat16)


def select_body(chunk, steps, pool, block, table_ref, list_ref, lengths_ref, slot_ref, row_ref, valid_ref):
    mem = lax.axis_index("mem")
    head_shard = lax.axis_index("heads")
    row_count, selected = list_ref.shape
    count = jnp.int32(0)
    for row in range(row_count):
        first = row * steps
        place = (lax.bitwise_xor(first // chunk, head_shard) * chunk + first % chunk) // steps
        length = lengths_ref[row]
        for i in range(selected):
            index = list_ref[row, i]
            slot = table_ref[row, index] - mem * pool
            slot_ref[count] = slot
            row_ref[count] = place
            valid_ref[count] = length - index * block
            count += ((slot >= 0) & (slot < pool)).astype(jnp.int32)
    for c in range(slot_ref.shape[0] - 1):
        live = c < count
        slot_ref[c] = jnp.where(live, slot_ref[c], 0)
        row_ref[c] = jnp.where(live, row_ref[c], row_count)
        valid_ref[c] = jnp.where(live, valid_ref[c], 0)


def project_body(places, tile, *refs):
    q_ref, k_ref, v_ref, out_ref = refs[len(places) :]
    chunks = [refs[places.index(i)] for i in range(len(places))]
    rows = jnp.concatenate([c[...].astype(jnp.float32) for c in chunks], axis=0)
    rows = rows.astype(jnp.bfloat16)
    at = 0
    for weight in (q_ref, k_ref, v_ref):
        width = min(tile, weight.shape[1])
        for col in range(0, weight.shape[1], width):
            product = jnp.dot(
                rows, weight[:, col : col + width], preferred_element_type=jnp.float32
            )
            for lane in range(0, width, LANES):
                out_ref[at : at + rows.shape[0]] = product[:, lane : lane + LANES]
                at += rows.shape[0]


def add_body(own_ref, other_ref, out_ref, *sent_refs):
    total = own_ref[...] + other_ref[...]
    for ref in (out_ref, *sent_refs):
        ref[...] = total.astype(ref.dtype)


def split_dot(weights, values):
    high = weights.astype(jnp.bfloat16)
    low = (weights - high.astype(jnp.float32)).astype(jnp.bfloat16)
    both = jnp.dot(
        jnp.concatenate([high, low], axis=0), values, preferred_element_type=jnp.float32
    )
    return both[: weights.shape[0]] + both[weights.shape[0] :]


def to_pieces(rows):
    pieces = []
    for _ in range(3):
        pieces.append(rows.astype(jnp.bfloat16))
        rows = rows - pieces[-1].astype(jnp.float32)
    return pieces


def from_pieces(pieces):
    high, middle, low = [piece.astype(jnp.float32) for piece in pieces]
    return low + middle + high


def group_lanes(query_count):
    lane = lax.broadcasted_iota(jnp.int32, (query_count, LANES), 1)
    row = lax.broadcasted_iota(jnp.int32, (query_count, LANES), 0)
    return lane - row


def pack_columns(columns, query_count):
    per_row = LANES // query_count
    offset = group_lanes(query_count)
    rows = []
    for first in range(0, len(columns), per_row):
        row = jnp.zeros((query_count, LANES), jnp.float32)
        for i, column in enumerate(columns[first : first + per_row]):
            row = jnp.where(offset == i * query_count, column, row)
        rows.append(jnp.sum(row, axis=0, keepdims=True))
    return rows


def unpack_column(row, place, query_count):
    spread = jnp.broadcast_to(row, (query_count, LANES))
    picked = jnp.where(group_lanes(query_count) == place * query_count, spread, 0.0)
    return jnp.sum(picked, axis=1, keepdims=True)


def attend_body(
    chunk,
    steps,
    scale,
    slot_ref,
    row_ref,
    valid_ref,
    own_ref,
    other_ref,
    key_ref,
    value_ref,
    out_ref,
    wide_ref,
    query_ref,
    score_ref,
    peak_ref,
    total_ref,
    accum_ref,
):
    mem = lax.axis_index("mem")
    head_shard = lax.axis_index("heads")
    row_count, kv_heads, query_count, head_dim = query_ref.shape
    capacity = score_ref.shape[0]
    tokens = row_count * steps
    per_kv = query_count // steps

    projected = (own_ref[...] + other_ref[...].astype(jnp.float32)).astype(jnp.bfloat16)
    wide_ref[...] = projected.astype(jnp.float32)
    for row in range(row_count):
        for g in range(kv_heads):
            first = g * per_kv * tokens + row * steps
            parts = [wide_ref[pl.ds(first + s, per_kv, stride=tokens)] for s in range(steps)]
            query_ref[row, g] = jnp.concatenate(parts, axis=0).astype(jnp.bfloat16)
    fresh_at = kv_heads * per_kv * tokens
    fresh = [
        projected[fresh_at + i * tokens : fresh_at + (i + 1) * tokens] for i in range(2 * kv_heads)
    ]
    new_keys, new_values = fresh[:kv_heads], fresh[kv_heads:]

    lane = lax.broadcasted_iota(jnp.int32, (query_count, LANES), 1)
    peak_ref[...] = jnp.full(peak_ref.shape, NEG_FILL, jnp.float32)
    total_ref[...] = jnp.zeros(total_ref.shape, jnp.float32)
    accum_ref[...] = jnp.zeros(accum_ref.shape, jnp.float32)
    contract_last = (((1,), (1,)), ((), ()))
    for c in range(capacity):
        slot, row, valid = slot_ref[c], row_ref[c], valid_ref[c]
        read_row = jnp.minimum(row, row_count - 1)
        for g in range(kv_heads):
            score = lax.dot_general(
                query_ref[read_row, g],
                key_ref[slot, g],
                contract_last,
                preferred_element_type=jnp.float32,
            )
            score = jnp.where(lane < valid, score * scale, NEG_FILL)
            score_ref[c, g] = score
            peak_ref[row, g] = jnp.maximum(peak_ref[row, g], score)

    shape = (row_count * query_count, tokens)
    query_row = lax.broadcasted_iota(jnp.int32, shape, 0)
    query_place = query_row // query_count * steps + query_row % query_count // per_kv
    key_place = lax.broadcasted_iota(jnp.int32, shape, 1)

    def token_of(place):
        return lax.bitwise_xor(place // chunk, head_shard) * chunk + place % chunk

    query_token, key_token = token_of(query_place), token_of(key_place)
    seen = (
        (query_token // steps == key_token // steps)
        & (key_token <= query_token)
        & (query_token // steps % lax.axis_size("mem") == mem)
    )
    peaks = [None] * (row_count * kv_heads)
    totals = [None] * (row_count * kv_heads)
    for g in range(kv_heads):
        score = lax.dot_general(
            query_ref[:, g].reshape(row_count * query_count, head_dim),
            new_keys[g],
            contract_last,
            preferred_element_type=jnp.float32,
        )
        score = jnp.where(seen, score * scale, NEG_FILL)
        old = jnp.max(
            peak_ref[:row_count, g].reshape(row_count * query_count, LANES), axis=1, keepdims=True
        )
        peak = jnp.maximum(old, jnp.max(score, axis=1, keepdims=True))
        weights = jnp.where(seen, jnp.exp(score - peak), 0.0)
        accum = split_dot(weights, new_values[g]).reshape(row_count, query_count, head_dim)
        total = jnp.sum(weights, axis=1, keepdims=True)
        wide = jnp.broadcast_to(peak, (row_count * query_count, LANES))
        wide = wide.reshape(row_count, query_count, LANES)
        peak_ref[:row_count, g] = wide
        accum_ref[:row_count, g] = accum
        total = jnp.broadcast_to(total, (row_count * query_count, LANES))
        total = total.reshape(row_count, query_count, LANES)
        for row in range(row_count):
            peaks[row * kv_heads + g] = wide[row]
            totals[row * kv_heads + g] = total[row]

    for c in range(capacity):
        slot, row, valid = slot_ref[c], row_ref[c], valid_ref[c]
        for g in range(kv_heads):
            weights = jnp.exp(score_ref[c, g] - peak_ref[row, g])
            weights = jnp.where(lane < valid, weights, 0.0)
            total_ref[row, g] += weights
            accum_ref[row, g] += split_dot(weights, value_ref[slot, g])

    for row in range(row_count):
        for g in range(kv_heads):
            group = row * kv_heads + g
            totals[group] = totals[group] + jnp.sum(total_ref[row, g], axis=1, keepdims=True)
    groups = row_count * kv_heads
    height = groups * query_count
    out_ref[:height] = accum_ref[:row_count].reshape(height, head_dim)
    packed = pack_columns(peaks, query_count) + pack_columns(totals, query_count)
    spare = out_ref.shape[0] - height - len(packed)
    packed.append(jnp.zeros((spare, LANES), jnp.float32))
    out_ref[height:] = jnp.concatenate(packed, axis=0)


def state_rows(groups, query_count):
    return -(-groups // (LANES // query_count))


def merge_states(query_count, groups, last, own_ref, other_ref):
    per_row = LANES // query_count
    height = groups * query_count
    rows = state_rows(groups, query_count)
    own_peak, own_total = (own_ref[height + i * rows : height + (i + 1) * rows] for i in range(2))
    if other_ref.dtype == jnp.bfloat16:
        tail = other_ref[height:]
        pieces = [tail[i * rows : (i + 1) * rows] for i in range(6)]
        other_peak, other_total = from_pieces(pieces[:3]), from_pieces(pieces[3:])
    else:
        other_peak, other_total = (
            other_ref[height + i * rows : height + (i + 1) * rows] for i in range(2)
        )
    peak = jnp.maximum(own_peak, other_peak)
    own_factor, other_factor = jnp.exp(own_peak - peak), jnp.exp(other_peak - peak)
    total = own_total * own_factor + other_total * other_factor
    if last:
        own_factor, other_factor = own_factor / total, other_factor / total
    values = []
    for group in range(groups):
        row, place = divmod(group, per_row)
        at = slice(group * query_count, (group + 1) * query_count)
        values.append(
            own_ref[at] * unpack_column(own_factor[row : row + 1], place, query_count)
            + other_ref[at].astype(jnp.float32)
            * unpack_column(other_factor[row : row + 1], place, query_count)
        )
    return peak, total, values


def combine_body(query_count, groups, own_ref, other_ref, *out_refs):
    height = groups * query_count
    peak, total, values = merge_states(query_count, groups, False, own_ref, other_ref)
    for ref in out_refs:
        tail = [peak, total]
        if ref.dtype == jnp.bfloat16:
            tail = to_pieces(peak) + to_pieces(total)
        spare = ref.shape[0] - height - len(tail) * peak.shape[0]
        tail.append(jnp.zeros((spare, LANES), ref.dtype))
        ref[height:] = jnp.concatenate(tail, axis=0)
        for group, value in enumerate(values):
            ref[group * query_count : (group + 1) * query_count] = value.astype(ref.dtype)


def output_body(kv_heads, steps, tile, own_ref, other_ref, weight_ref, *refs):
    out_refs, wide_ref = refs[:-1], refs[-1]
    heads = weight_ref.shape[0] // LANES
    per_kv = heads // kv_heads
    tokens = wide_ref.shape[0] // heads
    groups = tokens // steps * kv_heads
    _, _, values = merge_states(steps * per_kv, groups, True, own_ref, other_ref)
    for group, value in enumerate(values):
        row, g = divmod(group, kv_heads)
        for s in range(steps):
            first = g * per_kv * tokens + row * steps + s
            wide_ref[pl.ds(first, per_kv, stride=tokens)] = value[s * per_kv : (s + 1) * per_kv]
    rows = jnp.concatenate(
        [wide_ref[j * tokens : (j + 1) * tokens].astype(jnp.bfloat16) for j in range(heads)], axis=1
    )
    chunk = out_refs[0].shape[0]
    for col in range(0, weight_ref.shape[1], tile):
        product = jnp.dot(
            rows, weight_ref[:, col : col + tile], preferred_element_type=jnp.float32
        )
        for i, out_ref in enumerate(out_refs):
            out_ref[:, col : col + tile] = product[i * chunk : (i + 1) * chunk]


def shards(
    hidden,
    norm_gain,
    q_weight,
    k_weight,
    v_weight,
    o_weight,
    k_cache,
    v_cache,
    page_table,
    attend_list,
    lengths,
):
    mem_count, head_count = lax.axis_size("mem"), lax.axis_size("heads")
    chunk = hidden.shape[0]
    feature_cols = norm_gain.shape[0]
    query_cols, value_cols = q_weight.shape[1], k_weight.shape[1]
    pool, kv_heads, block, head_dim = k_cache.shape
    row_count, selected = attend_list.shape
    token_count = chunk * head_count
    steps = token_count // row_count
    per_kv = query_cols // head_dim // kv_heads
    query_count = steps * per_kv
    capacity = 2 * row_count * selected // mem_count
    f32, bf16 = jnp.float32, jnp.bfloat16

    normed = kernel_call(
        norm_body,
        "norm",
        jax.ShapeDtypeStruct((chunk, feature_cols), bf16),
        [pl.BlockSpec(memory_space=pltpu.HBM)] * 2,
        2,
        1e10,
        [pltpu.VMEM(hidden.shape, bf16), pltpu.VMEM(norm_gain.shape, bf16)]
        + [pltpu.SemaphoreType.DMA((2,))],
    )(*[pltpu.with_memory_space_constraint(a, pltpu.HBM) for a in (hidden, norm_gain)])
    distances = [*range(2, head_count), 1]
    pieces = [normed] + [swap(normed, "heads", d) for d in distances]

    chosen = kernel_call(
        functools.partial(select_body, chunk, steps, pool, block),
        "select",
        [jax.ShapeDtypeStruct((capacity + 1,), jnp.int32)] * 3,
        [IN_SMEM] * 3,
        2,
        1e10,
        out_space=IN_SMEM,
    )(page_table, attend_list, lengths)

    width = query_cols + 2 * value_cols
    summed = kernel_call(
        functools.partial(project_body, (0, *distances), 512),
        "project",
        jax.ShapeDtypeStruct((width // LANES * token_count, LANES), f32),
        [IN_VMEM] * (head_count + 3),
        4,
        2 * token_count * feature_cols * width,
    )(*pieces, q_weight, k_weight, v_weight)
    sent = summed
    distance = 1
    while 2 * distance < mem_count:
        added = kernel_call(
            add_body,
            "add",
            [jax.ShapeDtypeStruct(summed.shape, f32)],
            [IN_VMEM] * 2,
            2,
            1e10,
        )(summed, swap(sent, "mem", distance))
        summed, sent = added[0], added[-1]
        distance *= 2

    groups = row_count * kv_heads
    height = groups * query_count
    state = (kv_heads, query_count, LANES)
    partial = kernel_call(
        functools.partial(attend_body, chunk, steps, head_dim ** (-0.5)),
        "attend",
        jax.ShapeDtypeStruct((height + 8, LANES), f32),
        [IN_SMEM] * 3 + [IN_VMEM] * 4,
        4,
        1e10,
        [pltpu.VMEM(summed.shape, f32), pltpu.VMEM((row_count, *state), bf16)]
        + [pltpu.VMEM((capacity, *state), f32)]
        + [pltpu.VMEM((row_count + 1, *state), f32)] * 3,
    )(*chosen, summed, swap(sent.astype(jnp.float16), "mem", distance).astype(f32), k_cache, v_cache)

    sent = partial
    distance = 1
    while 2 * distance < mem_count:
        outs = [jax.ShapeDtypeStruct(partial.shape, f32)]
        if 4 * distance == mem_count:
            pad = -(-6 * state_rows(groups, query_count) // 16) * 16
            outs.append(jax.ShapeDtypeStruct((height + pad, LANES), bf16))
        merged = kernel_call(
            functools.partial(combine_body, query_count, groups),
            "combine",
            outs,
            [IN_VMEM] * 2,
            2,
            1e10,
        )(partial, swap(sent, "mem", distance))
        partial, sent = merged[0], merged[-1]
        distance *= 2

    out_cols = o_weight.shape[1]
    projected = kernel_call(
        functools.partial(output_body, kv_heads, steps, min(512, out_cols)),
        "output",
        [jax.ShapeDtypeStruct((chunk, out_cols), f32)] * head_count,
        [IN_VMEM] * 3,
        4,
        2 * token_count * query_cols * out_cols,
        [pltpu.VMEM((query_cols // LANES * token_count, LANES), f32)],
    )(partial, swap(sent, "mem", distance), o_weight)
    total = projected[0]
    for d in distances:
        total = total + swap(projected[d], "heads", d)
    return total.astype(bf16)


def solution(mesh):
    in_specs = (
        P(("groups", "heads"), None),
        P("mem"),
        P("mem", "heads"),
        P("mem", "heads"),
        P("mem", "heads"),
        P("heads", "mem"),
        P(("groups", "mem"), "heads", None, None),
        P(("groups", "mem"), "heads", None, None),
        P("groups", None),
        P("groups", None),
        P("groups"),
    )
    out_specs = P(("groups", "heads"), "mem")
    return jax.shard_map(shards, mesh=mesh, in_specs=in_specs, out_specs=out_specs, check_vma=False)
```

```python
import functools

import jax
import jax.numpy as jnp
from jax import lax
from jax.experimental import pallas as pl
from jax.experimental.pallas import tpu as pltpu
from jax.sharding import PartitionSpec as P

NEG_FILL = -1e30
EPSILON = 1e-05
LANES = 128
MIB = 1 << 20
IN_VMEM = pl.BlockSpec(memory_space=pltpu.VMEM)
IN_SMEM = pl.BlockSpec(memory_space=pltpu.SMEM)


def swap(array, axis, distance):
    count = lax.axis_size(axis)
    return lax.ppermute(array, axis, [(i, i ^ distance) for i in range(count)])


def kernel_call(body, name, outs, ins, vmem_mib, flops, scratch=(), out_space=IN_VMEM):
    return pl.pallas_call(
        body,
        out_shape=outs,
        in_specs=ins,
        out_specs=out_space if isinstance(out_space, list) else jax.tree.map(lambda _: out_space, outs),
        scratch_shapes=list(scratch),
        name=name,
        compiler_params=pltpu.CompilerParams(vmem_limit_bytes=vmem_mib * MIB),
        cost_estimate=pl.CostEstimate(flops=int(flops), bytes_accessed=1024, transcendentals=0),
    )


def norm_body(hidden_hbm, gain_hbm, out_ref, hidden_ref, gain_ref, sems):
    copies = [
        pltpu.make_async_copy(hidden_hbm, hidden_ref, sems.at[0]),
        pltpu.make_async_copy(gain_hbm, gain_ref, sems.at[1]),
    ]
    for copy in copies:
        copy.start()
    for copy in copies:
        copy.wait()
    cols = gain_ref.shape[0]
    start = pl.multiple_of(lax.axis_index("mem") * cols, cols)
    hidden = hidden_ref[...].astype(jnp.float32)
    mean_sq = jnp.mean(hidden * hidden, axis=-1, keepdims=True)
    own = hidden_ref[:, pl.ds(start, cols)].astype(jnp.float32)
    gain = gain_ref[...].astype(jnp.float32).reshape(1, cols)
    normed = own * lax.rsqrt(mean_sq + EPSILON) * gain
    out_ref[...] = normed.astype(jnp.bfloat16)


def select_body(
    chunk, steps, pool, block, per_kv, table_ref, list_ref, lengths_ref,
    chosen_ref, seen_ref,
):
    mem = lax.axis_index("mem")
    head_shard = lax.axis_index("heads")
    row_count, selected = list_ref.shape
    stride = chosen_ref.shape[0] // 3
    count = jnp.int32(0)
    for row in range(row_count):
        first = row * steps
        place = (lax.bitwise_xor(first // chunk, head_shard) * chunk + first % chunk) // steps
        length = lengths_ref[row]
        for i in range(selected):
            index = list_ref[row, i]
            slot = table_ref[row, index] - mem * pool
            chosen_ref[count] = slot
            chosen_ref[stride + count] = place
            chosen_ref[2 * stride + count] = length - index * block
            count += ((slot >= 0) & (slot < pool)).astype(jnp.int32)
    for c in range(stride - 1):
        live = c < count
        for at, blank in ((c, 0), (stride + c, row_count), (2 * stride + c, 0)):
            chosen_ref[at] = jnp.where(live, chosen_ref[at], blank)

    def token_of(place):
        return lax.bitwise_xor(place // chunk, head_shard) * chunk + place % chunk

    tokens = row_count * steps
    group_rows = steps * per_kv
    row_height = seen_ref.shape[0] // row_count
    at = lax.broadcasted_iota(jnp.int32, seen_ref.shape, 0)
    query_token = token_of(at // row_height * steps + at % group_rows // per_kv)
    query_head = at % row_height // group_rows
    lane = lax.broadcasted_iota(jnp.int32, seen_ref.shape, 1)
    key_head, key = lane // tokens, lane % tokens
    key_token = token_of(key % row_count * steps + key // row_count)
    seen = (
        (query_head == key_head)
        & (query_token // steps == key_token // steps)
        & (key_token <= query_token)
        & (query_token // steps % lax.axis_size("mem") == mem)
    )
    seen_ref[...] = seen.astype(jnp.float32)


def project_body(places, steps, kv_heads, tile, *refs):
    q_ref, k_ref, v_ref, out_ref = refs[len(places) :]
    chunks = [refs[places.index(i)][...].astype(jnp.float32) for i in range(len(places))]
    rows = jnp.concatenate(chunks, axis=0).astype(jnp.bfloat16)
    tokens = rows.shape[0]
    row_count = tokens // steps
    to = lax.broadcasted_iota(jnp.int32, (tokens, tokens), 0)
    come = lax.broadcasted_iota(jnp.int32, (tokens, tokens), 1)
    order = (to % row_count * steps + to // row_count == come).astype(jnp.bfloat16)
    rows = jnp.dot(order, rows, preferred_element_type=jnp.float32).astype(jnp.bfloat16)
    heads = q_ref.shape[1] // LANES
    per_kv = heads // kv_heads
    head = 0
    for weight in (q_ref, k_ref, v_ref):
        width = min(tile, weight.shape[1])
        for col in range(0, weight.shape[1], width):
            product = jnp.dot(
                rows, weight[:, col : col + width], preferred_element_type=jnp.float32
            )
            for lane in range(0, width, LANES):
                columns = product[:, lane : lane + LANES]
                if head < heads:
                    for s in range(steps):
                        at = (head // per_kv * steps + s) * per_kv + head % per_kv
                        out_ref[pl.ds(at, row_count, stride=heads * steps)] = columns[
                            s * row_count : (s + 1) * row_count
                        ]
                else:
                    out_ref[head * tokens : (head + 1) * tokens] = columns
                head += 1


def add_body(own_ref, other_ref, out_ref, *sent_refs):
    total = own_ref[...] + other_ref[...]
    for ref in (out_ref, *sent_refs):
        ref[...] = total.astype(ref.dtype)


def split_dot(weights, values):
    high = weights.astype(jnp.bfloat16)
    low = (weights - high.astype(jnp.float32)).astype(jnp.bfloat16)
    both = jnp.dot(
        jnp.concatenate([high, low], axis=0), values, preferred_element_type=jnp.float32
    )
    return both[: weights.shape[0]] + both[weights.shape[0] :]


def to_pieces(rows):
    pieces = []
    for _ in range(3):
        pieces.append(rows.astype(jnp.bfloat16))
        rows = rows - pieces[-1].astype(jnp.float32)
    return pieces


def from_pieces(pieces):
    high, middle, low = [piece.astype(jnp.float32) for piece in pieces]
    return low + middle + high


def group_lanes(query_count):
    lane = lax.broadcasted_iota(jnp.int32, (query_count, LANES), 1)
    row = lax.broadcasted_iota(jnp.int32, (query_count, LANES), 0)
    return lane - row


def pack_columns(column, query_count):
    per_row = LANES // query_count
    offset = group_lanes(query_count)
    groups = column.shape[0] // query_count
    rows = []
    for first in range(0, groups, per_row):
        row = jnp.zeros((query_count, LANES), jnp.float32)
        for i in range(min(per_row, groups - first)):
            at = (first + i) * query_count
            row = jnp.where(offset == i * query_count, column[at : at + query_count], row)
        rows.append(jnp.sum(row, axis=0, keepdims=True))
    return rows


def unpack_column(row, place, query_count):
    spread = jnp.broadcast_to(row, (query_count, LANES))
    picked = jnp.where(group_lanes(query_count) == place * query_count, spread, 0.0)
    return jnp.sum(picked, axis=1, keepdims=True)


def attend_body(
    scale,
    chosen_ref,
    seen_ref,
    own_ref,
    other_ref,
    key_ref,
    value_ref,
    out_ref,
    query_ref,
    score_ref,
    total_ref,
    accum_ref,
    *peak_refs,
):
    row_count, row_height, head_dim = query_ref.shape
    kv_heads = key_ref.shape[1]
    query_count = row_height // kv_heads
    capacity = score_ref.shape[0]
    height = row_count * row_height
    contract_last = (((1,), (1,)), ((), ()))

    projected = (own_ref[...] + other_ref[...]).astype(jnp.bfloat16)
    queries = projected[:height]
    query_ref[...] = queries.reshape(query_ref.shape)
    fresh = projected[height:]
    count = fresh.shape[0] // 2
    spare = jnp.zeros((LANES - count, head_dim), jnp.bfloat16)
    seen = seen_ref[...] > 0
    fresh_score = lax.dot_general(
        queries,
        jnp.concatenate([fresh[:count], spare], axis=0),
        contract_last,
        preferred_element_type=jnp.float32,
    )
    fresh_score = jnp.where(seen, fresh_score * scale, NEG_FILL)
    peak_ref = peak_refs[0]
    peak_ref[:row_count] = fresh_score.reshape(row_count, row_height, LANES)
    peak_ref[row_count] = jnp.full((row_height, LANES), NEG_FILL, jnp.float32)
    for ref in peak_refs[1:]:
        ref[...] = jnp.full(ref.shape, NEG_FILL, jnp.float32)
    stride = chosen_ref.shape[0] // 3

    lane = lax.broadcasted_iota(jnp.int32, (row_height, LANES), 1)
    for c in range(capacity):
        slot, row, valid = (chosen_ref[i * stride + c] for i in range(3))
        every = lax.dot_general(
            query_ref[jnp.minimum(row, row_count - 1)],
            key_ref[slot].reshape(kv_heads * LANES, head_dim),
            contract_last,
            preferred_element_type=jnp.float32,
        )
        score = jnp.concatenate(
            [
                every[g * query_count : (g + 1) * query_count, g * LANES : (g + 1) * LANES]
                for g in range(kv_heads)
            ],
            axis=0,
        )
        score = jnp.where(lane < valid, score * scale, NEG_FILL)
        score_ref[c] = score
        ref = peak_refs[c % len(peak_refs)]
        ref[row] = jnp.maximum(ref[row], score)

    peak = functools.reduce(jnp.maximum, [ref[:row_count] for ref in peak_refs])
    peak = jnp.max(peak.reshape(height, LANES), axis=1, keepdims=True)
    peak = jnp.broadcast_to(peak, (height, LANES))
    peak_ref[:row_count] = peak.reshape(row_count, row_height, LANES)
    weights = jnp.where(seen, jnp.exp(fresh_score - peak), 0.0)
    total_ref[:row_count] = weights.reshape(row_count, row_height, LANES)
    total_ref[row_count] = jnp.zeros((row_height, LANES), jnp.float32)
    accum = split_dot(weights, jnp.concatenate([fresh[count:], spare], axis=0))
    accum_ref[:row_count] = accum.reshape(row_count, row_height, head_dim)
    accum_ref[row_count] = jnp.zeros((row_height, head_dim), jnp.float32)

    for c in range(capacity):
        slot, row = chosen_ref[c], chosen_ref[stride + c]
        weights = jnp.exp(score_ref[c] - peak_ref[row])
        total_ref[row] += weights
        high = weights.astype(jnp.bfloat16)
        low = (weights - high.astype(jnp.float32)).astype(jnp.bfloat16)
        split = []
        for g in range(kv_heads):
            at = slice(g * query_count, (g + 1) * query_count)
            half = jnp.concatenate([high[at], low[at]], axis=0)
            blank = jnp.zeros_like(half)
            split.append(
                jnp.concatenate([half if i == g else blank for i in range(kv_heads)], axis=1)
            )
        both = jnp.dot(
            jnp.concatenate(split, axis=0),
            value_ref[slot].reshape(kv_heads * LANES, head_dim),
            preferred_element_type=jnp.float32,
        ).reshape(kv_heads, 2, query_count, head_dim)
        accum_ref[row] += (both[:, 0] + both[:, 1]).reshape(row_height, head_dim)

    total = jnp.sum(total_ref[:row_count].reshape(height, LANES), axis=1, keepdims=True)
    total = jnp.broadcast_to(total, (height, LANES))
    out_ref[:height] = accum_ref[:row_count].reshape(height, head_dim)
    packed = pack_columns(peak, query_count) + pack_columns(total, query_count)
    spare = out_ref.shape[0] - height - len(packed)
    packed.append(jnp.zeros((spare, LANES), jnp.float32))
    out_ref[height:] = jnp.concatenate(packed, axis=0)


def state_rows(groups, query_count):
    return -(-groups // (LANES // query_count))


def merge_states(query_count, groups, last, own_ref, other_ref):
    per_row = LANES // query_count
    height = groups * query_count
    rows = state_rows(groups, query_count)
    own_peak, own_total = (own_ref[height + i * rows : height + (i + 1) * rows] for i in range(2))
    if other_ref.dtype == jnp.bfloat16:
        tail = other_ref[height:]
        pieces = [tail[i * rows : (i + 1) * rows] for i in range(6)]
        other_peak, other_total = from_pieces(pieces[:3]), from_pieces(pieces[3:])
    else:
        other_peak, other_total = (
            other_ref[height + i * rows : height + (i + 1) * rows] for i in range(2)
        )
    peak = jnp.maximum(own_peak, other_peak)
    own_factor, other_factor = jnp.exp(own_peak - peak), jnp.exp(other_peak - peak)
    total = own_total * own_factor + other_total * other_factor
    if last:
        own_factor, other_factor = own_factor / total, other_factor / total
    values = []
    for group in range(groups):
        row, place = divmod(group, per_row)
        at = slice(group * query_count, (group + 1) * query_count)
        values.append(
            own_ref[at] * unpack_column(own_factor[row : row + 1], place, query_count)
            + other_ref[at].astype(jnp.float32)
            * unpack_column(other_factor[row : row + 1], place, query_count)
        )
    return peak, total, values


def combine_body(query_count, groups, own_ref, other_ref, *out_refs):
    height = groups * query_count
    peak, total, values = merge_states(query_count, groups, False, own_ref, other_ref)
    for ref in out_refs:
        tail = [peak, total]
        if ref.dtype == jnp.bfloat16:
            tail = to_pieces(peak) + to_pieces(total)
        spare = ref.shape[0] - height - len(tail) * peak.shape[0]
        tail.append(jnp.zeros((spare, LANES), ref.dtype))
        ref[height:] = jnp.concatenate(tail, axis=0)
        for group, value in enumerate(values):
            ref[group * query_count : (group + 1) * query_count] = value.astype(ref.dtype)


def output_body(kv_heads, steps, tile, own_ref, other_ref, weight_ref, *refs):
    out_refs, wide_ref = refs[:-1], refs[-1]
    heads = weight_ref.shape[0] // LANES
    per_kv = heads // kv_heads
    tokens = wide_ref.shape[0] // heads
    groups = tokens // steps * kv_heads
    _, _, values = merge_states(steps * per_kv, groups, True, own_ref, other_ref)
    for group, value in enumerate(values):
        row, g = divmod(group, kv_heads)
        for s in range(steps):
            first = g * per_kv * tokens + row * steps + s
            wide_ref[pl.ds(first, per_kv, stride=tokens)] = value[s * per_kv : (s + 1) * per_kv]
    rows = jnp.concatenate(
        [wide_ref[j * tokens : (j + 1) * tokens].astype(jnp.bfloat16) for j in range(heads)], axis=1
    )
    chunk = out_refs[0].shape[0]
    for col in range(0, weight_ref.shape[1], tile):
        product = jnp.dot(
            rows, weight_ref[:, col : col + tile], preferred_element_type=jnp.float32
        )
        for i, out_ref in enumerate(out_refs):
            out_ref[:, col : col + tile] = product[i * chunk : (i + 1) * chunk]


def shards(
    hidden,
    norm_gain,
    q_weight,
    k_weight,
    v_weight,
    o_weight,
    k_cache,
    v_cache,
    page_table,
    attend_list,
    lengths,
):
    mem_count, head_count = lax.axis_size("mem"), lax.axis_size("heads")
    chunk = hidden.shape[0]
    feature_cols = norm_gain.shape[0]
    query_cols, value_cols = q_weight.shape[1], k_weight.shape[1]
    pool, kv_heads, block, head_dim = k_cache.shape
    row_count, selected = attend_list.shape
    token_count = chunk * head_count
    steps = token_count // row_count
    per_kv = query_cols // head_dim // kv_heads
    query_count = steps * per_kv
    capacity = 2 * row_count * selected // mem_count
    groups = row_count * kv_heads
    height = groups * query_count
    f32, bf16 = jnp.float32, jnp.bfloat16

    normed = kernel_call(
        norm_body,
        "norm",
        jax.ShapeDtypeStruct((chunk, feature_cols), bf16),
        [pl.BlockSpec(memory_space=pltpu.HBM)] * 2,
        2,
        1e10,
        [pltpu.VMEM(hidden.shape, bf16), pltpu.VMEM(norm_gain.shape, bf16)]
        + [pltpu.SemaphoreType.DMA((2,))],
    )(*[pltpu.with_memory_space_constraint(a, pltpu.HBM) for a in (hidden, norm_gain)])
    distances = [*range(2, head_count), 1]
    pieces = [normed] + [swap(normed, "heads", d) for d in distances]

    chosen = kernel_call(
        functools.partial(select_body, chunk, steps, pool, block, per_kv),
        "select",
        [
            pltpu.SMEM((3 * (capacity + 1),), jnp.int32),
            jax.ShapeDtypeStruct((height, LANES), f32),
        ],
        [IN_SMEM] * 3,
        2,
        1e10,
        out_space=[IN_SMEM, IN_VMEM],
    )(page_table, attend_list, lengths)

    width = query_cols + 2 * value_cols
    summed = kernel_call(
        functools.partial(project_body, (0, *distances), steps, kv_heads, 512),
        "project",
        jax.ShapeDtypeStruct((width // LANES * token_count, LANES), f32),
        [IN_VMEM] * (head_count + 3),
        4,
        2 * token_count * feature_cols * width,
    )(*pieces, q_weight, k_weight, v_weight)
    sent = summed
    distance = 1
    while 2 * distance < mem_count:
        added = kernel_call(
            add_body,
            "add",
            [jax.ShapeDtypeStruct(summed.shape, f32)],
            [IN_VMEM] * 2,
            2,
            1e10,
        )(summed, swap(sent, "mem", distance))
        summed, sent = added[0], added[-1]
        distance *= 2

    state = (kv_heads * query_count, LANES)
    partial = kernel_call(
        functools.partial(attend_body, head_dim ** (-0.5)),
        "attend",
        jax.ShapeDtypeStruct((height + 8, LANES), f32),
        [IN_SMEM] + [IN_VMEM] * 5,
        4,
        1e10,
        [pltpu.VMEM((row_count, *state), bf16), pltpu.VMEM((capacity, *state), f32)]
        + [pltpu.VMEM((row_count + 1, *state), f32)] * 6,
    )(pltpu.with_memory_space_constraint(chosen[0], pltpu.SMEM), chosen[1], summed, swap(sent.astype(jnp.float16), "mem", distance).astype(f32), k_cache, v_cache)

    sent = partial
    distance = 1
    while 2 * distance < mem_count:
        outs = [jax.ShapeDtypeStruct(partial.shape, f32)]
        if 4 * distance == mem_count:
            pad = -(-6 * state_rows(groups, query_count) // 16) * 16
            outs.append(jax.ShapeDtypeStruct((height + pad, LANES), bf16))
        merged = kernel_call(
            functools.partial(combine_body, query_count, groups),
            "combine",
            outs,
            [IN_VMEM] * 2,
            2,
            1e10,
        )(partial, swap(sent, "mem", distance))
        partial, sent = merged[0], merged[-1]
        distance *= 2

    out_cols = o_weight.shape[1]
    projected = kernel_call(
        functools.partial(output_body, kv_heads, steps, min(512, out_cols)),
        "output",
        [jax.ShapeDtypeStruct((chunk, out_cols), f32)] * head_count,
        [IN_VMEM] * 3,
        4,
        2 * token_count * query_cols * out_cols,
        [pltpu.VMEM((query_cols // LANES * token_count, LANES), f32)],
    )(partial, swap(sent, "mem", distance), o_weight)
    total = projected[0]
    for d in distances:
        total = total + swap(projected[d], "heads", d)
    return total.astype(bf16)


def solution(mesh):
    in_specs = (
        P(("groups", "heads"), None),
        P("mem"),
        P("mem", "heads"),
        P("mem", "heads"),
        P("mem", "heads"),
        P("heads", "mem"),
        P(("groups", "mem"), "heads", None, None),
        P(("groups", "mem"), "heads", None, None),
        P("groups", None),
        P("groups", None),
        P("groups"),
    )
    out_specs = P(("groups", "heads"), "mem")
    return jax.shard_map(shards, mesh=mesh, in_specs=in_specs, out_specs=out_specs, check_vma=False)
```

```python
import functools

import jax
import jax.numpy as jnp
from jax import lax
from jax.experimental import pallas as pl
from jax.experimental.pallas import tpu as pltpu
from jax.sharding import PartitionSpec as P

NEG_FILL = -1e30
EPSILON = 1e-05
LANES = 128
MIB = 1 << 20
IN_VMEM = pl.BlockSpec(memory_space=pltpu.VMEM)
IN_SMEM = pl.BlockSpec(memory_space=pltpu.SMEM)


def swap(array, axis, distance):
    count = lax.axis_size(axis)
    return lax.ppermute(array, axis, [(i, i ^ distance) for i in range(count)])


def crossing(distance):
    return distance if distance == 1 else distance + 1


def swap_across(array, distance):
    heads = lax.axis_size("heads")
    count = lax.axis_size("mem") * heads
    pairs = [(i, i ^ heads ^ distance) for i in range(count)]
    return lax.ppermute(array, ("mem", "heads"), pairs)


def kernel_call(body, name, outs, ins, vmem_mib, flops, scratch=(), out_space=IN_VMEM):
    return pl.pallas_call(
        body,
        out_shape=outs,
        in_specs=ins,
        out_specs=out_space if isinstance(out_space, list) else jax.tree.map(lambda _: out_space, outs),
        scratch_shapes=list(scratch),
        name=name,
        compiler_params=pltpu.CompilerParams(vmem_limit_bytes=vmem_mib * MIB),
        cost_estimate=pl.CostEstimate(flops=int(flops), bytes_accessed=1024, transcendentals=0),
    )


def norm_body(hidden_hbm, own_ref, mate_ref, hidden_ref, sem):
    copy = pltpu.make_async_copy(hidden_hbm, hidden_ref, sem)
    copy.start()
    copy.wait()
    cols = own_ref.shape[1] - LANES
    mem = lax.axis_index("mem")
    hidden = hidden_ref[...].astype(jnp.float32)
    factor = lax.rsqrt(jnp.mean(hidden * hidden, axis=-1, keepdims=True) + EPSILON)
    lane = lax.broadcasted_iota(jnp.int32, (hidden.shape[0], LANES), 1)
    tail = jnp.zeros((hidden.shape[0], LANES), jnp.float32)
    for i, piece in enumerate(to_pieces(factor)):
        tail = jnp.where(lane == i, piece.astype(jnp.float32), tail)
    for ref, index in ((own_ref, mem), (mate_ref, lax.bitwise_xor(mem, 1))):
        start = pl.multiple_of(index * cols, cols)
        ref[:, :cols] = hidden_ref[:, pl.ds(start, cols)]
        ref[:, cols:] = tail.astype(ref.dtype)


def select_body(
    chunk, steps, pool, block, per_kv, table_ref, list_ref, lengths_ref,
    chosen_ref, seen_ref,
):
    mem = lax.axis_index("mem")
    head_shard = lax.axis_index("heads")
    row_count, selected = list_ref.shape
    stride = chosen_ref.shape[0] // 3
    count = jnp.int32(0)
    for row in range(row_count):
        first = row * steps
        place = (lax.bitwise_xor(first // chunk, head_shard) * chunk + first % chunk) // steps
        length = lengths_ref[row]
        for i in range(selected):
            index = list_ref[row, i]
            slot = table_ref[row, index] - mem * pool
            chosen_ref[count] = slot
            chosen_ref[stride + count] = place
            chosen_ref[2 * stride + count] = length - index * block
            count += ((slot >= 0) & (slot < pool)).astype(jnp.int32)
    for c in range(stride - 1):
        live = c < count
        for at, blank in ((c, 0), (stride + c, row_count), (2 * stride + c, 0)):
            chosen_ref[at] = jnp.where(live, chosen_ref[at], blank)

    def token_of(place):
        return lax.bitwise_xor(place // chunk, head_shard) * chunk + place % chunk

    tokens = row_count * steps
    group_rows = steps * per_kv
    row_height = seen_ref.shape[0] // row_count
    at = lax.broadcasted_iota(jnp.int32, seen_ref.shape, 0)
    query_token = token_of(at // row_height * steps + at % group_rows // per_kv)
    query_head = at % row_height // group_rows
    lane = lax.broadcasted_iota(jnp.int32, seen_ref.shape, 1)
    key_head, key = lane // tokens, lane % tokens
    key_token = token_of(key % row_count * steps + key // row_count)
    seen = (
        (query_head == key_head)
        & (query_token // steps == key_token // steps)
        & (key_token <= query_token)
        & (query_token // steps % lax.axis_size("mem") == mem)
    )
    seen_ref[...] = seen.astype(jnp.float32)


def project_body(places, steps, kv_heads, tile, *refs):
    gain_ref, q_ref, k_ref, v_ref, out_ref = refs[len(places) :]
    chunks = [refs[places.index(i)][...].astype(jnp.float32) for i in range(len(places))]
    rows = jnp.concatenate(chunks, axis=0)
    cols = gain_ref.shape[0]
    factor = from_pieces([rows[:, cols + i : cols + i + 1] for i in range(3)])
    gain = gain_ref[...].astype(jnp.float32).reshape(1, cols)
    rows = (rows[:, :cols] * factor * gain).astype(jnp.bfloat16)
    tokens = rows.shape[0]
    row_count = tokens // steps
    to = lax.broadcasted_iota(jnp.int32, (tokens, tokens), 0)
    come = lax.broadcasted_iota(jnp.int32, (tokens, tokens), 1)
    order = (to % row_count * steps + to // row_count == come).astype(jnp.bfloat16)
    rows = jnp.dot(order, rows, preferred_element_type=jnp.float32).astype(jnp.bfloat16)
    heads = q_ref.shape[1] // LANES
    per_kv = heads // kv_heads
    head = 0
    for weight in (q_ref, k_ref, v_ref):
        width = min(tile, weight.shape[1])
        for col in range(0, weight.shape[1], width):
            product = jnp.dot(
                rows, weight[:, col : col + width], preferred_element_type=jnp.float32
            )
            for lane in range(0, width, LANES):
                columns = product[:, lane : lane + LANES]
                if head < heads:
                    for s in range(steps):
                        at = (head // per_kv * steps + s) * per_kv + head % per_kv
                        out_ref[pl.ds(at, row_count, stride=heads * steps)] = columns[
                            s * row_count : (s + 1) * row_count
                        ]
                else:
                    out_ref[head * tokens : (head + 1) * tokens] = columns
                head += 1


def add_body(own_ref, other_ref, out_ref, *sent_refs):
    total = own_ref[...] + other_ref[...]
    for ref in (out_ref, *sent_refs):
        ref[...] = total.astype(ref.dtype)


def split_dot(weights, values):
    high = weights.astype(jnp.bfloat16)
    low = (weights - high.astype(jnp.float32)).astype(jnp.bfloat16)
    both = jnp.dot(
        jnp.concatenate([high, low], axis=0), values, preferred_element_type=jnp.float32
    )
    return both[: weights.shape[0]] + both[weights.shape[0] :]


def to_pieces(rows):
    pieces = []
    for _ in range(3):
        pieces.append(rows.astype(jnp.bfloat16))
        rows = rows - pieces[-1].astype(jnp.float32)
    return pieces


def from_pieces(pieces):
    high, middle, low = [piece.astype(jnp.float32) for piece in pieces]
    return low + middle + high


def group_lanes(query_count):
    lane = lax.broadcasted_iota(jnp.int32, (query_count, LANES), 1)
    row = lax.broadcasted_iota(jnp.int32, (query_count, LANES), 0)
    return lane - row


def pack_columns(column, query_count):
    per_row = LANES // query_count
    offset = group_lanes(query_count)
    groups = column.shape[0] // query_count
    rows = []
    for first in range(0, groups, per_row):
        row = jnp.zeros((query_count, LANES), jnp.float32)
        for i in range(min(per_row, groups - first)):
            at = (first + i) * query_count
            row = jnp.where(offset == i * query_count, column[at : at + query_count], row)
        rows.append(jnp.sum(row, axis=0, keepdims=True))
    return rows


def unpack_column(row, place, query_count):
    spread = jnp.broadcast_to(row, (query_count, LANES))
    picked = jnp.where(group_lanes(query_count) == place * query_count, spread, 0.0)
    return jnp.sum(picked, axis=1, keepdims=True)


def attend_body(
    scale,
    chosen_ref,
    seen_ref,
    own_ref,
    other_ref,
    key_ref,
    value_ref,
    out_ref,
    query_ref,
    score_ref,
    total_ref,
    accum_ref,
    *peak_refs,
):
    row_count, row_height, head_dim = query_ref.shape
    kv_heads = key_ref.shape[1]
    query_count = row_height // kv_heads
    capacity = score_ref.shape[0]
    height = row_count * row_height
    contract_last = (((1,), (1,)), ((), ()))

    projected = (own_ref[...] + other_ref[...]).astype(jnp.bfloat16)
    queries = projected[:height]
    query_ref[...] = queries.reshape(query_ref.shape)
    fresh = projected[height:]
    count = fresh.shape[0] // 2
    spare = jnp.zeros((LANES - count, head_dim), jnp.bfloat16)
    seen = seen_ref[...] > 0
    fresh_score = lax.dot_general(
        queries,
        jnp.concatenate([fresh[:count], spare], axis=0),
        contract_last,
        preferred_element_type=jnp.float32,
    )
    fresh_score = jnp.where(seen, fresh_score * scale, NEG_FILL)
    peak_ref = peak_refs[0]
    peak_ref[:row_count] = fresh_score.reshape(row_count, row_height, LANES)
    peak_ref[row_count] = jnp.full((row_height, LANES), NEG_FILL, jnp.float32)
    for ref in peak_refs[1:]:
        ref[...] = jnp.full(ref.shape, NEG_FILL, jnp.float32)
    stride = chosen_ref.shape[0] // 3

    lane = lax.broadcasted_iota(jnp.int32, (row_height, LANES), 1)
    for c in range(capacity):
        slot, row, valid = (chosen_ref[i * stride + c] for i in range(3))
        every = lax.dot_general(
            query_ref[jnp.minimum(row, row_count - 1)],
            key_ref[slot].reshape(kv_heads * LANES, head_dim),
            contract_last,
            preferred_element_type=jnp.float32,
        )
        score = jnp.concatenate(
            [
                every[g * query_count : (g + 1) * query_count, g * LANES : (g + 1) * LANES]
                for g in range(kv_heads)
            ],
            axis=0,
        )
        score = jnp.where(lane < valid, score * scale, NEG_FILL)
        score_ref[c] = score
        ref = peak_refs[c % len(peak_refs)]
        ref[row] = jnp.maximum(ref[row], score)

    peak = functools.reduce(jnp.maximum, [ref[:row_count] for ref in peak_refs])
    peak = jnp.max(peak.reshape(height, LANES), axis=1, keepdims=True)
    peak = jnp.broadcast_to(peak, (height, LANES))
    peak_ref[:row_count] = peak.reshape(row_count, row_height, LANES)
    weights = jnp.where(seen, jnp.exp(fresh_score - peak), 0.0)
    total_ref[:row_count] = weights.reshape(row_count, row_height, LANES)
    total_ref[row_count] = jnp.zeros((row_height, LANES), jnp.float32)
    accum = split_dot(weights, jnp.concatenate([fresh[count:], spare], axis=0))
    accum_ref[:row_count] = accum.reshape(row_count, row_height, head_dim)
    accum_ref[row_count] = jnp.zeros((row_height, head_dim), jnp.float32)

    for c in range(capacity):
        slot, row = chosen_ref[c], chosen_ref[stride + c]
        weights = jnp.exp(score_ref[c] - peak_ref[row])
        total_ref[row] += weights
        high = weights.astype(jnp.bfloat16)
        low = (weights - high.astype(jnp.float32)).astype(jnp.bfloat16)
        split = []
        for g in range(kv_heads):
            at = slice(g * query_count, (g + 1) * query_count)
            half = jnp.concatenate([high[at], low[at]], axis=0)
            blank = jnp.zeros_like(half)
            split.append(
                jnp.concatenate([half if i == g else blank for i in range(kv_heads)], axis=1)
            )
        both = jnp.dot(
            jnp.concatenate(split, axis=0),
            value_ref[slot].reshape(kv_heads * LANES, head_dim),
            preferred_element_type=jnp.float32,
        ).reshape(kv_heads, 2, query_count, head_dim)
        accum_ref[row] += (both[:, 0] + both[:, 1]).reshape(row_height, head_dim)

    total = jnp.sum(total_ref[:row_count].reshape(height, LANES), axis=1, keepdims=True)
    total = jnp.broadcast_to(total, (height, LANES))
    out_ref[:height] = accum_ref[:row_count].reshape(height, head_dim)
    packed = pack_columns(peak, query_count) + pack_columns(total, query_count)
    spare = out_ref.shape[0] - height - len(packed)
    packed.append(jnp.zeros((spare, LANES), jnp.float32))
    out_ref[height:] = jnp.concatenate(packed, axis=0)


def state_rows(groups, query_count):
    return -(-groups // (LANES // query_count))


def merge_states(query_count, groups, last, own_ref, other_ref):
    per_row = LANES // query_count
    height = groups * query_count
    rows = state_rows(groups, query_count)
    own_peak, own_total = (own_ref[height + i * rows : height + (i + 1) * rows] for i in range(2))
    if other_ref.dtype == jnp.bfloat16:
        tail = other_ref[height:]
        pieces = [tail[i * rows : (i + 1) * rows] for i in range(6)]
        other_peak, other_total = from_pieces(pieces[:3]), from_pieces(pieces[3:])
    else:
        other_peak, other_total = (
            other_ref[height + i * rows : height + (i + 1) * rows] for i in range(2)
        )
    peak = jnp.maximum(own_peak, other_peak)
    own_factor, other_factor = jnp.exp(own_peak - peak), jnp.exp(other_peak - peak)
    total = own_total * own_factor + other_total * other_factor
    if last:
        own_factor, other_factor = own_factor / total, other_factor / total
    values = []
    for group in range(groups):
        row, place = divmod(group, per_row)
        at = slice(group * query_count, (group + 1) * query_count)
        values.append(
            own_ref[at] * unpack_column(own_factor[row : row + 1], place, query_count)
            + other_ref[at].astype(jnp.float32)
            * unpack_column(other_factor[row : row + 1], place, query_count)
        )
    return peak, total, values


def combine_body(query_count, groups, own_ref, other_ref, *out_refs):
    height = groups * query_count
    peak, total, values = merge_states(query_count, groups, False, own_ref, other_ref)
    for ref in out_refs:
        tail = [peak, total]
        if ref.dtype == jnp.bfloat16:
            tail = to_pieces(peak) + to_pieces(total)
        spare = ref.shape[0] - height - len(tail) * peak.shape[0]
        tail.append(jnp.zeros((spare, LANES), ref.dtype))
        ref[height:] = jnp.concatenate(tail, axis=0)
        for group, value in enumerate(values):
            ref[group * query_count : (group + 1) * query_count] = value.astype(ref.dtype)


def output_body(kv_heads, steps, tile, own_ref, other_ref, weight_ref, *refs):
    out_refs, wide_ref = refs[:-1], refs[-1]
    heads = weight_ref.shape[0] // LANES
    per_kv = heads // kv_heads
    tokens = wide_ref.shape[0] // heads
    groups = tokens // steps * kv_heads
    _, _, values = merge_states(steps * per_kv, groups, True, own_ref, other_ref)
    for group, value in enumerate(values):
        row, g = divmod(group, kv_heads)
        for s in range(steps):
            first = g * per_kv * tokens + row * steps + s
            wide_ref[pl.ds(first, per_kv, stride=tokens)] = value[s * per_kv : (s + 1) * per_kv]
    rows = jnp.concatenate(
        [wide_ref[j * tokens : (j + 1) * tokens].astype(jnp.bfloat16) for j in range(heads)], axis=1
    )
    chunk = out_refs[0].shape[0]
    for col in range(0, weight_ref.shape[1], tile):
        product = jnp.dot(
            rows, weight_ref[:, col : col + tile], preferred_element_type=jnp.float32
        )
        for i, out_ref in enumerate(out_refs):
            out_ref[:, col : col + tile] = product[i * chunk : (i + 1) * chunk]


def shards(
    hidden,
    norm_gain,
    q_weight,
    k_weight,
    v_weight,
    o_weight,
    k_cache,
    v_cache,
    page_table,
    attend_list,
    lengths,
):
    mem_count, head_count = lax.axis_size("mem"), lax.axis_size("heads")
    chunk = hidden.shape[0]
    feature_cols = norm_gain.shape[0]
    query_cols, value_cols = q_weight.shape[1], k_weight.shape[1]
    pool, kv_heads, block, head_dim = k_cache.shape
    row_count, selected = attend_list.shape
    token_count = chunk * head_count
    steps = token_count // row_count
    per_kv = query_cols // head_dim // kv_heads
    query_count = steps * per_kv
    capacity = 2 * row_count * selected // mem_count
    groups = row_count * kv_heads
    height = groups * query_count
    f32, bf16 = jnp.float32, jnp.bfloat16

    own, mate = kernel_call(
        norm_body,
        "norm",
        [jax.ShapeDtypeStruct((chunk, feature_cols + LANES), bf16)] * 2,
        [pl.BlockSpec(memory_space=pltpu.HBM)],
        2,
        1e10,
        [pltpu.VMEM(hidden.shape, bf16), pltpu.SemaphoreType.DMA],
    )(pltpu.with_memory_space_constraint(hidden, pltpu.HBM))
    distances = [*range(2, head_count), 1]
    pieces = [own] + [swap_across(mate, d) for d in distances]

    chosen = kernel_call(
        functools.partial(select_body, chunk, steps, pool, block, per_kv),
        "select",
        [
            pltpu.SMEM((3 * (capacity + 1),), jnp.int32),
            jax.ShapeDtypeStruct((height, LANES), f32),
        ],
        [IN_SMEM] * 3,
        2,
        1e10,
        out_space=[IN_SMEM, IN_VMEM],
    )(page_table, attend_list, lengths)

    width = query_cols + 2 * value_cols
    summed = kernel_call(
        functools.partial(project_body, (0, *distances), steps, kv_heads, 512),
        "project",
        jax.ShapeDtypeStruct((width // LANES * token_count, LANES), f32),
        [IN_VMEM] * (head_count + 4),
        4,
        2 * token_count * feature_cols * width,
    )(*pieces, norm_gain, q_weight, k_weight, v_weight)
    sent = summed
    distance = 1
    while 2 * distance < mem_count:
        added = kernel_call(
            add_body,
            "add",
            [jax.ShapeDtypeStruct(summed.shape, f32)],
            [IN_VMEM] * 2,
            2,
            1e10,
        )(summed, swap(sent, "mem", crossing(distance)))
        summed, sent = added[0], added[-1]
        distance *= 2

    state = (kv_heads * query_count, LANES)
    partial = kernel_call(
        functools.partial(attend_body, head_dim ** (-0.5)),
        "attend",
        jax.ShapeDtypeStruct((height + 8, LANES), f32),
        [IN_SMEM] + [IN_VMEM] * 5,
        4,
        1e10,
        [pltpu.VMEM((row_count, *state), bf16), pltpu.VMEM((capacity, *state), f32)]
        + [pltpu.VMEM((row_count + 1, *state), f32)] * 6,
    )(pltpu.with_memory_space_constraint(chosen[0], pltpu.SMEM), chosen[1], summed, swap(sent.astype(jnp.float16), "mem", crossing(distance)).astype(f32), k_cache, v_cache)

    sent = partial
    distance = 1
    while 2 * distance < mem_count:
        outs = [jax.ShapeDtypeStruct(partial.shape, f32)]
        if 4 * distance == mem_count:
            pad = -(-6 * state_rows(groups, query_count) // 16) * 16
            outs.append(jax.ShapeDtypeStruct((height + pad, LANES), bf16))
        merged = kernel_call(
            functools.partial(combine_body, query_count, groups),
            "combine",
            outs,
            [IN_VMEM] * 2,
            2,
            1e10,
        )(partial, swap(sent, "mem", crossing(distance)))
        partial, sent = merged[0], merged[-1]
        distance *= 2

    out_cols = o_weight.shape[1]
    projected = kernel_call(
        functools.partial(output_body, kv_heads, steps, min(512, out_cols)),
        "output",
        [jax.ShapeDtypeStruct((chunk, out_cols), f32)] * head_count,
        [IN_VMEM] * 3,
        4,
        2 * token_count * query_cols * out_cols,
        [pltpu.VMEM((query_cols // LANES * token_count, LANES), f32)],
    )(partial, swap(sent, "mem", crossing(distance)), o_weight)
    total = projected[0]
    for d in distances:
        total = total + swap(projected[d], "heads", d)
    return total.astype(bf16)


def solution(mesh):
    in_specs = (
        P(("groups", "heads"), None),
        P("mem"),
        P("mem", "heads"),
        P("mem", "heads"),
        P("mem", "heads"),
        P("heads", "mem"),
        P(("groups", "mem"), "heads", None, None),
        P(("groups", "mem"), "heads", None, None),
        P("groups", None),
        P("groups", None),
        P("groups"),
    )
    out_specs = P(("groups", "heads"), "mem")
    return jax.shard_map(shards, mesh=mesh, in_specs=in_specs, out_specs=out_specs, check_vma=False)
```

```python
import functools

import jax
import jax.numpy as jnp
from jax import lax
from jax.experimental import pallas as pl
from jax.experimental.pallas import tpu as pltpu
from jax.sharding import PartitionSpec as P

NEG_FILL = -1e30
EPSILON = 1e-05
LANES = 128
MIB = 1 << 20
IN_VMEM = pl.BlockSpec(memory_space=pltpu.VMEM)
IN_SMEM = pl.BlockSpec(memory_space=pltpu.SMEM)


def swap(array, axis, distance):
    count = lax.axis_size(axis)
    return lax.ppermute(array, axis, [(i, i ^ distance) for i in range(count)])


def crossing(distance):
    return distance if distance == 1 else distance + 1


def swap_across(array, distance):
    heads = lax.axis_size("heads")
    count = lax.axis_size("mem") * heads
    pairs = [(i, i ^ heads ^ distance) for i in range(count)]
    return lax.ppermute(array, ("mem", "heads"), pairs)


def kernel_call(body, name, outs, ins, vmem_mib, flops, scratch=(), out_space=IN_VMEM):
    return pl.pallas_call(
        body,
        out_shape=outs,
        in_specs=ins,
        out_specs=out_space if isinstance(out_space, list) else jax.tree.map(lambda _: out_space, outs),
        scratch_shapes=list(scratch),
        name=name,
        compiler_params=pltpu.CompilerParams(vmem_limit_bytes=vmem_mib * MIB),
        cost_estimate=pl.CostEstimate(flops=int(flops), bytes_accessed=1024, transcendentals=0),
    )


def norm_body(hidden_hbm, own_ref, mate_ref, hidden_ref, sem):
    copy = pltpu.make_async_copy(hidden_hbm, hidden_ref, sem)
    copy.start()
    copy.wait()
    cols = own_ref.shape[1] - LANES
    mem = lax.axis_index("mem")
    hidden = hidden_ref[...].astype(jnp.float32)
    factor = lax.rsqrt(jnp.mean(hidden * hidden, axis=-1, keepdims=True) + EPSILON)
    lane = lax.broadcasted_iota(jnp.int32, (hidden.shape[0], LANES), 1)
    tail = jnp.zeros((hidden.shape[0], LANES), jnp.float32)
    for i, piece in enumerate(to_pieces(factor)):
        tail = jnp.where(lane == i, piece.astype(jnp.float32), tail)
    for ref, index in ((own_ref, mem), (mate_ref, lax.bitwise_xor(mem, 1))):
        start = pl.multiple_of(index * cols, cols)
        ref[:, :cols] = hidden_ref[:, pl.ds(start, cols)]
        ref[:, cols:] = tail.astype(ref.dtype)


def select_body(
    chunk, steps, per_kv, table_ref, list_ref, lengths_ref, key_ref, chosen_ref, seen_ref, turned_ref
):
    pool, kv_heads, block, head_dim = key_ref.shape
    mem = lax.axis_index("mem")
    head_shard = lax.axis_index("heads")
    row_count, selected = list_ref.shape
    stride = chosen_ref.shape[0] // 3
    count = jnp.int32(0)
    for row in range(row_count):
        first = row * steps
        place = (lax.bitwise_xor(first // chunk, head_shard) * chunk + first % chunk) // steps
        length = lengths_ref[row]
        for i in range(selected):
            index = list_ref[row, i]
            slot = table_ref[row, index] - mem * pool
            chosen_ref[count] = slot
            chosen_ref[stride + count] = place
            chosen_ref[2 * stride + count] = length - index * block
            count += ((slot >= 0) & (slot < pool)).astype(jnp.int32)
    for c in range(stride - 1):
        live = c < count
        for at, blank in ((c, 0), (stride + c, row_count), (2 * stride + c, 0)):
            chosen_ref[at] = jnp.where(live, chosen_ref[at], blank)
        keys = key_ref[chosen_ref[c]]
        for g in range(kv_heads):
            turned_ref[c, :, g * block : (g + 1) * block] = keys[g].T

    def token_of(place):
        return lax.bitwise_xor(place // chunk, head_shard) * chunk + place % chunk

    tokens = row_count * steps
    heads = kv_heads * per_kv
    at = lax.broadcasted_iota(jnp.int32, seen_ref.shape, 0)
    query_token = token_of(at // heads)
    query_head = at % heads // per_kv
    lane = lax.broadcasted_iota(jnp.int32, seen_ref.shape, 1)
    key_head, key = lane // tokens, lane % tokens
    key_token = token_of(key)
    seen = (
        (query_head == key_head)
        & (query_token // steps == key_token // steps)
        & (key_token <= query_token)
        & (query_token // steps % lax.axis_size("mem") == mem)
    )
    seen_ref[...] = seen.astype(jnp.float32)


def project_body(places, tile, *refs):
    gain_ref, q_ref, k_ref, v_ref, out_ref = refs[len(places) :]
    chunks = [refs[places.index(i)][...].astype(jnp.float32) for i in range(len(places))]
    rows = jnp.concatenate(chunks, axis=0)
    cols = gain_ref.shape[0]
    factor = from_pieces([rows[:, cols + i : cols + i + 1] for i in range(3)])
    gain = gain_ref[...].astype(jnp.float32).reshape(1, cols)
    rows = (rows[:, :cols] * factor * gain).astype(jnp.bfloat16)
    tokens = rows.shape[0]
    heads = q_ref.shape[1] // LANES
    head = 0
    for weight in (q_ref, k_ref, v_ref):
        width = min(tile, weight.shape[1])
        for col in range(0, weight.shape[1], width):
            product = jnp.dot(
                rows, weight[:, col : col + width], preferred_element_type=jnp.float32
            )
            for lane in range(0, width, LANES):
                columns = product[:, lane : lane + LANES]
                if head < heads:
                    out_ref[pl.ds(head, tokens, stride=heads)] = columns
                else:
                    out_ref[head * tokens : (head + 1) * tokens] = columns
                head += 1


def add_body(own_ref, other_ref, out_ref, *sent_refs):
    total = own_ref[...] + other_ref[...]
    for ref in (out_ref, *sent_refs):
        ref[...] = total.astype(ref.dtype)


def split_dot(weights, values):
    high = weights.astype(jnp.bfloat16)
    low = (weights - high.astype(jnp.float32)).astype(jnp.bfloat16)
    both = jnp.dot(
        jnp.concatenate([high, low], axis=0), values, preferred_element_type=jnp.float32
    )
    return both[: weights.shape[0]] + both[weights.shape[0] :]


def to_pieces(rows):
    pieces = []
    for _ in range(3):
        pieces.append(rows.astype(jnp.bfloat16))
        rows = rows - pieces[-1].astype(jnp.float32)
    return pieces


def from_pieces(pieces):
    high, middle, low = [piece.astype(jnp.float32) for piece in pieces]
    return low + middle + high


def group_lanes(query_count):
    lane = lax.broadcasted_iota(jnp.int32, (query_count, LANES), 1)
    row = lax.broadcasted_iota(jnp.int32, (query_count, LANES), 0)
    return lane - row


def pack_columns(column, query_count):
    per_row = LANES // query_count
    offset = group_lanes(query_count)
    groups = column.shape[0] // query_count
    rows = []
    for first in range(0, groups, per_row):
        row = jnp.zeros((query_count, LANES), jnp.float32)
        for i in range(min(per_row, groups - first)):
            at = (first + i) * query_count
            row = jnp.where(offset == i * query_count, column[at : at + query_count], row)
        rows.append(jnp.sum(row, axis=0, keepdims=True))
    return rows


def unpack_column(row, place, query_count):
    spread = jnp.broadcast_to(row, (query_count, LANES))
    picked = jnp.where(group_lanes(query_count) == place * query_count, spread, 0.0)
    return jnp.sum(picked, axis=1, keepdims=True)


def attend_body(
    scale,
    heads,
    query_count,
    chosen_ref,
    seen_ref,
    own_ref,
    other_ref,
    turned_ref,
    value_ref,
    out_ref,
    query_ref,
    score_ref,
    total_ref,
    accum_ref,
    *peak_refs,
):
    row_count, row_height, head_dim = query_ref.shape
    kv_heads = value_ref.shape[1]
    capacity = score_ref.shape[0]
    height = row_count * row_height
    contract_last = (((1,), (1,)), ((), ()))

    projected = (own_ref[...] + other_ref[...]).astype(jnp.bfloat16)
    queries = projected[:height]
    query_ref[...] = queries.reshape(query_ref.shape)
    fresh = projected[height:]
    count = fresh.shape[0] // 2
    spare = jnp.zeros((LANES - count, head_dim), jnp.bfloat16)
    seen = seen_ref[...] > 0
    fresh_score = lax.dot_general(
        queries,
        jnp.concatenate([fresh[:count], spare], axis=0),
        contract_last,
        preferred_element_type=jnp.float32,
    )
    fresh_score = jnp.where(seen, fresh_score * scale, NEG_FILL)
    peak_ref = peak_refs[0]
    peak_ref[:row_count] = fresh_score.reshape(row_count, row_height, LANES)
    peak_ref[row_count] = jnp.full((row_height, LANES), NEG_FILL, jnp.float32)
    for ref in peak_refs[1:]:
        ref[...] = jnp.full(ref.shape, NEG_FILL, jnp.float32)
    stride = chosen_ref.shape[0] // 3

    lane = lax.broadcasted_iota(jnp.int32, (row_height, LANES), 1)
    head_of = lax.broadcasted_iota(jnp.int32, (row_height, LANES), 0) % heads // (heads // kv_heads)
    for c in range(capacity):
        slot, row, valid = (chosen_ref[i * stride + c] for i in range(3))
        every = jnp.dot(
            query_ref[jnp.minimum(row, row_count - 1)],
            turned_ref[c],
            preferred_element_type=jnp.float32,
        )
        score = every[:, :LANES]
        for g in range(1, kv_heads):
            score = jnp.where(head_of == g, every[:, g * LANES : (g + 1) * LANES], score)
        score = jnp.where(lane < valid, score * scale, NEG_FILL)
        score_ref[c] = score
        ref = peak_refs[c % len(peak_refs)]
        ref[row] = jnp.maximum(ref[row], score)

    peak = functools.reduce(jnp.maximum, [ref[:row_count] for ref in peak_refs])
    peak = jnp.max(peak.reshape(height, LANES), axis=1, keepdims=True)
    peak = jnp.broadcast_to(peak, (height, LANES))
    peak_ref[:row_count] = peak.reshape(row_count, row_height, LANES)
    weights = jnp.where(seen, jnp.exp(fresh_score - peak), 0.0)
    total_ref[:row_count] = weights.reshape(row_count, row_height, LANES)
    total_ref[row_count] = jnp.zeros((row_height, LANES), jnp.float32)
    accum = split_dot(weights, jnp.concatenate([fresh[count:], spare], axis=0))
    accum_ref[:row_count] = accum.reshape(row_count, row_height, head_dim)
    accum_ref[row_count] = jnp.zeros((row_height, head_dim), jnp.float32)

    for c in range(capacity):
        slot, row = chosen_ref[c], chosen_ref[stride + c]
        weights = jnp.exp(score_ref[c] - peak_ref[row])
        total_ref[row] += weights
        spread = [jnp.where(head_of == g, weights, 0.0) for g in range(kv_heads)]
        accum_ref[row] += split_dot(
            jnp.concatenate(spread, axis=1), value_ref[slot].reshape(kv_heads * LANES, head_dim)
        )

    total = jnp.sum(total_ref[:row_count].reshape(height, LANES), axis=1, keepdims=True)
    total = jnp.broadcast_to(total, (height, LANES))
    out_ref[:height] = accum_ref[:row_count].reshape(height, head_dim)
    packed = pack_columns(peak, query_count) + pack_columns(total, query_count)
    spare = out_ref.shape[0] - height - len(packed)
    packed.append(jnp.zeros((spare, LANES), jnp.float32))
    out_ref[height:] = jnp.concatenate(packed, axis=0)


def state_rows(groups, query_count):
    return -(-groups // (LANES // query_count))


def merge_states(query_count, groups, last, own_ref, other_ref):
    per_row = LANES // query_count
    height = groups * query_count
    rows = state_rows(groups, query_count)
    own_peak, own_total = (own_ref[height + i * rows : height + (i + 1) * rows] for i in range(2))
    if other_ref.dtype == jnp.bfloat16:
        tail = other_ref[height:]
        pieces = [tail[i * rows : (i + 1) * rows] for i in range(6)]
        other_peak, other_total = from_pieces(pieces[:3]), from_pieces(pieces[3:])
    else:
        other_peak, other_total = (
            other_ref[height + i * rows : height + (i + 1) * rows] for i in range(2)
        )
    peak = jnp.maximum(own_peak, other_peak)
    own_factor, other_factor = jnp.exp(own_peak - peak), jnp.exp(other_peak - peak)
    total = own_total * own_factor + other_total * other_factor
    if last:
        own_factor, other_factor = own_factor / total, other_factor / total
    values = []
    for group in range(groups):
        row, place = divmod(group, per_row)
        at = slice(group * query_count, (group + 1) * query_count)
        values.append(
            own_ref[at] * unpack_column(own_factor[row : row + 1], place, query_count)
            + other_ref[at].astype(jnp.float32)
            * unpack_column(other_factor[row : row + 1], place, query_count)
        )
    return peak, total, values


def combine_body(query_count, groups, own_ref, other_ref, *out_refs):
    height = groups * query_count
    peak, total, values = merge_states(query_count, groups, False, own_ref, other_ref)
    for ref in out_refs:
        tail = [peak, total]
        if ref.dtype == jnp.bfloat16:
            tail = to_pieces(peak) + to_pieces(total)
        spare = ref.shape[0] - height - len(tail) * peak.shape[0]
        tail.append(jnp.zeros((spare, LANES), ref.dtype))
        ref[height:] = jnp.concatenate(tail, axis=0)
        for group, value in enumerate(values):
            ref[group * query_count : (group + 1) * query_count] = value.astype(ref.dtype)


def output_body(query_count, tile, own_ref, other_ref, weight_ref, *refs):
    out_refs, wide_ref = refs[:-1], refs[-1]
    heads = weight_ref.shape[0] // LANES
    tokens = wide_ref.shape[0] // heads
    groups = wide_ref.shape[0] // query_count
    _, _, values = merge_states(query_count, groups, True, own_ref, other_ref)
    for group, value in enumerate(values):
        wide_ref[group * query_count : (group + 1) * query_count] = value
    rows = [wide_ref[pl.ds(head, tokens, stride=heads)] for head in range(heads)]
    rows = jnp.concatenate(rows, axis=1).astype(jnp.bfloat16)
    chunk = out_refs[0].shape[0]
    for col in range(0, weight_ref.shape[1], tile):
        product = jnp.dot(
            rows, weight_ref[:, col : col + tile], preferred_element_type=jnp.float32
        )
        for i, out_ref in enumerate(out_refs):
            out_ref[:, col : col + tile] = product[i * chunk : (i + 1) * chunk]


def shards(
    hidden,
    norm_gain,
    q_weight,
    k_weight,
    v_weight,
    o_weight,
    k_cache,
    v_cache,
    page_table,
    attend_list,
    lengths,
):
    mem_count, head_count = lax.axis_size("mem"), lax.axis_size("heads")
    chunk = hidden.shape[0]
    feature_cols = norm_gain.shape[0]
    query_cols, value_cols = q_weight.shape[1], k_weight.shape[1]
    pool, kv_heads, block, head_dim = k_cache.shape
    row_count, selected = attend_list.shape
    token_count = chunk * head_count
    steps = token_count // row_count
    per_kv = query_cols // head_dim // kv_heads
    query_count = steps * per_kv
    capacity = 2 * row_count * selected // mem_count
    groups = row_count * kv_heads
    height = groups * query_count
    f32, bf16 = jnp.float32, jnp.bfloat16

    own, mate = kernel_call(
        norm_body,
        "norm",
        [jax.ShapeDtypeStruct((chunk, feature_cols + LANES), bf16)] * 2,
        [pl.BlockSpec(memory_space=pltpu.HBM)],
        2,
        1e10,
        [pltpu.VMEM(hidden.shape, bf16), pltpu.SemaphoreType.DMA],
    )(pltpu.with_memory_space_constraint(hidden, pltpu.HBM))
    distances = [*range(2, head_count), 1]
    gathered = distances[::-1]
    pieces = [own] + [swap_across(mate, d) for d in gathered]

    chosen, seen, turned = kernel_call(
        functools.partial(select_body, chunk, steps, per_kv),
        "select",
        [
            pltpu.SMEM((3 * (capacity + 1),), jnp.int32),
            jax.ShapeDtypeStruct((height, LANES), f32),
            jax.ShapeDtypeStruct((capacity, head_dim, kv_heads * block), bf16),
        ],
        [IN_SMEM] * 3 + [IN_VMEM],
        4,
        1e10,
        out_space=[IN_SMEM, IN_VMEM, IN_VMEM],
    )(page_table, attend_list, lengths, k_cache)

    width = query_cols + 2 * value_cols
    summed = kernel_call(
        functools.partial(project_body, (0, *gathered), 512),
        "project",
        jax.ShapeDtypeStruct((width // LANES * token_count, LANES), f32),
        [IN_VMEM] * (head_count + 4),
        4,
        2 * token_count * feature_cols * width,
    )(*pieces, norm_gain, q_weight, k_weight, v_weight)
    sent = summed
    distance = 1
    while 2 * distance < mem_count:
        added = kernel_call(
            add_body,
            "add",
            [jax.ShapeDtypeStruct(summed.shape, f32)],
            [IN_VMEM] * 2,
            2,
            1e10,
        )(summed, swap(sent, "mem", crossing(distance)))
        summed, sent = added[0], added[-1]
        distance *= 2

    state = (kv_heads * query_count, LANES)
    partial = kernel_call(
        functools.partial(attend_body, head_dim ** (-0.5), kv_heads * per_kv, query_count),
        "attend",
        jax.ShapeDtypeStruct((height + 8, LANES), f32),
        [IN_SMEM] + [IN_VMEM] * 5,
        4,
        1e10,
        [pltpu.VMEM((row_count, *state), bf16), pltpu.VMEM((capacity, *state), f32)]
        + [pltpu.VMEM((row_count + 1, *state), f32)] * 6,
    )(
        pltpu.with_memory_space_constraint(chosen, pltpu.SMEM),
        seen,
        summed,
        swap(sent.astype(jnp.float16), "mem", crossing(distance)).astype(f32),
        turned,
        v_cache,
    )

    sent = partial
    distance = 1
    while 2 * distance < mem_count:
        outs = [jax.ShapeDtypeStruct(partial.shape, f32)]
        if 4 * distance == mem_count:
            pad = -(-6 * state_rows(groups, query_count) // 16) * 16
            outs.append(jax.ShapeDtypeStruct((height + pad, LANES), bf16))
        merged = kernel_call(
            functools.partial(combine_body, query_count, groups),
            "combine",
            outs,
            [IN_VMEM] * 2,
            2,
            1e10,
        )(partial, swap(sent, "mem", crossing(distance)))
        partial, sent = merged[0], merged[-1]
        distance *= 2

    out_cols = o_weight.shape[1]
    projected = kernel_call(
        functools.partial(output_body, query_count, min(512, out_cols)),
        "output",
        [jax.ShapeDtypeStruct((chunk, out_cols), f32)] * head_count,
        [IN_VMEM] * 3,
        4,
        2 * token_count * query_cols * out_cols,
        [pltpu.VMEM((query_cols // LANES * token_count, LANES), f32)],
    )(partial, swap(sent, "mem", crossing(distance)), o_weight)
    total = projected[0]
    for d in distances:
        total = total + swap(projected[d], "heads", d)
    return total.astype(bf16)


def solution(mesh):
    in_specs = (
        P(("groups", "heads"), None),
        P("mem"),
        P("mem", "heads"),
        P("mem", "heads"),
        P("mem", "heads"),
        P("heads", "mem"),
        P(("groups", "mem"), "heads", None, None),
        P(("groups", "mem"), "heads", None, None),
        P("groups", None),
        P("groups", None),
        P("groups"),
    )
    out_specs = P(("groups", "heads"), "mem")
    return jax.shard_map(shards, mesh=mesh, in_specs=in_specs, out_specs=out_specs, check_vma=False)
```

```python
import functools

import jax
import jax.numpy as jnp
from jax import lax
from jax.experimental import pallas as pl
from jax.experimental.pallas import tpu as pltpu
from jax.sharding import PartitionSpec as P

NEG_FILL = -1e30
EPSILON = 1e-05
LANES = 128
MIB = 1 << 20
IN_VMEM = pl.BlockSpec(memory_space=pltpu.VMEM)
IN_SMEM = pl.BlockSpec(memory_space=pltpu.SMEM)


def swap(array, axis, distance):
    count = lax.axis_size(axis)
    return lax.ppermute(array, axis, [(i, i ^ distance) for i in range(count)])


def crossing(distance):
    return distance if distance == 1 else distance + 1


def swap_across(array, distance):
    heads = lax.axis_size("heads")
    count = lax.axis_size("mem") * heads
    pairs = [(i, i ^ heads ^ distance) for i in range(count)]
    return lax.ppermute(array, ("mem", "heads"), pairs)


def kernel_call(body, name, outs, ins, vmem_mib, flops, scratch=(), out_space=IN_VMEM):
    return pl.pallas_call(
        body,
        out_shape=outs,
        in_specs=ins,
        out_specs=out_space if isinstance(out_space, list) else jax.tree.map(lambda _: out_space, outs),
        scratch_shapes=list(scratch),
        name=name,
        compiler_params=pltpu.CompilerParams(vmem_limit_bytes=vmem_mib * MIB),
        cost_estimate=pl.CostEstimate(flops=int(flops), bytes_accessed=1024, transcendentals=0),
    )


def norm_body(hidden_hbm, own_ref, mate_ref, hidden_ref, sem):
    copy = pltpu.make_async_copy(hidden_hbm, hidden_ref, sem)
    copy.start()
    copy.wait()
    cols = own_ref.shape[1] - LANES
    mem = lax.axis_index("mem")
    hidden = hidden_ref[...].astype(jnp.float32)
    factor = lax.rsqrt(jnp.mean(hidden * hidden, axis=-1, keepdims=True) + EPSILON)
    lane = lax.broadcasted_iota(jnp.int32, (hidden.shape[0], LANES), 1)
    tail = jnp.zeros((hidden.shape[0], LANES), jnp.float32)
    for i, piece in enumerate(to_pieces(factor)):
        tail = jnp.where(lane == i, piece.astype(jnp.float32), tail)
    for ref, index in ((own_ref, mem), (mate_ref, lax.bitwise_xor(mem, 1))):
        start = pl.multiple_of(index * cols, cols)
        ref[:, :cols] = hidden_ref[:, pl.ds(start, cols)]
        ref[:, cols:] = tail.astype(ref.dtype)


def select_body(
    chunk, steps, per_kv, table_ref, list_ref, lengths_ref, key_ref, chosen_ref, seen_ref, turned_ref
):
    pool, kv_heads, block, head_dim = key_ref.shape
    mem = lax.axis_index("mem")
    head_shard = lax.axis_index("heads")
    row_count, selected = list_ref.shape
    stride = chosen_ref.shape[0] // 3
    count = jnp.int32(0)
    for row in range(row_count):
        first = row * steps
        place = (lax.bitwise_xor(first // chunk, head_shard) * chunk + first % chunk) // steps
        length = lengths_ref[row]
        for i in range(selected):
            index = list_ref[row, i]
            slot = table_ref[row, index] - mem * pool
            chosen_ref[count] = slot
            chosen_ref[stride + count] = place
            chosen_ref[2 * stride + count] = length - index * block
            count += ((slot >= 0) & (slot < pool)).astype(jnp.int32)
    for c in range(stride - 1):
        live = c < count
        for at, blank in ((c, 0), (stride + c, row_count), (2 * stride + c, 0)):
            chosen_ref[at] = jnp.where(live, chosen_ref[at], blank)
        keys = key_ref[chosen_ref[c]]
        for g in range(kv_heads):
            turned_ref[c, :, g * block : (g + 1) * block] = keys[g].T

    def token_of(place):
        return lax.bitwise_xor(place // chunk, head_shard) * chunk + place % chunk

    tokens = row_count * steps
    heads = kv_heads * per_kv
    at = lax.broadcasted_iota(jnp.int32, seen_ref.shape, 0)
    query_token = token_of(at // heads)
    query_head = at % heads // per_kv
    lane = lax.broadcasted_iota(jnp.int32, seen_ref.shape, 1)
    key_head, key = lane // tokens, lane % tokens
    key_token = token_of(key)
    seen = (
        (query_head == key_head)
        & (query_token // steps == key_token // steps)
        & (key_token <= query_token)
        & (query_token // steps % lax.axis_size("mem") == mem)
    )
    seen_ref[...] = seen.astype(jnp.float32)


def project_body(places, tile, *refs):
    gain_ref, q_ref, k_ref, v_ref, out_ref = refs[len(places) :]
    chunks = [refs[places.index(i)][...].astype(jnp.float32) for i in range(len(places))]
    rows = jnp.concatenate(chunks, axis=0)
    cols = gain_ref.shape[0]
    factor = from_pieces([rows[:, cols + i : cols + i + 1] for i in range(3)])
    gain = gain_ref[...].astype(jnp.float32).reshape(1, cols)
    rows = (rows[:, :cols] * factor * gain).astype(jnp.bfloat16)
    tokens = rows.shape[0]
    heads = q_ref.shape[1] // LANES
    head = 0
    for weight in (q_ref, k_ref, v_ref):
        width = min(tile, weight.shape[1])
        for col in range(0, weight.shape[1], width):
            product = jnp.dot(
                rows, weight[:, col : col + width], preferred_element_type=jnp.float32
            )
            for lane in range(0, width, LANES):
                columns = product[:, lane : lane + LANES]
                if head < heads:
                    out_ref[pl.ds(head, tokens, stride=heads)] = columns
                else:
                    out_ref[head * tokens : (head + 1) * tokens] = columns
                head += 1


def add_body(own_ref, other_ref, out_ref, *sent_refs):
    total = own_ref[...] + other_ref[...]
    for ref in (out_ref, *sent_refs):
        ref[...] = total.astype(ref.dtype)


def split_dot(weights, values):
    high = weights.astype(jnp.bfloat16)
    low = (weights - high.astype(jnp.float32)).astype(jnp.bfloat16)
    both = jnp.dot(
        jnp.concatenate([high, low], axis=0), values, preferred_element_type=jnp.float32
    )
    return both[: weights.shape[0]] + both[weights.shape[0] :]


def to_pieces(rows):
    pieces = []
    for _ in range(3):
        pieces.append(rows.astype(jnp.bfloat16))
        rows = rows - pieces[-1].astype(jnp.float32)
    return pieces


def from_pieces(pieces):
    high, middle, low = [piece.astype(jnp.float32) for piece in pieces]
    return low + middle + high


def group_lanes(query_count):
    lane = lax.broadcasted_iota(jnp.int32, (query_count, LANES), 1)
    row = lax.broadcasted_iota(jnp.int32, (query_count, LANES), 0)
    return lane - row


def pack_columns(column, query_count):
    per_row = LANES // query_count
    offset = group_lanes(query_count)
    groups = column.shape[0] // query_count
    rows = []
    for first in range(0, groups, per_row):
        row = jnp.zeros((query_count, LANES), jnp.float32)
        for i in range(min(per_row, groups - first)):
            at = (first + i) * query_count
            row = jnp.where(offset == i * query_count, column[at : at + query_count], row)
        rows.append(jnp.sum(row, axis=0, keepdims=True))
    return rows


def unpack_column(row, place, query_count):
    spread = jnp.broadcast_to(row, (query_count, LANES))
    picked = jnp.where(group_lanes(query_count) == place * query_count, spread, 0.0)
    return jnp.sum(picked, axis=1, keepdims=True)


def attend_body(
    scale,
    heads,
    query_count,
    chosen_ref,
    seen_ref,
    own_ref,
    other_ref,
    turned_ref,
    value_ref,
    out_ref,
    query_ref,
    score_ref,
    total_ref,
    accum_ref,
    *peak_refs,
):
    row_count, row_height, head_dim = query_ref.shape
    kv_heads = value_ref.shape[1]
    capacity = score_ref.shape[0]
    height = row_count * row_height
    contract_last = (((1,), (1,)), ((), ()))

    projected = (own_ref[...] + other_ref[...]).astype(jnp.bfloat16)
    queries = projected[:height]
    query_ref[...] = queries.reshape(query_ref.shape)
    fresh = projected[height:]
    count = fresh.shape[0] // 2
    spare = jnp.zeros((LANES - count, head_dim), jnp.bfloat16)
    seen = seen_ref[...] > 0
    fresh_score = lax.dot_general(
        queries,
        jnp.concatenate([fresh[:count], spare], axis=0),
        contract_last,
        preferred_element_type=jnp.float32,
    )
    fresh_score = jnp.where(seen, fresh_score * scale, NEG_FILL)
    peak_ref = peak_refs[0]
    peak_ref[:row_count] = fresh_score.reshape(row_count, row_height, LANES)
    peak_ref[row_count] = jnp.full((row_height, LANES), NEG_FILL, jnp.float32)
    for ref in peak_refs[1:]:
        ref[...] = jnp.full(ref.shape, NEG_FILL, jnp.float32)
    stride = chosen_ref.shape[0] // 3

    lane = lax.broadcasted_iota(jnp.int32, (row_height, LANES), 1)
    head_of = lax.broadcasted_iota(jnp.int32, (row_height, LANES), 0) % heads // (heads // kv_heads)
    for c in range(capacity):
        slot, row, valid = (chosen_ref[i * stride + c] for i in range(3))
        every = jnp.dot(
            query_ref[jnp.minimum(row, row_count - 1)],
            turned_ref[c],
            preferred_element_type=jnp.float32,
        )
        score = every[:, :LANES]
        for g in range(1, kv_heads):
            score = jnp.where(head_of == g, every[:, g * LANES : (g + 1) * LANES], score)
        score = jnp.where(lane < valid, score * scale, NEG_FILL)
        score_ref[c] = score
        ref = peak_refs[c % len(peak_refs)]
        ref[row] = jnp.maximum(ref[row], score)

    peak = functools.reduce(jnp.maximum, [ref[:row_count] for ref in peak_refs])
    peak = jnp.max(peak.reshape(height, LANES), axis=1, keepdims=True)
    peak = jnp.broadcast_to(peak, (height, LANES))
    peak_ref[:row_count] = peak.reshape(row_count, row_height, LANES)
    weights = jnp.where(seen, jnp.exp(fresh_score - peak), 0.0)
    total_ref[:row_count] = weights.reshape(row_count, row_height, LANES)
    total_ref[row_count] = jnp.zeros((row_height, LANES), jnp.float32)
    accum = split_dot(weights, jnp.concatenate([fresh[count:], spare], axis=0))
    accum_ref[:row_count] = accum.reshape(row_count, row_height, head_dim)
    accum_ref[row_count] = jnp.zeros((row_height, head_dim), jnp.float32)

    for c in range(capacity):
        slot, row = chosen_ref[c], chosen_ref[stride + c]
        weights = jnp.exp(score_ref[c] - peak_ref[row])
        total_ref[row] += weights
        spread = [jnp.where(head_of == g, weights, 0.0) for g in range(kv_heads)]
        accum_ref[row] += split_dot(
            jnp.concatenate(spread, axis=1), value_ref[slot].reshape(kv_heads * LANES, head_dim)
        )

    total = jnp.sum(total_ref[:row_count].reshape(height, LANES), axis=1, keepdims=True)
    total = jnp.broadcast_to(total, (height, LANES))
    out_ref[:height] = accum_ref[:row_count].reshape(height, head_dim)
    packed = pack_columns(peak, query_count) + pack_columns(total, query_count)
    spare = out_ref.shape[0] - height - len(packed)
    packed.append(jnp.zeros((spare, LANES), jnp.float32))
    out_ref[height:] = jnp.concatenate(packed, axis=0)


def state_rows(groups, query_count):
    return -(-groups // (LANES // query_count))


def merge_states(query_count, groups, last, own_ref, other_ref):
    per_row = LANES // query_count
    height = groups * query_count
    rows = state_rows(groups, query_count)
    own_peak, own_total = (own_ref[height + i * rows : height + (i + 1) * rows] for i in range(2))
    if other_ref.dtype == jnp.bfloat16:
        tail = other_ref[height:]
        pieces = [tail[i * rows : (i + 1) * rows] for i in range(6)]
        other_peak, other_total = from_pieces(pieces[:3]), from_pieces(pieces[3:])
    else:
        other_peak, other_total = (
            other_ref[height + i * rows : height + (i + 1) * rows] for i in range(2)
        )
    peak = jnp.maximum(own_peak, other_peak)
    own_factor, other_factor = jnp.exp(own_peak - peak), jnp.exp(other_peak - peak)
    total = own_total * own_factor + other_total * other_factor
    if last:
        own_factor, other_factor = own_factor / total, other_factor / total
    values = []
    for group in range(groups):
        row, place = divmod(group, per_row)
        at = slice(group * query_count, (group + 1) * query_count)
        values.append(
            own_ref[at] * unpack_column(own_factor[row : row + 1], place, query_count)
            + other_ref[at].astype(jnp.float32)
            * unpack_column(other_factor[row : row + 1], place, query_count)
        )
    return peak, total, values


def combine_body(query_count, groups, own_ref, other_ref, *out_refs):
    height = groups * query_count
    peak, total, values = merge_states(query_count, groups, False, own_ref, other_ref)
    for ref in out_refs:
        tail = [peak, total]
        if ref.dtype == jnp.bfloat16:
            tail = to_pieces(peak) + to_pieces(total)
        spare = ref.shape[0] - height - len(tail) * peak.shape[0]
        tail.append(jnp.zeros((spare, LANES), ref.dtype))
        ref[height:] = jnp.concatenate(tail, axis=0)
        for group, value in enumerate(values):
            ref[group * query_count : (group + 1) * query_count] = value.astype(ref.dtype)


def output_body(query_count, tile, own_ref, other_ref, weight_ref, *refs):
    out_refs, wide_ref = refs[:-1], refs[-1]
    heads = weight_ref.shape[0] // LANES
    tokens = wide_ref.shape[0] // heads
    groups = wide_ref.shape[0] // query_count
    _, _, values = merge_states(query_count, groups, True, own_ref, other_ref)
    for group, value in enumerate(values):
        wide_ref[group * query_count : (group + 1) * query_count] = value
    rows = [wide_ref[pl.ds(head, tokens, stride=heads)] for head in range(heads)]
    rows = jnp.concatenate(rows, axis=1).astype(jnp.bfloat16)
    chunk = out_refs[0].shape[0]
    for col in range(0, weight_ref.shape[1], tile):
        product = jnp.dot(
            rows, weight_ref[:, col : col + tile], preferred_element_type=jnp.float32
        )
        for i, out_ref in enumerate(out_refs):
            out_ref[:, col : col + tile] = product[i * chunk : (i + 1) * chunk].astype(out_ref.dtype)


def shards(
    hidden,
    norm_gain,
    q_weight,
    k_weight,
    v_weight,
    o_weight,
    k_cache,
    v_cache,
    page_table,
    attend_list,
    lengths,
):
    mem_count, head_count = lax.axis_size("mem"), lax.axis_size("heads")
    chunk = hidden.shape[0]
    feature_cols = norm_gain.shape[0]
    query_cols, value_cols = q_weight.shape[1], k_weight.shape[1]
    pool, kv_heads, block, head_dim = k_cache.shape
    row_count, selected = attend_list.shape
    token_count = chunk * head_count
    steps = token_count // row_count
    per_kv = query_cols // head_dim // kv_heads
    query_count = steps * per_kv
    capacity = 2 * row_count * selected // mem_count
    groups = row_count * kv_heads
    height = groups * query_count
    f32, bf16 = jnp.float32, jnp.bfloat16

    own, mate = kernel_call(
        norm_body,
        "norm",
        [jax.ShapeDtypeStruct((chunk, feature_cols + LANES), bf16)] * 2,
        [pl.BlockSpec(memory_space=pltpu.HBM)],
        2,
        1e10,
        [pltpu.VMEM(hidden.shape, bf16), pltpu.SemaphoreType.DMA],
    )(pltpu.with_memory_space_constraint(hidden, pltpu.HBM))
    distances = [*range(2, head_count), 1]
    gathered = distances[::-1]
    pieces = [own] + [swap_across(mate, d) for d in gathered]

    chosen, seen, turned = kernel_call(
        functools.partial(select_body, chunk, steps, per_kv),
        "select",
        [
            pltpu.SMEM((3 * (capacity + 1),), jnp.int32),
            jax.ShapeDtypeStruct((height, LANES), f32),
            jax.ShapeDtypeStruct((capacity, head_dim, kv_heads * block), bf16),
        ],
        [IN_SMEM] * 3 + [IN_VMEM],
        4,
        1e10,
        out_space=[IN_SMEM, IN_VMEM, IN_VMEM],
    )(page_table, attend_list, lengths, k_cache)

    width = query_cols + 2 * value_cols
    summed = kernel_call(
        functools.partial(project_body, (0, *gathered), 512),
        "project",
        jax.ShapeDtypeStruct((width // LANES * token_count, LANES), f32),
        [IN_VMEM] * (head_count + 4),
        4,
        2 * token_count * feature_cols * width,
    )(*pieces, norm_gain, q_weight, k_weight, v_weight)
    sent = summed
    distance = 1
    while 2 * distance < mem_count:
        added = kernel_call(
            add_body,
            "add",
            [jax.ShapeDtypeStruct(summed.shape, f32)],
            [IN_VMEM] * 2,
            2,
            1e10,
        )(summed, swap(sent, "mem", crossing(distance)))
        summed, sent = added[0], added[-1]
        distance *= 2

    state = (kv_heads * query_count, LANES)
    partial = kernel_call(
        functools.partial(attend_body, head_dim ** (-0.5), kv_heads * per_kv, query_count),
        "attend",
        jax.ShapeDtypeStruct((height + 8, LANES), f32),
        [IN_SMEM] + [IN_VMEM] * 5,
        4,
        1e10,
        [pltpu.VMEM((row_count, *state), bf16), pltpu.VMEM((capacity, *state), f32)]
        + [pltpu.VMEM((row_count + 1, *state), f32)] * 6,
    )(
        pltpu.with_memory_space_constraint(chosen, pltpu.SMEM),
        seen,
        summed,
        swap(sent.astype(jnp.float16), "mem", crossing(distance)).astype(f32),
        turned,
        v_cache,
    )

    sent = partial
    distance = 1
    while 2 * distance < mem_count:
        outs = [jax.ShapeDtypeStruct(partial.shape, f32)]
        if 4 * distance == mem_count:
            pad = -(-6 * state_rows(groups, query_count) // 16) * 16
            outs.append(jax.ShapeDtypeStruct((height + pad, LANES), bf16))
        merged = kernel_call(
            functools.partial(combine_body, query_count, groups),
            "combine",
            outs,
            [IN_VMEM] * 2,
            2,
            1e10,
        )(partial, swap(sent, "mem", crossing(distance)))
        partial, sent = merged[0], merged[-1]
        distance *= 2

    out_cols = o_weight.shape[1]
    projected = kernel_call(
        functools.partial(output_body, query_count, min(512, out_cols)),
        "output",
        [jax.ShapeDtypeStruct((chunk, out_cols), bf16 if i else f32) for i in range(head_count)],
        [IN_VMEM] * 3,
        4,
        2 * token_count * query_cols * out_cols,
        [pltpu.VMEM((query_cols // LANES * token_count, LANES), f32)],
    )(partial, swap(sent, "mem", crossing(distance)), o_weight)
    total = projected[0]
    for d in distances:
        total = total + swap(projected[d], "heads", d).astype(f32)
    return total.astype(bf16)


def solution(mesh):
    in_specs = (
        P(("groups", "heads"), None),
        P("mem"),
        P("mem", "heads"),
        P("mem", "heads"),
        P("mem", "heads"),
        P("heads", "mem"),
        P(("groups", "mem"), "heads", None, None),
        P(("groups", "mem"), "heads", None, None),
        P("groups", None),
        P("groups", None),
        P("groups"),
    )
    out_specs = P(("groups", "heads"), "mem")
    return jax.shard_map(shards, mesh=mesh, in_specs=in_specs, out_specs=out_specs, check_vma=False)
```

```python
import functools

import jax
import jax.numpy as jnp
from jax import lax
from jax.experimental import pallas as pl
from jax.experimental.pallas import tpu as pltpu
from jax.sharding import PartitionSpec as P

NEG_FILL = -1e30
EPSILON = 1e-05
LANES = 128
MIB = 1 << 20
IN_VMEM = pl.BlockSpec(memory_space=pltpu.VMEM)
IN_SMEM = pl.BlockSpec(memory_space=pltpu.SMEM)


def swap(array, axis, distance):
    count = lax.axis_size(axis)
    return lax.ppermute(array, axis, [(i, i ^ distance) for i in range(count)])


def crossing(distance):
    return distance if distance == 1 else distance + 1


def swap_across(array, distance):
    heads = lax.axis_size("heads")
    count = lax.axis_size("mem") * heads
    pairs = [(i, i ^ heads ^ distance) for i in range(count)]
    return lax.ppermute(array, ("mem", "heads"), pairs)


def kernel_call(body, name, outs, ins, vmem_mib, flops, scratch=(), out_space=IN_VMEM):
    return pl.pallas_call(
        body,
        out_shape=outs,
        in_specs=ins,
        out_specs=out_space if isinstance(out_space, list) else jax.tree.map(lambda _: out_space, outs),
        scratch_shapes=list(scratch),
        name=name,
        compiler_params=pltpu.CompilerParams(vmem_limit_bytes=vmem_mib * MIB),
        cost_estimate=pl.CostEstimate(flops=int(flops), bytes_accessed=1024, transcendentals=0),
    )


def norm_body(hidden_hbm, own_ref, mate_ref, hidden_ref, sem):
    copy = pltpu.make_async_copy(hidden_hbm, hidden_ref, sem)
    copy.start()
    copy.wait()
    cols = own_ref.shape[1] - 3 * LANES
    mem = lax.axis_index("mem")
    hidden = hidden_ref[...].astype(jnp.float32)
    factor = lax.rsqrt(jnp.mean(hidden * hidden, axis=-1, keepdims=True) + EPSILON)
    wide = jnp.broadcast_to(factor, (hidden.shape[0], LANES))
    tail = jnp.concatenate(to_pieces(wide), axis=1)
    for ref, index in ((own_ref, mem), (mate_ref, lax.bitwise_xor(mem, 1))):
        start = pl.multiple_of(index * cols, cols)
        ref[:, :cols] = hidden_ref[:, pl.ds(start, cols)]
        ref[:, cols:] = tail


def select_body(
    chunk, steps, per_kv, table_ref, list_ref, lengths_ref, key_ref, chosen_ref, seen_ref, turned_ref
):
    pool, kv_heads, block, head_dim = key_ref.shape
    mem = lax.axis_index("mem")
    head_shard = lax.axis_index("heads")
    row_count, selected = list_ref.shape
    stride = chosen_ref.shape[0] // 3
    count = jnp.int32(0)
    for row in range(row_count):
        first = row * steps
        place = (lax.bitwise_xor(first // chunk, head_shard) * chunk + first % chunk) // steps
        length = lengths_ref[row]
        for i in range(selected):
            index = list_ref[row, i]
            slot = table_ref[row, index] - mem * pool
            chosen_ref[count] = slot
            chosen_ref[stride + count] = place
            chosen_ref[2 * stride + count] = length - index * block
            count += ((slot >= 0) & (slot < pool)).astype(jnp.int32)
    for c in range(stride - 1):
        live = c < count
        for at, blank in ((c, 0), (stride + c, row_count), (2 * stride + c, 0)):
            chosen_ref[at] = jnp.where(live, chosen_ref[at], blank)
        keys = key_ref[chosen_ref[c]]
        for g in range(kv_heads):
            turned_ref[c, :, g * block : (g + 1) * block] = keys[g].T

    def token_of(place):
        return lax.bitwise_xor(place // chunk, head_shard) * chunk + place % chunk

    tokens = row_count * steps
    heads = kv_heads * per_kv
    at = lax.broadcasted_iota(jnp.int32, seen_ref.shape, 0)
    query_token = token_of(at // heads)
    query_head = at % heads // per_kv
    lane = lax.broadcasted_iota(jnp.int32, seen_ref.shape, 1)
    key_head, key = lane // tokens, lane % tokens
    key_token = token_of(key)
    seen = (
        (query_head == key_head)
        & (query_token // steps == key_token // steps)
        & (key_token <= query_token)
        & (query_token // steps % lax.axis_size("mem") == mem)
    )
    seen_ref[...] = seen.astype(jnp.float32)


def pass_body(in_ref, out_ref):
    out_ref[...] = in_ref[...]


def project_body(places, tile, *refs):
    gain_ref, q_ref, k_ref, v_ref, out_ref = refs[len(places) :]
    chunks = [refs[places.index(i)][...].astype(jnp.float32) for i in range(len(places))]
    rows = jnp.concatenate(chunks, axis=0)
    cols = gain_ref.shape[0]
    gain = gain_ref[...].astype(jnp.float32).reshape(1, cols)
    tail = [rows[:, cols + i * LANES : cols + (i + 1) * LANES] for i in range(3)]
    factor = jnp.concatenate([from_pieces(tail)] * (cols // LANES), axis=1)
    rows = (rows[:, :cols] * factor * gain).astype(jnp.bfloat16)
    tokens = rows.shape[0]
    heads = q_ref.shape[1] // LANES
    head = 0
    for weight in (q_ref, k_ref, v_ref):
        width = min(tile, weight.shape[1])
        for col in range(0, weight.shape[1], width):
            product = jnp.dot(
                rows, weight[:, col : col + width], preferred_element_type=jnp.float32
            )
            for lane in range(0, width, LANES):
                columns = product[:, lane : lane + LANES]
                if head < heads:
                    out_ref[pl.ds(head, tokens, stride=heads)] = columns
                else:
                    out_ref[head * tokens : (head + 1) * tokens] = columns
                head += 1


def add_body(own_ref, other_ref, out_ref, *sent_refs):
    total = own_ref[...] + other_ref[...]
    for ref in (out_ref, *sent_refs):
        ref[...] = total.astype(ref.dtype)


def split_dot(weights, values):
    high = weights.astype(jnp.bfloat16)
    low = (weights - high.astype(jnp.float32)).astype(jnp.bfloat16)
    both = jnp.dot(
        jnp.concatenate([high, low], axis=0), values, preferred_element_type=jnp.float32
    )
    return both[: weights.shape[0]] + both[weights.shape[0] :]


def to_pieces(rows):
    pieces = []
    for _ in range(3):
        pieces.append(rows.astype(jnp.bfloat16))
        rows = rows - pieces[-1].astype(jnp.float32)
    return pieces


def from_pieces(pieces):
    high, middle, low = [piece.astype(jnp.float32) for piece in pieces]
    return low + middle + high


def group_lanes(query_count):
    lane = lax.broadcasted_iota(jnp.int32, (query_count, LANES), 1)
    row = lax.broadcasted_iota(jnp.int32, (query_count, LANES), 0)
    return lane - row


def pack_columns(column, query_count):
    per_row = LANES // query_count
    offset = group_lanes(query_count)
    groups = column.shape[0] // query_count
    rows = []
    for first in range(0, groups, per_row):
        row = jnp.zeros((query_count, LANES), jnp.float32)
        for i in range(min(per_row, groups - first)):
            at = (first + i) * query_count
            row = jnp.where(offset == i * query_count, column[at : at + query_count], row)
        rows.append(jnp.sum(row, axis=0, keepdims=True))
    return rows


def unpack_column(row, place, query_count):
    spread = jnp.broadcast_to(row, (query_count, LANES))
    picked = jnp.where(group_lanes(query_count) == place * query_count, spread, 0.0)
    return jnp.sum(picked, axis=1, keepdims=True)


def attend_body(
    scale,
    heads,
    query_count,
    chosen_ref,
    seen_ref,
    own_ref,
    other_ref,
    turned_ref,
    value_ref,
    out_ref,
    query_ref,
    score_ref,
    total_ref,
    accum_ref,
    *peak_refs,
):
    row_count, row_height, head_dim = query_ref.shape
    kv_heads = value_ref.shape[1]
    capacity = score_ref.shape[0]
    height = row_count * row_height
    contract_last = (((1,), (1,)), ((), ()))

    projected = (own_ref[...] + other_ref[...]).astype(jnp.bfloat16)
    queries = projected[:height]
    query_ref[...] = queries.reshape(query_ref.shape)
    fresh = projected[height:]
    count = fresh.shape[0] // 2
    spare = jnp.zeros((LANES - count, head_dim), jnp.bfloat16)
    seen = seen_ref[...] > 0
    fresh_score = lax.dot_general(
        queries,
        jnp.concatenate([fresh[:count], spare], axis=0),
        contract_last,
        preferred_element_type=jnp.float32,
    )
    fresh_score = jnp.where(seen, fresh_score * scale, NEG_FILL)
    peak_ref = peak_refs[0]
    peak_ref[:row_count] = fresh_score.reshape(row_count, row_height, LANES)
    peak_ref[row_count] = jnp.full((row_height, LANES), NEG_FILL, jnp.float32)
    for ref in peak_refs[1:]:
        ref[...] = jnp.full(ref.shape, NEG_FILL, jnp.float32)
    stride = chosen_ref.shape[0] // 3

    lane = lax.broadcasted_iota(jnp.int32, (row_height, LANES), 1)
    head_of = lax.broadcasted_iota(jnp.int32, (row_height, LANES), 0) % heads // (heads // kv_heads)
    for c in range(capacity):
        slot, row, valid = (chosen_ref[i * stride + c] for i in range(3))
        every = jnp.dot(
            query_ref[jnp.minimum(row, row_count - 1)],
            turned_ref[c],
            preferred_element_type=jnp.float32,
        )
        score = every[:, :LANES]
        for g in range(1, kv_heads):
            score = jnp.where(head_of == g, every[:, g * LANES : (g + 1) * LANES], score)
        score = jnp.where(lane < valid, score * scale, NEG_FILL)
        score_ref[c] = score
        ref = peak_refs[c % len(peak_refs)]
        ref[row] = jnp.maximum(ref[row], score)

    peak = functools.reduce(jnp.maximum, [ref[:row_count] for ref in peak_refs])
    peak = jnp.max(peak.reshape(height, LANES), axis=1, keepdims=True)
    peak = jnp.broadcast_to(peak, (height, LANES))
    peak_ref[:row_count] = peak.reshape(row_count, row_height, LANES)
    weights = jnp.where(seen, jnp.exp(fresh_score - peak), 0.0)
    total_ref[:row_count] = weights.reshape(row_count, row_height, LANES)
    total_ref[row_count] = jnp.zeros((row_height, LANES), jnp.float32)
    accum = split_dot(weights, jnp.concatenate([fresh[count:], spare], axis=0))
    accum_ref[:row_count] = accum.reshape(row_count, row_height, head_dim)
    accum_ref[row_count] = jnp.zeros((row_height, head_dim), jnp.float32)

    for c in range(capacity):
        slot, row = chosen_ref[c], chosen_ref[stride + c]
        weights = jnp.exp(score_ref[c] - peak_ref[row])
        total_ref[row] += weights
        spread = [jnp.where(head_of == g, weights, 0.0) for g in range(kv_heads)]
        accum_ref[row] += split_dot(
            jnp.concatenate(spread, axis=1), value_ref[slot].reshape(kv_heads * LANES, head_dim)
        )

    total = jnp.sum(total_ref[:row_count].reshape(height, LANES), axis=1, keepdims=True)
    total = jnp.broadcast_to(total, (height, LANES))
    out_ref[:height] = accum_ref[:row_count].reshape(height, head_dim)
    packed = pack_columns(peak, query_count) + pack_columns(total, query_count)
    spare = out_ref.shape[0] - height - len(packed)
    packed.append(jnp.zeros((spare, LANES), jnp.float32))
    out_ref[height:] = jnp.concatenate(packed, axis=0)


def state_rows(groups, query_count):
    return -(-groups // (LANES // query_count))


def merge_states(query_count, groups, last, own_ref, other_ref):
    per_row = LANES // query_count
    height = groups * query_count
    rows = state_rows(groups, query_count)
    own_peak, own_total = (own_ref[height + i * rows : height + (i + 1) * rows] for i in range(2))
    if other_ref.dtype == jnp.bfloat16:
        tail = other_ref[height:]
        pieces = [tail[i * rows : (i + 1) * rows] for i in range(6)]
        other_peak, other_total = from_pieces(pieces[:3]), from_pieces(pieces[3:])
    else:
        other_peak, other_total = (
            other_ref[height + i * rows : height + (i + 1) * rows] for i in range(2)
        )
    peak = jnp.maximum(own_peak, other_peak)
    own_factor, other_factor = jnp.exp(own_peak - peak), jnp.exp(other_peak - peak)
    total = own_total * own_factor + other_total * other_factor
    if last:
        own_factor, other_factor = own_factor / total, other_factor / total
    values = []
    for group in range(groups):
        row, place = divmod(group, per_row)
        at = slice(group * query_count, (group + 1) * query_count)
        values.append(
            own_ref[at] * unpack_column(own_factor[row : row + 1], place, query_count)
            + other_ref[at].astype(jnp.float32)
            * unpack_column(other_factor[row : row + 1], place, query_count)
        )
    return peak, total, values


def combine_body(query_count, groups, own_ref, other_ref, *out_refs):
    height = groups * query_count
    peak, total, values = merge_states(query_count, groups, False, own_ref, other_ref)
    for ref in out_refs:
        tail = [peak, total]
        if ref.dtype == jnp.bfloat16:
            tail = to_pieces(peak) + to_pieces(total)
        spare = ref.shape[0] - height - len(tail) * peak.shape[0]
        tail.append(jnp.zeros((spare, LANES), ref.dtype))
        ref[height:] = jnp.concatenate(tail, axis=0)
        for group, value in enumerate(values):
            ref[group * query_count : (group + 1) * query_count] = value.astype(ref.dtype)


def output_body(query_count, tile, own_ref, other_ref, weight_ref, *refs):
    out_refs, wide_ref = refs[:-1], refs[-1]
    heads = weight_ref.shape[0] // LANES
    tokens = wide_ref.shape[0] // heads
    groups = wide_ref.shape[0] // query_count
    _, _, values = merge_states(query_count, groups, True, own_ref, other_ref)
    for group, value in enumerate(values):
        wide_ref[group * query_count : (group + 1) * query_count] = value
    rows = [wide_ref[pl.ds(head, tokens, stride=heads)] for head in range(heads)]
    rows = jnp.concatenate(rows, axis=1).astype(jnp.bfloat16)
    chunk = out_refs[0].shape[0]
    for col in range(0, weight_ref.shape[1], tile):
        product = jnp.dot(
            rows, weight_ref[:, col : col + tile], preferred_element_type=jnp.float32
        )
        for i, out_ref in enumerate(out_refs):
            out_ref[:, col : col + tile] = product[i * chunk : (i + 1) * chunk].astype(out_ref.dtype)


def shards(
    hidden,
    norm_gain,
    q_weight,
    k_weight,
    v_weight,
    o_weight,
    k_cache,
    v_cache,
    page_table,
    attend_list,
    lengths,
):
    mem_count, head_count = lax.axis_size("mem"), lax.axis_size("heads")
    chunk = hidden.shape[0]
    feature_cols = norm_gain.shape[0]
    query_cols, value_cols = q_weight.shape[1], k_weight.shape[1]
    pool, kv_heads, block, head_dim = k_cache.shape
    row_count, selected = attend_list.shape
    token_count = chunk * head_count
    steps = token_count // row_count
    per_kv = query_cols // head_dim // kv_heads
    query_count = steps * per_kv
    capacity = 2 * row_count * selected // mem_count
    groups = row_count * kv_heads
    height = groups * query_count
    f32, bf16 = jnp.float32, jnp.bfloat16

    own, mate = kernel_call(
        norm_body,
        "norm",
        [jax.ShapeDtypeStruct((chunk, feature_cols + 3 * LANES), bf16)] * 2,
        [pl.BlockSpec(memory_space=pltpu.HBM)],
        2,
        1,
        [pltpu.VMEM(hidden.shape, bf16), pltpu.SemaphoreType.DMA],
    )(pltpu.with_memory_space_constraint(hidden, pltpu.HBM))
    mate = kernel_call(
        pass_body,
        "pass",
        jax.ShapeDtypeStruct(mate.shape, bf16),
        [IN_VMEM],
        1,
        1e10,
    )(mate)
    distances = [*range(2, head_count), 1]
    gathered = distances[::-1]
    pieces = [own] + [swap_across(mate, d) for d in gathered]

    chosen, seen, turned = kernel_call(
        functools.partial(select_body, chunk, steps, per_kv),
        "select",
        [
            pltpu.SMEM((3 * (capacity + 1),), jnp.int32),
            jax.ShapeDtypeStruct((height, LANES), f32),
            jax.ShapeDtypeStruct((capacity, head_dim, kv_heads * block), bf16),
        ],
        [IN_SMEM] * 3 + [IN_VMEM],
        4,
        1e10,
        out_space=[IN_SMEM, IN_VMEM, IN_VMEM],
    )(page_table, attend_list, lengths, k_cache)

    width = query_cols + 2 * value_cols
    summed = kernel_call(
        functools.partial(project_body, (0, *gathered), 512),
        "project",
        jax.ShapeDtypeStruct((width // LANES * token_count, LANES), f32),
        [IN_VMEM] * (head_count + 4),
        4,
        2 * token_count * feature_cols * width,
    )(*pieces, norm_gain, q_weight, k_weight, v_weight)
    sent = summed
    distance = 1
    while 2 * distance < mem_count:
        added = kernel_call(
            add_body,
            "add",
            [jax.ShapeDtypeStruct(summed.shape, f32)],
            [IN_VMEM] * 2,
            2,
            1e10,
        )(summed, swap(sent, "mem", crossing(distance)))
        summed, sent = added[0], added[-1]
        distance *= 2

    state = (kv_heads * query_count, LANES)
    partial = kernel_call(
        functools.partial(attend_body, head_dim ** (-0.5), kv_heads * per_kv, query_count),
        "attend",
        jax.ShapeDtypeStruct((height + 8, LANES), f32),
        [IN_SMEM] + [IN_VMEM] * 5,
        4,
        1e10,
        [pltpu.VMEM((row_count, *state), bf16), pltpu.VMEM((capacity, *state), f32)]
        + [pltpu.VMEM((row_count + 1, *state), f32)] * 6,
    )(
        pltpu.with_memory_space_constraint(chosen, pltpu.SMEM),
        seen,
        summed,
        swap(sent.astype(jnp.float16), "mem", crossing(distance)).astype(f32),
        turned,
        v_cache,
    )

    sent = partial
    distance = 1
    while 2 * distance < mem_count:
        outs = [jax.ShapeDtypeStruct(partial.shape, f32)]
        if 4 * distance == mem_count:
            pad = -(-6 * state_rows(groups, query_count) // 16) * 16
            outs.append(jax.ShapeDtypeStruct((height + pad, LANES), bf16))
        merged = kernel_call(
            functools.partial(combine_body, query_count, groups),
            "combine",
            outs,
            [IN_VMEM] * 2,
            2,
            1e10,
        )(partial, swap(sent, "mem", crossing(distance)))
        partial, sent = merged[0], merged[-1]
        distance *= 2

    out_cols = o_weight.shape[1]
    projected = kernel_call(
        functools.partial(output_body, query_count, min(512, out_cols)),
        "output",
        [jax.ShapeDtypeStruct((chunk, out_cols), bf16 if i else f32) for i in range(head_count)],
        [IN_VMEM] * 3,
        4,
        2 * token_count * query_cols * out_cols,
        [pltpu.VMEM((query_cols // LANES * token_count, LANES), f32)],
    )(partial, swap(sent, "mem", crossing(distance)), o_weight)
    total = projected[0]
    for d in distances:
        total = total + swap(projected[d], "heads", d).astype(f32)
    return total.astype(bf16)


def solution(mesh):
    in_specs = (
        P(("groups", "heads"), None),
        P("mem"),
        P("mem", "heads"),
        P("mem", "heads"),
        P("mem", "heads"),
        P("heads", "mem"),
        P(("groups", "mem"), "heads", None, None),
        P(("groups", "mem"), "heads", None, None),
        P("groups", None),
        P("groups", None),
        P("groups"),
    )
    out_specs = P(("groups", "heads"), "mem")
    return jax.shard_map(shards, mesh=mesh, in_specs=in_specs, out_specs=out_specs, check_vma=False)
```

```python
import functools
import math

import jax
import jax.numpy as jnp
from jax import lax
from jax.experimental import pallas as pl
from jax.experimental.pallas import tpu as pltpu
from jax.sharding import PartitionSpec as P

NEG_FILL = -1e30
EPSILON = 1e-05
LANES = 128
MIB = 1 << 20
IN_VMEM = pl.BlockSpec(memory_space=pltpu.VMEM)
IN_SMEM = pl.BlockSpec(memory_space=pltpu.SMEM)


def swap(array, axis, distance):
    count = lax.axis_size(axis)
    return lax.ppermute(array, axis, [(i, i ^ distance) for i in range(count)])


def crossing(distance):
    return distance if distance == 1 else distance + 1


def swap_across(array, distance):
    heads = lax.axis_size("heads")
    count = lax.axis_size("mem") * heads
    pairs = [(i, i ^ heads ^ distance) for i in range(count)]
    return lax.ppermute(array, ("mem", "heads"), pairs)


def kernel_call(body, name, outs, ins, vmem_mib, flops, scratch=(), out_space=IN_VMEM):
    return pl.pallas_call(
        body,
        out_shape=outs,
        in_specs=ins,
        out_specs=out_space if isinstance(out_space, list) else jax.tree.map(lambda _: out_space, outs),
        scratch_shapes=list(scratch),
        name=name,
        compiler_params=pltpu.CompilerParams(vmem_limit_bytes=vmem_mib * MIB),
        cost_estimate=pl.CostEstimate(flops=int(flops), bytes_accessed=1024, transcendentals=0),
    )


def norm_body(hidden_hbm, own_ref, mate_ref, hidden_ref, sem):
    copy = pltpu.make_async_copy(hidden_hbm, hidden_ref, sem)
    copy.start()
    copy.wait()
    cols = own_ref.shape[1] - 3 * LANES
    mem = lax.axis_index("mem")
    hidden = hidden_ref[...].astype(jnp.float32)
    factor = lax.rsqrt(jnp.mean(hidden * hidden, axis=-1, keepdims=True) + EPSILON)
    wide = jnp.broadcast_to(factor, (hidden.shape[0], LANES))
    tail = jnp.concatenate(to_pieces(wide), axis=1)
    for ref, index in ((own_ref, mem), (mate_ref, lax.bitwise_xor(mem, 1))):
        start = pl.multiple_of(index * cols, cols)
        ref[:, :cols] = hidden_ref[:, pl.ds(start, cols)]
        ref[:, cols:] = tail


def select_body(
    chunk, steps, per_kv, table_ref, list_ref, lengths_ref, key_ref, chosen_ref, seen_ref, turned_ref
):
    pool, kv_heads, block, head_dim = key_ref.shape
    mem = lax.axis_index("mem")
    head_shard = lax.axis_index("heads")
    row_count, selected = list_ref.shape
    stride = chosen_ref.shape[0] // 3
    count = jnp.int32(0)
    for row in range(row_count):
        first = row * steps
        place = (lax.bitwise_xor(first // chunk, head_shard) * chunk + first % chunk) // steps
        length = lengths_ref[row]
        for i in range(selected):
            index = list_ref[row, i]
            slot = table_ref[row, index] - mem * pool
            chosen_ref[count] = slot
            chosen_ref[stride + count] = place
            chosen_ref[2 * stride + count] = length - index * block
            count += ((slot >= 0) & (slot < pool)).astype(jnp.int32)
    for c in range(stride - 1):
        live = c < count
        for at, blank in ((c, 0), (stride + c, row_count), (2 * stride + c, 0)):
            chosen_ref[at] = jnp.where(live, chosen_ref[at], blank)
        keys = key_ref[chosen_ref[c]]
        for g in range(kv_heads):
            turned_ref[c, :, g * block : (g + 1) * block] = keys[g].T

    def token_of(place):
        return lax.bitwise_xor(place // chunk, head_shard) * chunk + place % chunk

    tokens = row_count * steps
    heads = kv_heads * per_kv
    at = lax.broadcasted_iota(jnp.int32, seen_ref.shape, 0)
    query_token = token_of(at // heads)
    query_head = at % heads // per_kv
    lane = lax.broadcasted_iota(jnp.int32, seen_ref.shape, 1)
    key_head, key = lane // tokens, lane % tokens
    key_token = token_of(key)
    seen = (
        (query_head == key_head)
        & (query_token // steps == key_token // steps)
        & (key_token <= query_token)
        & (query_token // steps % lax.axis_size("mem") == mem)
    )
    seen_ref[...] = seen.astype(jnp.float32)


def pass_body(in_ref, out_ref):
    out_ref[...] = in_ref[...]


def project_body(places, tile, *refs):
    gain_ref, q_ref, k_ref, v_ref, out_ref = refs[len(places) :]
    chunks = [refs[places.index(i)][...].astype(jnp.float32) for i in range(len(places))]
    rows = jnp.concatenate(chunks, axis=0)
    cols = gain_ref.shape[0]
    gain = gain_ref[...].astype(jnp.float32).reshape(1, cols)
    tail = [rows[:, cols + i * LANES : cols + (i + 1) * LANES] for i in range(3)]
    factor = jnp.concatenate([from_pieces(tail)] * (cols // LANES), axis=1)
    rows = (rows[:, :cols] * factor * gain).astype(jnp.bfloat16)
    tokens = rows.shape[0]
    heads = q_ref.shape[1] // LANES
    head = 0
    for weight in (q_ref, k_ref, v_ref):
        width = min(tile, weight.shape[1])
        for col in range(0, weight.shape[1], width):
            product = jnp.dot(
                rows, weight[:, col : col + width], preferred_element_type=jnp.float32
            )
            for lane in range(0, width, LANES):
                columns = product[:, lane : lane + LANES]
                if head < heads:
                    out_ref[pl.ds(head, tokens, stride=heads)] = columns
                else:
                    out_ref[head * tokens : (head + 1) * tokens] = columns
                head += 1


def add_body(values, own_ref, other_ref, out_ref, *sent_refs):
    total = own_ref[...] + other_ref[...]
    out_ref[...] = total
    for ref in sent_refs:
        height = total.shape[0]
        top = jnp.max(jnp.abs(total[height - values :]), axis=0, keepdims=True)
        top = jnp.maximum(jnp.max(top, axis=1, keepdims=True), 1e-30)
        exponent = jnp.ceil(jnp.log(top) * (1 / math.log(2)))
        ref[: height - values] = total[: height - values]
        ref[height - values : height] = total[height - values :] * jnp.exp2(-exponent)
        ref[height:] = jnp.broadcast_to(exponent, (ref.shape[0] - height, LANES))


def add_sent(own_ref, sent_ref, values):
    height = own_ref.shape[0]
    scale = jnp.exp2(sent_ref[height : height + 1])
    sent_values = sent_ref[height - values : height] * scale
    sent = jnp.concatenate([sent_ref[: height - values], sent_values], axis=0)
    return own_ref[...] + sent


def split_dot(weights, values):
    high = weights.astype(jnp.bfloat16)
    low = (weights - high.astype(jnp.float32)).astype(jnp.bfloat16)
    both = jnp.dot(
        jnp.concatenate([high, low], axis=0), values, preferred_element_type=jnp.float32
    )
    return both[: weights.shape[0]] + both[weights.shape[0] :]


def to_pieces(rows):
    pieces = []
    for _ in range(3):
        pieces.append(rows.astype(jnp.bfloat16))
        rows = rows - pieces[-1].astype(jnp.float32)
    return pieces


def from_pieces(pieces):
    high, middle, low = [piece.astype(jnp.float32) for piece in pieces]
    return low + middle + high


def group_lanes(query_count):
    lane = lax.broadcasted_iota(jnp.int32, (query_count, LANES), 1)
    row = lax.broadcasted_iota(jnp.int32, (query_count, LANES), 0)
    return lane - row


def pack_columns(column, query_count):
    per_row = LANES // query_count
    offset = group_lanes(query_count)
    groups = column.shape[0] // query_count
    rows = []
    for first in range(0, groups, per_row):
        row = jnp.zeros((query_count, LANES), jnp.float32)
        for i in range(min(per_row, groups - first)):
            at = (first + i) * query_count
            row = jnp.where(offset == i * query_count, column[at : at + query_count], row)
        rows.append(jnp.sum(row, axis=0, keepdims=True))
    return rows


def unpack_column(row, place, query_count):
    spread = jnp.broadcast_to(row, (query_count, LANES))
    picked = jnp.where(group_lanes(query_count) == place * query_count, spread, 0.0)
    return jnp.sum(picked, axis=1, keepdims=True)


def attend_body(
    scale,
    heads,
    query_count,
    chosen_ref,
    seen_ref,
    own_ref,
    other_ref,
    turned_ref,
    value_ref,
    out_ref,
    query_ref,
    score_ref,
    total_ref,
    accum_ref,
    *peak_refs,
):
    row_count, row_height, head_dim = query_ref.shape
    kv_heads = value_ref.shape[1]
    capacity = score_ref.shape[0]
    height = row_count * row_height
    contract_last = (((1,), (1,)), ((), ()))

    values = (own_ref.shape[0] - height) // 2
    projected = add_sent(own_ref, other_ref, values).astype(jnp.bfloat16)
    queries = projected[:height]
    query_ref[...] = queries.reshape(query_ref.shape)
    fresh = projected[height:]
    count = fresh.shape[0] // 2
    spare = jnp.zeros((LANES - count, head_dim), jnp.bfloat16)
    seen = seen_ref[...] > 0
    fresh_score = lax.dot_general(
        queries,
        jnp.concatenate([fresh[:count], spare], axis=0),
        contract_last,
        preferred_element_type=jnp.float32,
    )
    fresh_score = jnp.where(seen, fresh_score * scale, NEG_FILL)
    peak_ref = peak_refs[0]
    peak_ref[:row_count] = fresh_score.reshape(row_count, row_height, LANES)
    peak_ref[row_count] = jnp.full((row_height, LANES), NEG_FILL, jnp.float32)
    for ref in peak_refs[1:]:
        ref[...] = jnp.full(ref.shape, NEG_FILL, jnp.float32)
    stride = chosen_ref.shape[0] // 3

    lane = lax.broadcasted_iota(jnp.int32, (row_height, LANES), 1)
    head_of = lax.broadcasted_iota(jnp.int32, (row_height, LANES), 0) % heads // (heads // kv_heads)
    for c in range(capacity):
        slot, row, valid = (chosen_ref[i * stride + c] for i in range(3))
        every = jnp.dot(
            query_ref[jnp.minimum(row, row_count - 1)],
            turned_ref[c],
            preferred_element_type=jnp.float32,
        )
        score = every[:, :LANES]
        for g in range(1, kv_heads):
            score = jnp.where(head_of == g, every[:, g * LANES : (g + 1) * LANES], score)
        score = jnp.where(lane < valid, score * scale, NEG_FILL)
        score_ref[c] = score
        ref = peak_refs[c % len(peak_refs)]
        ref[row] = jnp.maximum(ref[row], score)

    peak = functools.reduce(jnp.maximum, [ref[:row_count] for ref in peak_refs])
    peak = jnp.max(peak.reshape(height, LANES), axis=1, keepdims=True)
    peak = jnp.broadcast_to(peak, (height, LANES))
    peak_ref[:row_count] = peak.reshape(row_count, row_height, LANES)
    weights = jnp.where(seen, jnp.exp(fresh_score - peak), 0.0)
    total_ref[:row_count] = weights.reshape(row_count, row_height, LANES)
    total_ref[row_count] = jnp.zeros((row_height, LANES), jnp.float32)
    accum = split_dot(weights, jnp.concatenate([fresh[count:], spare], axis=0))
    accum_ref[:row_count] = accum.reshape(row_count, row_height, head_dim)
    accum_ref[row_count] = jnp.zeros((row_height, head_dim), jnp.float32)

    for c in range(capacity):
        slot, row = chosen_ref[c], chosen_ref[stride + c]
        weights = jnp.exp(score_ref[c] - peak_ref[row])
        total_ref[row] += weights
        spread = [jnp.where(head_of == g, weights, 0.0) for g in range(kv_heads)]
        accum_ref[row] += split_dot(
            jnp.concatenate(spread, axis=1), value_ref[slot].reshape(kv_heads * LANES, head_dim)
        )

    total = jnp.sum(total_ref[:row_count].reshape(height, LANES), axis=1, keepdims=True)
    total = jnp.broadcast_to(total, (height, LANES))
    out_ref[:height] = accum_ref[:row_count].reshape(height, head_dim)
    packed = pack_columns(peak, query_count) + pack_columns(total, query_count)
    spare = out_ref.shape[0] - height - len(packed)
    packed.append(jnp.zeros((spare, LANES), jnp.float32))
    out_ref[height:] = jnp.concatenate(packed, axis=0)


def state_rows(groups, query_count):
    return -(-groups // (LANES // query_count))


def merge_states(query_count, groups, last, own_ref, other_ref):
    per_row = LANES // query_count
    height = groups * query_count
    rows = state_rows(groups, query_count)
    own_peak, own_total = (own_ref[height + i * rows : height + (i + 1) * rows] for i in range(2))
    if other_ref.dtype == jnp.bfloat16:
        tail = other_ref[height:]
        pieces = [tail[i * rows : (i + 1) * rows] for i in range(6)]
        other_peak, other_total = from_pieces(pieces[:3]), from_pieces(pieces[3:])
    else:
        other_peak, other_total = (
            other_ref[height + i * rows : height + (i + 1) * rows] for i in range(2)
        )
    peak = jnp.maximum(own_peak, other_peak)
    own_factor, other_factor = jnp.exp(own_peak - peak), jnp.exp(other_peak - peak)
    total = own_total * own_factor + other_total * other_factor
    if last:
        own_factor, other_factor = own_factor / total, other_factor / total
    values = []
    for group in range(groups):
        row, place = divmod(group, per_row)
        at = slice(group * query_count, (group + 1) * query_count)
        values.append(
            own_ref[at] * unpack_column(own_factor[row : row + 1], place, query_count)
            + other_ref[at].astype(jnp.float32)
            * unpack_column(other_factor[row : row + 1], place, query_count)
        )
    return peak, total, values


def combine_body(query_count, groups, own_ref, other_ref, *out_refs):
    height = groups * query_count
    peak, total, values = merge_states(query_count, groups, False, own_ref, other_ref)
    for ref in out_refs:
        tail = [peak, total]
        if ref.dtype == jnp.bfloat16:
            tail = to_pieces(peak) + to_pieces(total)
        spare = ref.shape[0] - height - len(tail) * peak.shape[0]
        tail.append(jnp.zeros((spare, LANES), ref.dtype))
        ref[height:] = jnp.concatenate(tail, axis=0)
        for group, value in enumerate(values):
            ref[group * query_count : (group + 1) * query_count] = value.astype(ref.dtype)


def output_body(query_count, tile, own_ref, other_ref, weight_ref, *refs):
    out_refs, wide_ref = refs[:-1], refs[-1]
    heads = weight_ref.shape[0] // LANES
    tokens = wide_ref.shape[0] // heads
    groups = wide_ref.shape[0] // query_count
    _, _, values = merge_states(query_count, groups, True, own_ref, other_ref)
    for group, value in enumerate(values):
        wide_ref[group * query_count : (group + 1) * query_count] = value
    rows = [wide_ref[pl.ds(head, tokens, stride=heads)] for head in range(heads)]
    rows = jnp.concatenate(rows, axis=1).astype(jnp.bfloat16)
    chunk = out_refs[0].shape[0]
    for col in range(0, weight_ref.shape[1], tile):
        product = jnp.dot(
            rows, weight_ref[:, col : col + tile], preferred_element_type=jnp.float32
        )
        for i, out_ref in enumerate(out_refs):
            out_ref[:, col : col + tile] = product[i * chunk : (i + 1) * chunk].astype(out_ref.dtype)


def shards(
    hidden,
    norm_gain,
    q_weight,
    k_weight,
    v_weight,
    o_weight,
    k_cache,
    v_cache,
    page_table,
    attend_list,
    lengths,
):
    mem_count, head_count = lax.axis_size("mem"), lax.axis_size("heads")
    chunk = hidden.shape[0]
    feature_cols = norm_gain.shape[0]
    query_cols, value_cols = q_weight.shape[1], k_weight.shape[1]
    pool, kv_heads, block, head_dim = k_cache.shape
    row_count, selected = attend_list.shape
    token_count = chunk * head_count
    steps = token_count // row_count
    per_kv = query_cols // head_dim // kv_heads
    query_count = steps * per_kv
    capacity = 2 * row_count * selected // mem_count
    groups = row_count * kv_heads
    height = groups * query_count
    f32, bf16 = jnp.float32, jnp.bfloat16

    own, mate = kernel_call(
        norm_body,
        "norm",
        [jax.ShapeDtypeStruct((chunk, feature_cols + 3 * LANES), bf16)] * 2,
        [pl.BlockSpec(memory_space=pltpu.HBM)],
        2,
        1,
        [pltpu.VMEM(hidden.shape, bf16), pltpu.SemaphoreType.DMA],
    )(pltpu.with_memory_space_constraint(hidden, pltpu.HBM))
    mate = kernel_call(
        pass_body,
        "pass",
        jax.ShapeDtypeStruct(mate.shape, bf16),
        [IN_VMEM],
        1,
        1e10,
    )(mate)
    distances = [*range(2, head_count), 1]
    gathered = distances[::-1]
    pieces = [own] + [swap_across(mate, d) for d in gathered]

    chosen, seen, turned = kernel_call(
        functools.partial(select_body, chunk, steps, per_kv),
        "select",
        [
            pltpu.SMEM((3 * (capacity + 1),), jnp.int32),
            jax.ShapeDtypeStruct((height, LANES), f32),
            jax.ShapeDtypeStruct((capacity, head_dim, kv_heads * block), bf16),
        ],
        [IN_SMEM] * 3 + [IN_VMEM],
        4,
        1e10,
        out_space=[IN_SMEM, IN_VMEM, IN_VMEM],
    )(page_table, attend_list, lengths, k_cache)

    width = query_cols + 2 * value_cols
    summed = kernel_call(
        functools.partial(project_body, (0, *gathered), 512),
        "project",
        jax.ShapeDtypeStruct((width // LANES * token_count, LANES), f32),
        [IN_VMEM] * (head_count + 4),
        4,
        2 * token_count * feature_cols * width,
    )(*pieces, norm_gain, q_weight, k_weight, v_weight)
    sent = summed
    distance = 1
    while 2 * distance < mem_count:
        outs = [jax.ShapeDtypeStruct(summed.shape, f32)]
        if 4 * distance == mem_count:
            outs.append(jax.ShapeDtypeStruct((summed.shape[0] + 16, LANES), f32))
        added = kernel_call(
            functools.partial(add_body, kv_heads * token_count),
            "add",
            outs,
            [IN_VMEM] * 2,
            2,
            1e10,
        )(summed, swap(sent, "mem", crossing(distance)))
        summed, sent = added[0], added[-1]
        distance *= 2

    state = (kv_heads * query_count, LANES)
    partial = kernel_call(
        functools.partial(attend_body, head_dim ** (-0.5), kv_heads * per_kv, query_count),
        "attend",
        jax.ShapeDtypeStruct((height + 8, LANES), f32),
        [IN_SMEM] + [IN_VMEM] * 5,
        4,
        1e10,
        [pltpu.VMEM((row_count, *state), bf16), pltpu.VMEM((capacity, *state), f32)]
        + [pltpu.VMEM((row_count + 1, *state), f32)] * 6,
    )(
        pltpu.with_memory_space_constraint(chosen, pltpu.SMEM),
        seen,
        summed,
        swap(sent.astype(jnp.float16), "mem", crossing(distance)).astype(f32),
        turned,
        v_cache,
    )

    sent = partial
    distance = 1
    while 2 * distance < mem_count:
        outs = [jax.ShapeDtypeStruct(partial.shape, f32)]
        if 4 * distance == mem_count:
            pad = -(-6 * state_rows(groups, query_count) // 16) * 16
            outs.append(jax.ShapeDtypeStruct((height + pad, LANES), bf16))
        merged = kernel_call(
            functools.partial(combine_body, query_count, groups),
            "combine",
            outs,
            [IN_VMEM] * 2,
            2,
            1e10,
        )(partial, swap(sent, "mem", crossing(distance)))
        partial, sent = merged[0], merged[-1]
        distance *= 2

    out_cols = o_weight.shape[1]
    projected = kernel_call(
        functools.partial(output_body, query_count, min(512, out_cols)),
        "output",
        [jax.ShapeDtypeStruct((chunk, out_cols), bf16 if i else f32) for i in range(head_count)],
        [IN_VMEM] * 3,
        4,
        2 * token_count * query_cols * out_cols,
        [pltpu.VMEM((query_cols // LANES * token_count, LANES), f32)],
    )(partial, swap(sent, "mem", crossing(distance)), o_weight)
    total = projected[0]
    for d in distances:
        total = total + swap(projected[d], "heads", d).astype(f32)
    return total.astype(bf16)


def solution(mesh):
    in_specs = (
        P(("groups", "heads"), None),
        P("mem"),
        P("mem", "heads"),
        P("mem", "heads"),
        P("mem", "heads"),
        P("heads", "mem"),
        P(("groups", "mem"), "heads", None, None),
        P(("groups", "mem"), "heads", None, None),
        P("groups", None),
        P("groups", None),
        P("groups"),
    )
    out_specs = P(("groups", "heads"), "mem")
    return jax.shard_map(shards, mesh=mesh, in_specs=in_specs, out_specs=out_specs, check_vma=False)
```

```python
import functools
import math

import jax
import jax.numpy as jnp
from jax import lax
from jax.experimental import pallas as pl
from jax.experimental.pallas import tpu as pltpu
from jax.sharding import PartitionSpec as P

NEG_FILL = -1e30
EPSILON = 1e-05
LANES = 128
MIB = 1 << 20
IN_VMEM = pl.BlockSpec(memory_space=pltpu.VMEM)
IN_SMEM = pl.BlockSpec(memory_space=pltpu.SMEM)


def swap(array, axis, distance):
    count = lax.axis_size(axis)
    return lax.ppermute(array, axis, [(i, i ^ distance) for i in range(count)])


def crossing(distance):
    return distance if distance == 1 else distance + 1


def swap_across(array, distance):
    heads = lax.axis_size("heads")
    count = lax.axis_size("mem") * heads
    pairs = [(i, i ^ heads ^ distance) for i in range(count)]
    return lax.ppermute(array, ("mem", "heads"), pairs)


def kernel_call(body, name, outs, ins, vmem_mib, flops, scratch=(), out_space=IN_VMEM):
    return pl.pallas_call(
        body,
        out_shape=outs,
        in_specs=ins,
        out_specs=out_space if isinstance(out_space, list) else jax.tree.map(lambda _: out_space, outs),
        scratch_shapes=list(scratch),
        name=name,
        compiler_params=pltpu.CompilerParams(vmem_limit_bytes=vmem_mib * MIB),
        cost_estimate=pl.CostEstimate(flops=int(flops), bytes_accessed=1024, transcendentals=0),
    )


def norm_body(hidden_hbm, own_ref, mate_ref, hidden_ref, sem):
    copy = pltpu.make_async_copy(hidden_hbm, hidden_ref, sem)
    copy.start()
    copy.wait()
    cols = own_ref.shape[1] - 3 * LANES
    mem = lax.axis_index("mem")
    hidden = hidden_ref[...].astype(jnp.float32)
    factor = lax.rsqrt(jnp.mean(hidden * hidden, axis=-1, keepdims=True) + EPSILON)
    wide = jnp.broadcast_to(factor, (hidden.shape[0], LANES))
    tail = jnp.concatenate(to_pieces(wide), axis=1)
    for ref, index in ((own_ref, mem), (mate_ref, lax.bitwise_xor(mem, 1))):
        start = pl.multiple_of(index * cols, cols)
        ref[:, :cols] = hidden_ref[:, pl.ds(start, cols)]
        ref[:, cols:] = tail


def select_body(
    chunk, steps, per_kv, table_ref, list_ref, lengths_ref, key_ref, chosen_ref, seen_ref, turned_ref
):
    pool, kv_heads, block, head_dim = key_ref.shape
    mem = lax.axis_index("mem")
    head_shard = lax.axis_index("heads")
    row_count, selected = list_ref.shape
    stride = chosen_ref.shape[0] // 3
    count = jnp.int32(0)
    for row in range(row_count):
        first = row * steps
        place = (lax.bitwise_xor(first // chunk, head_shard) * chunk + first % chunk) // steps
        length = lengths_ref[row]
        for i in range(selected):
            index = list_ref[row, i]
            slot = table_ref[row, index] - mem * pool
            chosen_ref[count] = slot
            chosen_ref[stride + count] = place
            chosen_ref[2 * stride + count] = length - index * block
            count += ((slot >= 0) & (slot < pool)).astype(jnp.int32)
    for c in range(stride - 1):
        live = c < count
        for at, blank in ((c, 0), (stride + c, row_count), (2 * stride + c, 0)):
            chosen_ref[at] = jnp.where(live, chosen_ref[at], blank)
        keys = key_ref[chosen_ref[c]]
        for g in range(kv_heads):
            turned_ref[c, :, g * block : (g + 1) * block] = keys[g].T

    def token_of(place):
        return lax.bitwise_xor(place // chunk, head_shard) * chunk + place % chunk

    tokens = row_count * steps
    heads = kv_heads * per_kv
    at = lax.broadcasted_iota(jnp.int32, seen_ref.shape, 0)
    query_token = token_of(at // heads)
    query_head = at % heads // per_kv
    lane = lax.broadcasted_iota(jnp.int32, seen_ref.shape, 1)
    key_head, key = lane // tokens, lane % tokens
    key_token = token_of(key)
    seen = (
        (query_head == key_head)
        & (query_token // steps == key_token // steps)
        & (key_token <= query_token)
        & (query_token // steps % lax.axis_size("mem") == mem)
    )
    seen_ref[...] = seen.astype(jnp.float32)


def pass_body(in_ref, out_ref):
    out_ref[...] = in_ref[...]


def project_body(places, tile, *refs):
    gain_ref, q_ref, k_ref, v_ref, out_ref = refs[len(places) :]
    chunks = [refs[places.index(i)][...].astype(jnp.float32) for i in range(len(places))]
    rows = jnp.concatenate(chunks, axis=0)
    cols = gain_ref.shape[0]
    gain = gain_ref[...].astype(jnp.float32).reshape(1, cols)
    tail = [rows[:, cols + i * LANES : cols + (i + 1) * LANES] for i in range(3)]
    factor = jnp.concatenate([from_pieces(tail)] * (cols // LANES), axis=1)
    rows = (rows[:, :cols] * factor * gain).astype(jnp.bfloat16)
    tokens = rows.shape[0]
    heads = q_ref.shape[1] // LANES
    head = 0
    for weight in (q_ref, k_ref, v_ref):
        width = min(tile, weight.shape[1])
        for col in range(0, weight.shape[1], width):
            product = jnp.dot(
                rows, weight[:, col : col + width], preferred_element_type=jnp.float32
            )
            for lane in range(0, width, LANES):
                columns = product[:, lane : lane + LANES]
                if head < heads:
                    out_ref[pl.ds(head, tokens, stride=heads)] = columns
                else:
                    out_ref[head * tokens : (head + 1) * tokens] = columns
                head += 1


def add_body(values, own_ref, other_ref, out_ref, *sent_refs):
    total = own_ref[...] + other_ref[...]
    out_ref[...] = total
    for ref in sent_refs:
        height = total.shape[0]
        top = jnp.max(jnp.abs(total[height - values :]), axis=0, keepdims=True)
        top = jnp.maximum(top, 1e-30)
        exponent = jnp.ceil(jnp.log(top) * (1 / math.log(2)))
        ref[: height - values] = total[: height - values]
        ref[height - values : height] = total[height - values :] * jnp.exp2(-exponent)
        ref[height:] = jnp.broadcast_to(exponent, (ref.shape[0] - height, LANES))


def add_sent(own_ref, sent_ref, values):
    height = own_ref.shape[0]
    scale = jnp.exp2(sent_ref[height : height + 1])
    sent_values = sent_ref[height - values : height] * scale
    sent = jnp.concatenate([sent_ref[: height - values], sent_values], axis=0)
    return own_ref[...] + sent


def split_dot(weights, values):
    high = weights.astype(jnp.bfloat16)
    low = (weights - high.astype(jnp.float32)).astype(jnp.bfloat16)
    both = jnp.dot(
        jnp.concatenate([high, low], axis=0), values, preferred_element_type=jnp.float32
    )
    return both[: weights.shape[0]] + both[weights.shape[0] :]


def to_pieces(rows):
    pieces = []
    for _ in range(3):
        pieces.append(rows.astype(jnp.bfloat16))
        rows = rows - pieces[-1].astype(jnp.float32)
    return pieces


def from_pieces(pieces):
    high, middle, low = [piece.astype(jnp.float32) for piece in pieces]
    return low + middle + high


def group_lanes(query_count):
    lane = lax.broadcasted_iota(jnp.int32, (query_count, LANES), 1)
    row = lax.broadcasted_iota(jnp.int32, (query_count, LANES), 0)
    return lane - row


def pack_columns(column, query_count):
    per_row = LANES // query_count
    offset = group_lanes(query_count)
    groups = column.shape[0] // query_count
    rows = []
    for first in range(0, groups, per_row):
        row = jnp.zeros((query_count, LANES), jnp.float32)
        for i in range(min(per_row, groups - first)):
            at = (first + i) * query_count
            row = jnp.where(offset == i * query_count, column[at : at + query_count], row)
        rows.append(jnp.sum(row, axis=0, keepdims=True))
    return rows


def unpack_column(row, place, query_count):
    spread = jnp.broadcast_to(row, (query_count, LANES))
    picked = jnp.where(group_lanes(query_count) == place * query_count, spread, 0.0)
    return jnp.sum(picked, axis=1, keepdims=True)


def attend_body(
    scale,
    heads,
    query_count,
    chosen_ref,
    seen_ref,
    own_ref,
    other_ref,
    turned_ref,
    value_ref,
    out_ref,
    query_ref,
    score_ref,
    total_ref,
    accum_ref,
    *peak_refs,
):
    row_count, row_height, head_dim = query_ref.shape
    kv_heads = value_ref.shape[1]
    capacity = score_ref.shape[0]
    height = row_count * row_height
    contract_last = (((1,), (1,)), ((), ()))

    values = (own_ref.shape[0] - height) // 2
    projected = add_sent(own_ref, other_ref, values).astype(jnp.bfloat16)
    queries = projected[:height]
    query_ref[...] = queries.reshape(query_ref.shape)
    fresh = projected[height:]
    count = fresh.shape[0] // 2
    spare = jnp.zeros((LANES - count, head_dim), jnp.bfloat16)
    seen = seen_ref[...] > 0
    fresh_score = lax.dot_general(
        queries,
        jnp.concatenate([fresh[:count], spare], axis=0),
        contract_last,
        preferred_element_type=jnp.float32,
    )
    fresh_score = jnp.where(seen, fresh_score * scale, NEG_FILL)
    peak_ref = peak_refs[0]
    peak_ref[:row_count] = fresh_score.reshape(row_count, row_height, LANES)
    peak_ref[row_count] = jnp.full((row_height, LANES), NEG_FILL, jnp.float32)
    for ref in peak_refs[1:]:
        ref[...] = jnp.full(ref.shape, NEG_FILL, jnp.float32)
    stride = chosen_ref.shape[0] // 3

    lane = lax.broadcasted_iota(jnp.int32, (row_height, LANES), 1)
    head_of = lax.broadcasted_iota(jnp.int32, (row_height, LANES), 0) % heads // (heads // kv_heads)
    for c in range(capacity):
        slot, row, valid = (chosen_ref[i * stride + c] for i in range(3))
        every = jnp.dot(
            query_ref[jnp.minimum(row, row_count - 1)],
            turned_ref[c],
            preferred_element_type=jnp.float32,
        )
        score = every[:, :LANES]
        for g in range(1, kv_heads):
            score = jnp.where(head_of == g, every[:, g * LANES : (g + 1) * LANES], score)
        score = jnp.where(lane < valid, score * scale, NEG_FILL)
        score_ref[c] = score
        ref = peak_refs[c % len(peak_refs)]
        ref[row] = jnp.maximum(ref[row], score)

    peak = functools.reduce(jnp.maximum, [ref[:row_count] for ref in peak_refs])
    peak = jnp.max(peak.reshape(height, LANES), axis=1, keepdims=True)
    peak = jnp.broadcast_to(peak, (height, LANES))
    peak_ref[:row_count] = peak.reshape(row_count, row_height, LANES)
    weights = jnp.where(seen, jnp.exp(fresh_score - peak), 0.0)
    total_ref[:row_count] = weights.reshape(row_count, row_height, LANES)
    total_ref[row_count] = jnp.zeros((row_height, LANES), jnp.float32)
    accum = split_dot(weights, jnp.concatenate([fresh[count:], spare], axis=0))
    accum_ref[:row_count] = accum.reshape(row_count, row_height, head_dim)
    accum_ref[row_count] = jnp.zeros((row_height, head_dim), jnp.float32)

    for c in range(capacity):
        slot, row = chosen_ref[c], chosen_ref[stride + c]
        weights = jnp.exp(score_ref[c] - peak_ref[row])
        total_ref[row] += weights
        spread = [jnp.where(head_of == g, weights, 0.0) for g in range(kv_heads)]
        accum_ref[row] += split_dot(
            jnp.concatenate(spread, axis=1), value_ref[slot].reshape(kv_heads * LANES, head_dim)
        )

    total = jnp.sum(total_ref[:row_count].reshape(height, LANES), axis=1, keepdims=True)
    total = jnp.broadcast_to(total, (height, LANES))
    out_ref[:height] = accum_ref[:row_count].reshape(height, head_dim)
    packed = pack_columns(peak, query_count) + pack_columns(total, query_count)
    spare = out_ref.shape[0] - height - len(packed)
    packed.append(jnp.zeros((spare, LANES), jnp.float32))
    out_ref[height:] = jnp.concatenate(packed, axis=0)


def state_rows(groups, query_count):
    return -(-groups // (LANES // query_count))


def merge_states(query_count, groups, last, own_ref, other_ref):
    per_row = LANES // query_count
    height = groups * query_count
    rows = state_rows(groups, query_count)
    own_peak, own_total = (own_ref[height + i * rows : height + (i + 1) * rows] for i in range(2))
    if other_ref.dtype == jnp.bfloat16:
        tail = other_ref[height:]
        pieces = [tail[i * rows : (i + 1) * rows] for i in range(6)]
        other_peak, other_total = from_pieces(pieces[:3]), from_pieces(pieces[3:])
    else:
        other_peak, other_total = (
            other_ref[height + i * rows : height + (i + 1) * rows] for i in range(2)
        )
    peak = jnp.maximum(own_peak, other_peak)
    own_factor, other_factor = jnp.exp(own_peak - peak), jnp.exp(other_peak - peak)
    total = own_total * own_factor + other_total * other_factor
    if last:
        own_factor, other_factor = own_factor / total, other_factor / total
    values = []
    for group in range(groups):
        row, place = divmod(group, per_row)
        at = slice(group * query_count, (group + 1) * query_count)
        values.append(
            own_ref[at] * unpack_column(own_factor[row : row + 1], place, query_count)
            + other_ref[at].astype(jnp.float32)
            * unpack_column(other_factor[row : row + 1], place, query_count)
        )
    return peak, total, values


def combine_body(query_count, groups, own_ref, other_ref, *out_refs):
    height = groups * query_count
    peak, total, values = merge_states(query_count, groups, False, own_ref, other_ref)
    for ref in out_refs:
        tail = [peak, total]
        if ref.dtype == jnp.bfloat16:
            tail = to_pieces(peak) + to_pieces(total)
        spare = ref.shape[0] - height - len(tail) * peak.shape[0]
        tail.append(jnp.zeros((spare, LANES), ref.dtype))
        ref[height:] = jnp.concatenate(tail, axis=0)
        for group, value in enumerate(values):
            ref[group * query_count : (group + 1) * query_count] = value.astype(ref.dtype)


def output_body(query_count, tile, own_ref, other_ref, weight_ref, *refs):
    out_refs, wide_ref = refs[:-1], refs[-1]
    heads = weight_ref.shape[0] // LANES
    tokens = wide_ref.shape[0] // heads
    groups = wide_ref.shape[0] // query_count
    _, _, values = merge_states(query_count, groups, True, own_ref, other_ref)
    for group, value in enumerate(values):
        wide_ref[group * query_count : (group + 1) * query_count] = value
    rows = [wide_ref[pl.ds(head, tokens, stride=heads)] for head in range(heads)]
    rows = jnp.concatenate(rows, axis=1).astype(jnp.bfloat16)
    chunk = out_refs[0].shape[0]
    for col in range(0, weight_ref.shape[1], tile):
        product = jnp.dot(
            rows, weight_ref[:, col : col + tile], preferred_element_type=jnp.float32
        )
        for i, out_ref in enumerate(out_refs):
            out_ref[:, col : col + tile] = product[i * chunk : (i + 1) * chunk].astype(out_ref.dtype)


def shards(
    hidden,
    norm_gain,
    q_weight,
    k_weight,
    v_weight,
    o_weight,
    k_cache,
    v_cache,
    page_table,
    attend_list,
    lengths,
):
    mem_count, head_count = lax.axis_size("mem"), lax.axis_size("heads")
    chunk = hidden.shape[0]
    feature_cols = norm_gain.shape[0]
    query_cols, value_cols = q_weight.shape[1], k_weight.shape[1]
    pool, kv_heads, block, head_dim = k_cache.shape
    row_count, selected = attend_list.shape
    token_count = chunk * head_count
    steps = token_count // row_count
    per_kv = query_cols // head_dim // kv_heads
    query_count = steps * per_kv
    capacity = 2 * row_count * selected // mem_count
    groups = row_count * kv_heads
    height = groups * query_count
    f32, bf16 = jnp.float32, jnp.bfloat16

    own, mate = kernel_call(
        norm_body,
        "norm",
        [jax.ShapeDtypeStruct((chunk, feature_cols + 3 * LANES), bf16)] * 2,
        [pl.BlockSpec(memory_space=pltpu.HBM)],
        2,
        1,
        [pltpu.VMEM(hidden.shape, bf16), pltpu.SemaphoreType.DMA],
    )(pltpu.with_memory_space_constraint(hidden, pltpu.HBM))
    mate = kernel_call(
        pass_body,
        "pass",
        jax.ShapeDtypeStruct(mate.shape, bf16),
        [IN_VMEM],
        1,
        1e10,
    )(mate)
    distances = [*range(2, head_count), 1]
    gathered = distances[::-1]
    pieces = [own] + [swap_across(mate, d) for d in gathered]

    chosen, seen, turned = kernel_call(
        functools.partial(select_body, chunk, steps, per_kv),
        "select",
        [
            pltpu.SMEM((3 * (capacity + 1),), jnp.int32),
            jax.ShapeDtypeStruct((height, LANES), f32),
            jax.ShapeDtypeStruct((capacity, head_dim, kv_heads * block), bf16),
        ],
        [IN_SMEM] * 3 + [IN_VMEM],
        4,
        1e10,
        out_space=[IN_SMEM, IN_VMEM, IN_VMEM],
    )(page_table, attend_list, lengths, k_cache)

    width = query_cols + 2 * value_cols
    summed = kernel_call(
        functools.partial(project_body, (0, *gathered), 512),
        "project",
        jax.ShapeDtypeStruct((width // LANES * token_count, LANES), f32),
        [IN_VMEM] * (head_count + 4),
        4,
        2 * token_count * feature_cols * width,
    )(*pieces, norm_gain, q_weight, k_weight, v_weight)
    sent = summed
    distance = 1
    while 2 * distance < mem_count:
        outs = [jax.ShapeDtypeStruct(summed.shape, f32)]
        if 4 * distance == mem_count:
            outs.append(jax.ShapeDtypeStruct((summed.shape[0] + 16, LANES), f32))
        added = kernel_call(
            functools.partial(add_body, kv_heads * token_count),
            "add",
            outs,
            [IN_VMEM] * 2,
            2,
            1e10,
        )(summed, swap(sent, "mem", crossing(distance)))
        summed, sent = added[0], added[-1]
        distance *= 2

    state = (kv_heads * query_count, LANES)
    partial = kernel_call(
        functools.partial(attend_body, head_dim ** (-0.5), kv_heads * per_kv, query_count),
        "attend",
        jax.ShapeDtypeStruct((height + 8, LANES), f32),
        [IN_SMEM] + [IN_VMEM] * 5,
        4,
        1e10,
        [pltpu.VMEM((row_count, *state), bf16), pltpu.VMEM((capacity, *state), f32)]
        + [pltpu.VMEM((row_count + 1, *state), f32)] * 6,
    )(
        pltpu.with_memory_space_constraint(chosen, pltpu.SMEM),
        seen,
        summed,
        swap(sent.astype(jnp.float16), "mem", crossing(distance)).astype(f32),
        turned,
        v_cache,
    )

    sent = partial
    distance = 1
    while 2 * distance < mem_count:
        outs = [jax.ShapeDtypeStruct(partial.shape, f32)]
        if 4 * distance == mem_count:
            pad = -(-6 * state_rows(groups, query_count) // 16) * 16
            outs.append(jax.ShapeDtypeStruct((height + pad, LANES), bf16))
        merged = kernel_call(
            functools.partial(combine_body, query_count, groups),
            "combine",
            outs,
            [IN_VMEM] * 2,
            2,
            1e10,
        )(partial, swap(sent, "mem", crossing(distance)))
        partial, sent = merged[0], merged[-1]
        distance *= 2

    out_cols = o_weight.shape[1]
    projected = kernel_call(
        functools.partial(output_body, query_count, min(512, out_cols)),
        "output",
        [jax.ShapeDtypeStruct((chunk, out_cols), bf16 if i else f32) for i in range(head_count)],
        [IN_VMEM] * 3,
        4,
        2 * token_count * query_cols * out_cols,
        [pltpu.VMEM((query_cols // LANES * token_count, LANES), f32)],
    )(partial, swap(sent, "mem", crossing(distance)), o_weight)
    total = projected[0]
    for d in distances:
        total = total + swap(projected[d], "heads", d).astype(f32)
    return total.astype(bf16)


def solution(mesh):
    in_specs = (
        P(("groups", "heads"), None),
        P("mem"),
        P("mem", "heads"),
        P("mem", "heads"),
        P("mem", "heads"),
        P("heads", "mem"),
        P(("groups", "mem"), "heads", None, None),
        P(("groups", "mem"), "heads", None, None),
        P("groups", None),
        P("groups", None),
        P("groups"),
    )
    out_specs = P(("groups", "heads"), "mem")
    return jax.shard_map(shards, mesh=mesh, in_specs=in_specs, out_specs=out_specs, check_vma=False)
```

```python
import functools
import math

import jax
import jax.numpy as jnp
from jax import lax
from jax.experimental import pallas as pl
from jax.experimental.pallas import tpu as pltpu
from jax.sharding import PartitionSpec as P

NEG_FILL = -1e30
EPSILON = 1e-05
LANES = 128
MIB = 1 << 20
IN_VMEM = pl.BlockSpec(memory_space=pltpu.VMEM)
IN_SMEM = pl.BlockSpec(memory_space=pltpu.SMEM)


def swap(array, axis, distance):
    count = lax.axis_size(axis)
    return lax.ppermute(array, axis, [(i, i ^ distance) for i in range(count)])


def crossing(distance):
    return distance if distance == 1 else distance + 1


def swap_across(array, distance):
    heads = lax.axis_size("heads")
    count = lax.axis_size("mem") * heads
    pairs = [(i, i ^ heads ^ distance) for i in range(count)]
    return lax.ppermute(array, ("mem", "heads"), pairs)


def kernel_call(body, name, outs, ins, vmem_mib, flops, scratch=(), out_space=IN_VMEM):
    return pl.pallas_call(
        body,
        out_shape=outs,
        in_specs=ins,
        out_specs=out_space if isinstance(out_space, list) else jax.tree.map(lambda _: out_space, outs),
        scratch_shapes=list(scratch),
        name=name,
        compiler_params=pltpu.CompilerParams(vmem_limit_bytes=vmem_mib * MIB),
        cost_estimate=pl.CostEstimate(flops=int(flops), bytes_accessed=1024, transcendentals=0),
    )


def norm_body(hidden_hbm, own_ref, mate_ref, hidden_ref, sem):
    copy = pltpu.make_async_copy(hidden_hbm, hidden_ref, sem)
    copy.start()
    copy.wait()
    cols = own_ref.shape[1] - 3 * LANES
    mem = lax.axis_index("mem")
    hidden = hidden_ref[...].astype(jnp.float32)
    factor = lax.rsqrt(jnp.mean(hidden * hidden, axis=-1, keepdims=True) + EPSILON)
    wide = jnp.broadcast_to(factor, (hidden.shape[0], LANES))
    tail = jnp.concatenate(to_pieces(wide), axis=1)
    for ref, index in ((own_ref, mem), (mate_ref, lax.bitwise_xor(mem, 1))):
        start = pl.multiple_of(index * cols, cols)
        ref[:, :cols] = hidden_ref[:, pl.ds(start, cols)]
        ref[:, cols:] = tail


def select_body(
    chunk, steps, per_kv, table_ref, list_ref, lengths_ref, key_ref, chosen_ref, seen_ref, turned_ref
):
    pool, kv_heads, block, head_dim = key_ref.shape
    mem = lax.axis_index("mem")
    head_shard = lax.axis_index("heads")
    row_count, selected = list_ref.shape
    stride = chosen_ref.shape[0] // 3
    count = jnp.int32(0)
    for row in range(row_count):
        first = row * steps
        place = (lax.bitwise_xor(first // chunk, head_shard) * chunk + first % chunk) // steps
        length = lengths_ref[row]
        for i in range(selected):
            index = list_ref[row, i]
            slot = table_ref[row, index] - mem * pool
            chosen_ref[count] = slot
            chosen_ref[stride + count] = place
            chosen_ref[2 * stride + count] = length - index * block
            count += ((slot >= 0) & (slot < pool)).astype(jnp.int32)
    for c in range(stride - 1):
        live = c < count
        for at, blank in ((c, 0), (stride + c, row_count), (2 * stride + c, 0)):
            chosen_ref[at] = jnp.where(live, chosen_ref[at], blank)
        keys = key_ref[chosen_ref[c]]
        for g in range(kv_heads):
            turned_ref[c, :, g * block : (g + 1) * block] = keys[g].T

    def token_of(place):
        return lax.bitwise_xor(place // chunk, head_shard) * chunk + place % chunk

    tokens = row_count * steps
    heads = kv_heads * per_kv
    at = lax.broadcasted_iota(jnp.int32, seen_ref.shape, 0)
    query_token = token_of(at // heads)
    query_head = at % heads // per_kv
    place = at // heads // steps
    half = lax.axis_size("mem") // 2
    owner = place // (row_count // 2) * half + place % half
    lane = lax.broadcasted_iota(jnp.int32, seen_ref.shape, 1)
    key_head, key = lane // tokens, lane % tokens
    key_token = token_of(key)
    seen = (
        (query_head == key_head)
        & (query_token // steps == key_token // steps)
        & (key_token <= query_token)
        & (owner == mem)
    )
    seen_ref[...] = seen.astype(jnp.float32)


def pass_body(in_ref, out_ref):
    out_ref[...] = in_ref[...]


def project_body(places, tile, *refs):
    gain_ref, q_ref, k_ref, v_ref, out_ref = refs[len(places) :]
    chunks = [refs[places.index(i)][...].astype(jnp.float32) for i in range(len(places))]
    rows = jnp.concatenate(chunks, axis=0)
    cols = gain_ref.shape[0]
    gain = gain_ref[...].astype(jnp.float32).reshape(1, cols)
    tail = [rows[:, cols + i * LANES : cols + (i + 1) * LANES] for i in range(3)]
    factor = jnp.concatenate([from_pieces(tail)] * (cols // LANES), axis=1)
    rows = (rows[:, :cols] * factor * gain).astype(jnp.bfloat16)
    tokens = rows.shape[0]
    heads = q_ref.shape[1] // LANES
    head = 0
    for weight in (q_ref, k_ref, v_ref):
        width = min(tile, weight.shape[1])
        for col in range(0, weight.shape[1], width):
            product = jnp.dot(
                rows, weight[:, col : col + width], preferred_element_type=jnp.float32
            )
            for lane in range(0, width, LANES):
                columns = product[:, lane : lane + LANES]
                if head < heads:
                    out_ref[pl.ds(head, tokens, stride=heads)] = columns
                else:
                    out_ref[head * tokens : (head + 1) * tokens] = columns
                head += 1


def add_body(values, tokens, own_ref, other_ref, out_ref, *sent_refs):
    total = own_ref[...] + other_ref[...]
    out_ref[...] = total
    for ref in sent_refs:
        height = total.shape[0]
        top = jnp.max(jnp.abs(total[height - values :]), axis=0, keepdims=True)
        top = jnp.maximum(top, 1e-30)
        exponent = jnp.ceil(jnp.log(top) * (1 / math.log(2)))
        mem, half = lax.axis_index("mem"), lax.axis_size("mem") // 2
        theirs = pl.multiple_of((1 - mem // half) * (tokens // 2), tokens // 2)
        first = height - 2 * values
        ref[:first] = total[:first]
        at = first
        for block in range(first, height, tokens):
            rows = out_ref[pl.ds(block + theirs, tokens // 2)]
            if block >= height - values:
                rows = rows * jnp.exp2(-exponent)
            ref[at : at + tokens // 2] = rows
            at += tokens // 2
        ref[at:] = jnp.broadcast_to(exponent, (ref.shape[0] - at, LANES))


def add_sent(own_ref, sent_ref, values, tokens):
    height = own_ref.shape[0]
    first = height - 2 * values
    parts = [sent_ref[:first]]
    scale = jnp.exp2(sent_ref[first + values : first + values + 1])
    for at in range(first, first + values, tokens // 2):
        rows = sent_ref[at : at + tokens // 2]
        if at >= first + values // 2:
            rows = rows * scale
        parts += [rows, rows]
    return own_ref[...] + jnp.concatenate(parts, axis=0)


def split_dot(weights, values):
    high = weights.astype(jnp.bfloat16)
    low = (weights - high.astype(jnp.float32)).astype(jnp.bfloat16)
    both = jnp.dot(
        jnp.concatenate([high, low], axis=0), values, preferred_element_type=jnp.float32
    )
    return both[: weights.shape[0]] + both[weights.shape[0] :]


def to_pieces(rows):
    pieces = []
    for _ in range(3):
        pieces.append(rows.astype(jnp.bfloat16))
        rows = rows - pieces[-1].astype(jnp.float32)
    return pieces


def from_pieces(pieces):
    high, middle, low = [piece.astype(jnp.float32) for piece in pieces]
    return low + middle + high


def group_lanes(query_count):
    lane = lax.broadcasted_iota(jnp.int32, (query_count, LANES), 1)
    row = lax.broadcasted_iota(jnp.int32, (query_count, LANES), 0)
    return lane - row


def pack_columns(column, query_count):
    per_row = LANES // query_count
    offset = group_lanes(query_count)
    groups = column.shape[0] // query_count
    rows = []
    for first in range(0, groups, per_row):
        row = jnp.zeros((query_count, LANES), jnp.float32)
        for i in range(min(per_row, groups - first)):
            at = (first + i) * query_count
            row = jnp.where(offset == i * query_count, column[at : at + query_count], row)
        rows.append(jnp.sum(row, axis=0, keepdims=True))
    return rows


def unpack_column(row, place, query_count):
    spread = jnp.broadcast_to(row, (query_count, LANES))
    picked = jnp.where(group_lanes(query_count) == place * query_count, spread, 0.0)
    return jnp.sum(picked, axis=1, keepdims=True)


def attend_body(
    scale,
    heads,
    query_count,
    chosen_ref,
    seen_ref,
    own_ref,
    other_ref,
    turned_ref,
    value_ref,
    out_ref,
    query_ref,
    score_ref,
    total_ref,
    accum_ref,
    *peak_refs,
):
    row_count, row_height, head_dim = query_ref.shape
    kv_heads = value_ref.shape[1]
    capacity = score_ref.shape[0]
    height = row_count * row_height
    contract_last = (((1,), (1,)), ((), ()))

    values = (own_ref.shape[0] - height) // 2
    projected = add_sent(own_ref, other_ref, values, values // kv_heads).astype(jnp.bfloat16)
    queries = projected[:height]
    query_ref[...] = queries.reshape(query_ref.shape)
    fresh = projected[height:]
    count = fresh.shape[0] // 2
    spare = jnp.zeros((LANES - count, head_dim), jnp.bfloat16)
    seen = seen_ref[...] > 0
    fresh_score = lax.dot_general(
        queries,
        jnp.concatenate([fresh[:count], spare], axis=0),
        contract_last,
        preferred_element_type=jnp.float32,
    )
    fresh_score = jnp.where(seen, fresh_score * scale, NEG_FILL)
    peak_ref = peak_refs[0]
    peak_ref[:row_count] = fresh_score.reshape(row_count, row_height, LANES)
    peak_ref[row_count] = jnp.full((row_height, LANES), NEG_FILL, jnp.float32)
    for ref in peak_refs[1:]:
        ref[...] = jnp.full(ref.shape, NEG_FILL, jnp.float32)
    stride = chosen_ref.shape[0] // 3

    lane = lax.broadcasted_iota(jnp.int32, (row_height, LANES), 1)
    head_of = lax.broadcasted_iota(jnp.int32, (row_height, LANES), 0) % heads // (heads // kv_heads)
    for c in range(capacity):
        slot, row, valid = (chosen_ref[i * stride + c] for i in range(3))
        every = jnp.dot(
            query_ref[jnp.minimum(row, row_count - 1)],
            turned_ref[c],
            preferred_element_type=jnp.float32,
        )
        score = every[:, :LANES]
        for g in range(1, kv_heads):
            score = jnp.where(head_of == g, every[:, g * LANES : (g + 1) * LANES], score)
        score = jnp.where(lane < valid, score * scale, NEG_FILL)
        score_ref[c] = score
        ref = peak_refs[c % len(peak_refs)]
        ref[row] = jnp.maximum(ref[row], score)

    peak = functools.reduce(jnp.maximum, [ref[:row_count] for ref in peak_refs])
    peak = jnp.max(peak.reshape(height, LANES), axis=1, keepdims=True)
    peak = jnp.broadcast_to(peak, (height, LANES))
    peak_ref[:row_count] = peak.reshape(row_count, row_height, LANES)
    weights = jnp.where(seen, jnp.exp(fresh_score - peak), 0.0)
    total_ref[:row_count] = weights.reshape(row_count, row_height, LANES)
    total_ref[row_count] = jnp.zeros((row_height, LANES), jnp.float32)
    accum = split_dot(weights, jnp.concatenate([fresh[count:], spare], axis=0))
    accum_ref[:row_count] = accum.reshape(row_count, row_height, head_dim)
    accum_ref[row_count] = jnp.zeros((row_height, head_dim), jnp.float32)

    for c in range(capacity):
        slot, row = chosen_ref[c], chosen_ref[stride + c]
        weights = jnp.exp(score_ref[c] - peak_ref[row])
        total_ref[row] += weights
        spread = [jnp.where(head_of == g, weights, 0.0) for g in range(kv_heads)]
        accum_ref[row] += split_dot(
            jnp.concatenate(spread, axis=1), value_ref[slot].reshape(kv_heads * LANES, head_dim)
        )

    total = jnp.sum(total_ref[:row_count].reshape(height, LANES), axis=1, keepdims=True)
    total = jnp.broadcast_to(total, (height, LANES))
    out_ref[:height] = accum_ref[:row_count].reshape(height, head_dim)
    packed = pack_columns(peak, query_count) + pack_columns(total, query_count)
    spare = out_ref.shape[0] - height - len(packed)
    packed.append(jnp.zeros((spare, LANES), jnp.float32))
    out_ref[height:] = jnp.concatenate(packed, axis=0)


def state_rows(groups, query_count):
    return -(-groups // (LANES // query_count))


def merge_states(query_count, groups, last, own_ref, other_ref):
    per_row = LANES // query_count
    height = groups * query_count
    rows = state_rows(groups, query_count)
    own_peak, own_total = (own_ref[height + i * rows : height + (i + 1) * rows] for i in range(2))
    if other_ref.dtype == jnp.bfloat16:
        tail = other_ref[height:]
        pieces = [tail[i * rows : (i + 1) * rows] for i in range(6)]
        other_peak, other_total = from_pieces(pieces[:3]), from_pieces(pieces[3:])
    else:
        other_peak, other_total = (
            other_ref[height + i * rows : height + (i + 1) * rows] for i in range(2)
        )
    peak = jnp.maximum(own_peak, other_peak)
    own_factor, other_factor = jnp.exp(own_peak - peak), jnp.exp(other_peak - peak)
    total = own_total * own_factor + other_total * other_factor
    if last:
        own_factor, other_factor = own_factor / total, other_factor / total
    values = []
    for group in range(groups):
        row, place = divmod(group, per_row)
        at = slice(group * query_count, (group + 1) * query_count)
        values.append(
            own_ref[at] * unpack_column(own_factor[row : row + 1], place, query_count)
            + other_ref[at].astype(jnp.float32)
            * unpack_column(other_factor[row : row + 1], place, query_count)
        )
    return peak, total, values


def combine_body(query_count, groups, own_ref, other_ref, *out_refs):
    height = groups * query_count
    peak, total, values = merge_states(query_count, groups, False, own_ref, other_ref)
    for ref in out_refs:
        tail = [peak, total]
        if ref.dtype == jnp.bfloat16:
            tail = to_pieces(peak) + to_pieces(total)
        spare = ref.shape[0] - height - len(tail) * peak.shape[0]
        tail.append(jnp.zeros((spare, LANES), ref.dtype))
        ref[height:] = jnp.concatenate(tail, axis=0)
        for group, value in enumerate(values):
            ref[group * query_count : (group + 1) * query_count] = value.astype(ref.dtype)


def output_body(query_count, tile, own_ref, other_ref, weight_ref, *refs):
    out_refs, wide_ref = refs[:-1], refs[-1]
    heads = weight_ref.shape[0] // LANES
    tokens = wide_ref.shape[0] // heads
    groups = wide_ref.shape[0] // query_count
    _, _, values = merge_states(query_count, groups, True, own_ref, other_ref)
    for group, value in enumerate(values):
        wide_ref[group * query_count : (group + 1) * query_count] = value
    rows = [wide_ref[pl.ds(head, tokens, stride=heads)] for head in range(heads)]
    rows = jnp.concatenate(rows, axis=1).astype(jnp.bfloat16)
    chunk = out_refs[0].shape[0]
    for col in range(0, weight_ref.shape[1], tile):
        product = jnp.dot(
            rows, weight_ref[:, col : col + tile], preferred_element_type=jnp.float32
        )
        for i, out_ref in enumerate(out_refs):
            out_ref[:, col : col + tile] = product[i * chunk : (i + 1) * chunk].astype(out_ref.dtype)


def shards(
    hidden,
    norm_gain,
    q_weight,
    k_weight,
    v_weight,
    o_weight,
    k_cache,
    v_cache,
    page_table,
    attend_list,
    lengths,
):
    mem_count, head_count = lax.axis_size("mem"), lax.axis_size("heads")
    chunk = hidden.shape[0]
    feature_cols = norm_gain.shape[0]
    query_cols, value_cols = q_weight.shape[1], k_weight.shape[1]
    pool, kv_heads, block, head_dim = k_cache.shape
    row_count, selected = attend_list.shape
    token_count = chunk * head_count
    steps = token_count // row_count
    per_kv = query_cols // head_dim // kv_heads
    query_count = steps * per_kv
    capacity = 2 * row_count * selected // mem_count
    groups = row_count * kv_heads
    height = groups * query_count
    f32, bf16 = jnp.float32, jnp.bfloat16

    own, mate = kernel_call(
        norm_body,
        "norm",
        [jax.ShapeDtypeStruct((chunk, feature_cols + 3 * LANES), bf16)] * 2,
        [pl.BlockSpec(memory_space=pltpu.HBM)],
        2,
        1,
        [pltpu.VMEM(hidden.shape, bf16), pltpu.SemaphoreType.DMA],
    )(pltpu.with_memory_space_constraint(hidden, pltpu.HBM))
    mate = kernel_call(
        pass_body,
        "pass",
        jax.ShapeDtypeStruct(mate.shape, bf16),
        [IN_VMEM],
        1,
        1e10,
    )(mate)
    distances = [*range(2, head_count), 1]
    gathered = distances[::-1]
    pieces = [own] + [swap_across(mate, d) for d in gathered]

    chosen, seen, turned = kernel_call(
        functools.partial(select_body, chunk, steps, per_kv),
        "select",
        [
            pltpu.SMEM((3 * (capacity + 1),), jnp.int32),
            jax.ShapeDtypeStruct((height, LANES), f32),
            jax.ShapeDtypeStruct((capacity, head_dim, kv_heads * block), bf16),
        ],
        [IN_SMEM] * 3 + [IN_VMEM],
        4,
        1e10,
        out_space=[IN_SMEM, IN_VMEM, IN_VMEM],
    )(page_table, attend_list, lengths, k_cache)

    width = query_cols + 2 * value_cols
    summed = kernel_call(
        functools.partial(project_body, (0, *gathered), 512),
        "project",
        jax.ShapeDtypeStruct((width // LANES * token_count, LANES), f32),
        [IN_VMEM] * (head_count + 4),
        4,
        2 * token_count * feature_cols * width,
    )(*pieces, norm_gain, q_weight, k_weight, v_weight)
    sent = summed
    distance = 1
    while 2 * distance < mem_count:
        outs = [jax.ShapeDtypeStruct(summed.shape, f32)]
        if 4 * distance == mem_count:
            outs.append(jax.ShapeDtypeStruct((summed.shape[0] - kv_heads * token_count + 16, LANES), f32))
        added = kernel_call(
            functools.partial(add_body, kv_heads * token_count, token_count),
            "add",
            outs,
            [IN_VMEM] * 2,
            2,
            1e10,
        )(summed, swap(sent, "mem", crossing(distance)))
        summed, sent = added[0], added[-1]
        distance *= 2

    state = (kv_heads * query_count, LANES)
    partial = kernel_call(
        functools.partial(attend_body, head_dim ** (-0.5), kv_heads * per_kv, query_count),
        "attend",
        jax.ShapeDtypeStruct((height + 8, LANES), f32),
        [IN_SMEM] + [IN_VMEM] * 5,
        4,
        1e10,
        [pltpu.VMEM((row_count, *state), bf16), pltpu.VMEM((capacity, *state), f32)]
        + [pltpu.VMEM((row_count + 1, *state), f32)] * 6,
    )(
        pltpu.with_memory_space_constraint(chosen, pltpu.SMEM),
        seen,
        summed,
        swap(sent.astype(jnp.float16), "mem", crossing(distance)).astype(f32),
        turned,
        v_cache,
    )

    sent = partial
    distance = 1
    while 2 * distance < mem_count:
        outs = [jax.ShapeDtypeStruct(partial.shape, f32)]
        if 4 * distance == mem_count:
            pad = -(-6 * state_rows(groups, query_count) // 16) * 16
            outs.append(jax.ShapeDtypeStruct((height + pad, LANES), bf16))
        merged = kernel_call(
            functools.partial(combine_body, query_count, groups),
            "combine",
            outs,
            [IN_VMEM] * 2,
            2,
            1e10,
        )(partial, swap(sent, "mem", crossing(distance)))
        partial, sent = merged[0], merged[-1]
        distance *= 2

    out_cols = o_weight.shape[1]
    projected = kernel_call(
        functools.partial(output_body, query_count, min(512, out_cols)),
        "output",
        [jax.ShapeDtypeStruct((chunk, out_cols), bf16 if i else f32) for i in range(head_count)],
        [IN_VMEM] * 3,
        4,
        2 * token_count * query_cols * out_cols,
        [pltpu.VMEM((query_cols // LANES * token_count, LANES), f32)],
    )(partial, swap(sent, "mem", crossing(distance)), o_weight)
    total = projected[0]
    for d in distances:
        total = total + swap(projected[d], "heads", d).astype(f32)
    return total.astype(bf16)


def solution(mesh):
    in_specs = (
        P(("groups", "heads"), None),
        P("mem"),
        P("mem", "heads"),
        P("mem", "heads"),
        P("mem", "heads"),
        P("heads", "mem"),
        P(("groups", "mem"), "heads", None, None),
        P(("groups", "mem"), "heads", None, None),
        P("groups", None),
        P("groups", None),
        P("groups"),
    )
    out_specs = P(("groups", "heads"), "mem")
    return jax.shard_map(shards, mesh=mesh, in_specs=in_specs, out_specs=out_specs, check_vma=False)
```

```python
import functools
import math

import jax
import jax.numpy as jnp
from jax import lax
from jax.experimental import pallas as pl
from jax.experimental.pallas import tpu as pltpu
from jax.sharding import PartitionSpec as P

NEG_FILL = -1e30
EPSILON = 1e-05
LANES = 128
MIB = 1 << 20
IN_VMEM = pl.BlockSpec(memory_space=pltpu.VMEM)
IN_SMEM = pl.BlockSpec(memory_space=pltpu.SMEM)


def swap(array, axis, distance):
    count = lax.axis_size(axis)
    return lax.ppermute(array, axis, [(i, i ^ distance) for i in range(count)])


def crossing(distance):
    return distance if distance == 1 else distance + 1


def swap_across(array, distance):
    heads = lax.axis_size("heads")
    count = lax.axis_size("mem") * heads
    pairs = [(i, i ^ heads ^ distance) for i in range(count)]
    return lax.ppermute(array, ("mem", "heads"), pairs)


def kernel_call(body, name, outs, ins, vmem_mib, flops, scratch=(), out_space=IN_VMEM):
    return pl.pallas_call(
        body,
        out_shape=outs,
        in_specs=ins,
        out_specs=out_space if isinstance(out_space, list) else jax.tree.map(lambda _: out_space, outs),
        scratch_shapes=list(scratch),
        name=name,
        compiler_params=pltpu.CompilerParams(vmem_limit_bytes=vmem_mib * MIB),
        cost_estimate=pl.CostEstimate(flops=int(flops), bytes_accessed=1024, transcendentals=0),
    )


def norm_body(hidden_hbm, own_ref, mate_ref, hidden_ref, sem):
    copy = pltpu.make_async_copy(hidden_hbm, hidden_ref, sem)
    copy.start()
    copy.wait()
    cols = own_ref.shape[1] - 3 * LANES
    mem = lax.axis_index("mem")
    hidden = hidden_ref[...].astype(jnp.float32)
    factor = lax.rsqrt(jnp.mean(hidden * hidden, axis=-1, keepdims=True) + EPSILON)
    wide = jnp.broadcast_to(factor, (hidden.shape[0], LANES))
    tail = jnp.concatenate(to_pieces(wide), axis=1)
    for ref, index in ((own_ref, mem), (mate_ref, lax.bitwise_xor(mem, 1))):
        start = pl.multiple_of(index * cols, cols)
        ref[:, :cols] = hidden_ref[:, pl.ds(start, cols)]
        ref[:, cols:] = tail


def select_body(
    chunk, steps, per_kv, table_ref, list_ref, lengths_ref, key_ref, chosen_ref, seen_ref, turned_ref
):
    pool, kv_heads, block, head_dim = key_ref.shape
    mem = lax.axis_index("mem")
    head_shard = lax.axis_index("heads")
    row_count, selected = list_ref.shape
    stride = chosen_ref.shape[0] // 3
    count = jnp.int32(0)
    for row in range(row_count):
        first = row * steps
        place = (lax.bitwise_xor(first // chunk, head_shard) * chunk + first % chunk) // steps
        length = lengths_ref[row]
        for i in range(selected):
            index = list_ref[row, i]
            slot = table_ref[row, index] - mem * pool
            chosen_ref[count] = slot
            chosen_ref[stride + count] = place
            chosen_ref[2 * stride + count] = length - index * block
            count += ((slot >= 0) & (slot < pool)).astype(jnp.int32)
    for c in range(stride - 1):
        live = c < count
        for at, blank in ((c, 0), (stride + c, row_count), (2 * stride + c, 0)):
            chosen_ref[at] = jnp.where(live, chosen_ref[at], blank)
        keys = key_ref[chosen_ref[c]]
        for g in range(kv_heads):
            turned_ref[c, :, g * block : (g + 1) * block] = keys[g].T

    def token_of(place):
        return lax.bitwise_xor(place // chunk, head_shard) * chunk + place % chunk

    tokens = row_count * steps
    heads = kv_heads * per_kv
    at = lax.broadcasted_iota(jnp.int32, seen_ref.shape, 0)
    query_token = token_of(at // heads)
    query_head = at % heads // per_kv
    place = at // heads // steps
    half = lax.axis_size("mem") // 2
    owner = place // (row_count // 2) * half + place % half
    lane = lax.broadcasted_iota(jnp.int32, seen_ref.shape, 1)
    key_head, key = lane // tokens, lane % tokens
    key_token = token_of(key)
    seen = (
        (query_head == key_head)
        & (query_token // steps == key_token // steps)
        & (key_token <= query_token)
        & (owner == mem)
    )
    seen_ref[...] = seen.astype(jnp.float32)


def pass_body(in_ref, out_ref):
    out_ref[...] = in_ref[...]


def project_body(places, tile, *refs):
    gain_ref, q_ref, k_ref, v_ref, out_ref = refs[len(places) :]
    chunks = [refs[places.index(i)][...].astype(jnp.float32) for i in range(len(places))]
    rows = jnp.concatenate(chunks, axis=0)
    cols = gain_ref.shape[0]
    gain = gain_ref[...].astype(jnp.float32).reshape(1, cols)
    tail = [rows[:, cols + i * LANES : cols + (i + 1) * LANES] for i in range(3)]
    factor = jnp.concatenate([from_pieces(tail)] * (cols // LANES), axis=1)
    rows = (rows[:, :cols] * factor * gain).astype(jnp.bfloat16)
    tokens = rows.shape[0]
    heads = q_ref.shape[1] // LANES
    head = 0
    for weight in (q_ref, k_ref, v_ref):
        width = min(tile, weight.shape[1])
        for col in range(0, weight.shape[1], width):
            product = jnp.dot(
                rows, weight[:, col : col + width], preferred_element_type=jnp.float32
            )
            for lane in range(0, width, LANES):
                columns = product[:, lane : lane + LANES]
                if head < heads:
                    out_ref[pl.ds(head, tokens, stride=heads)] = columns
                else:
                    out_ref[head * tokens : (head + 1) * tokens] = columns
                head += 1


def add_body(values, tokens, own_ref, other_ref, out_ref, *sent_refs):
    total = own_ref[...] + other_ref[...]
    out_ref[...] = total
    for ref in sent_refs:
        height = total.shape[0]
        top = jnp.max(jnp.abs(total[height - values :]), axis=0, keepdims=True)
        top = jnp.maximum(top, 1e-30)
        exponent = jnp.ceil(jnp.log(top) * (1 / math.log(2)))
        mem, half = lax.axis_index("mem"), lax.axis_size("mem") // 2
        theirs = pl.multiple_of((1 - mem // half) * (tokens // 2), tokens // 2)
        first = height - 2 * values
        ref[:first] = total[:first]
        at = first
        for block in range(first, height, tokens):
            rows = out_ref[pl.ds(block + theirs, tokens // 2)]
            if block >= height - values:
                rows = rows * jnp.exp2(-exponent)
            ref[at : at + tokens // 2] = rows
            at += tokens // 2
        ref[at:] = jnp.broadcast_to(exponent, (ref.shape[0] - at, LANES))


def add_sent(own_ref, sent_ref, values, tokens):
    height = own_ref.shape[0]
    first = height - 2 * values
    parts = [sent_ref[:first]]
    scale = jnp.exp2(sent_ref[first + values : first + values + 1])
    for at in range(first, first + values, tokens // 2):
        rows = sent_ref[at : at + tokens // 2]
        if at >= first + values // 2:
            rows = rows * scale
        parts += [rows, rows]
    return own_ref[...] + jnp.concatenate(parts, axis=0)


def split_dot(weights, values):
    high = weights.astype(jnp.bfloat16)
    low = (weights - high.astype(jnp.float32)).astype(jnp.bfloat16)
    both = jnp.dot(
        jnp.concatenate([high, low], axis=0), values, preferred_element_type=jnp.float32
    )
    return both[: weights.shape[0]] + both[weights.shape[0] :]


def to_pieces(rows):
    pieces = []
    for _ in range(3):
        pieces.append(rows.astype(jnp.bfloat16))
        rows = rows - pieces[-1].astype(jnp.float32)
    return pieces


def from_pieces(pieces):
    high, middle, low = [piece.astype(jnp.float32) for piece in pieces]
    return low + middle + high


def group_lanes(query_count):
    lane = lax.broadcasted_iota(jnp.int32, (query_count, LANES), 1)
    row = lax.broadcasted_iota(jnp.int32, (query_count, LANES), 0)
    return lane - row


def pack_columns(column, query_count):
    per_row = LANES // query_count
    offset = group_lanes(query_count)
    groups = column.shape[0] // query_count
    rows = []
    for first in range(0, groups, per_row):
        row = jnp.zeros((query_count, LANES), jnp.float32)
        for i in range(min(per_row, groups - first)):
            at = (first + i) * query_count
            row = jnp.where(offset == i * query_count, column[at : at + query_count], row)
        rows.append(jnp.sum(row, axis=0, keepdims=True))
    return rows


def unpack_column(row, place, query_count):
    spread = jnp.broadcast_to(row, (query_count, LANES))
    picked = jnp.where(group_lanes(query_count) == place * query_count, spread, 0.0)
    return jnp.sum(picked, axis=1, keepdims=True)


def attend_body(
    scale,
    heads,
    query_count,
    chosen_ref,
    seen_ref,
    own_ref,
    other_ref,
    turned_ref,
    value_ref,
    out_ref,
    query_ref,
    score_ref,
    total_ref,
    accum_ref,
    *peak_refs,
):
    row_count, row_height, head_dim = query_ref.shape
    row_count -= 1
    kv_heads = value_ref.shape[1]
    capacity = score_ref.shape[0]
    height = row_count * row_height
    contract_last = (((1,), (1,)), ((), ()))

    values = (own_ref.shape[0] - height) // 2
    projected = add_sent(own_ref, other_ref, values, values // kv_heads).astype(jnp.bfloat16)
    queries = projected[:height]
    query_ref[:row_count] = queries.reshape(row_count, row_height, head_dim)
    query_ref[row_count] = jnp.zeros((row_height, head_dim), jnp.bfloat16)
    fresh = projected[height:]
    count = fresh.shape[0] // 2
    spare = jnp.zeros((LANES - count, head_dim), jnp.bfloat16)
    seen = seen_ref[...] > 0
    fresh_score = lax.dot_general(
        queries,
        jnp.concatenate([fresh[:count], spare], axis=0),
        contract_last,
        preferred_element_type=jnp.float32,
    )
    fresh_score = jnp.where(seen, fresh_score * scale, NEG_FILL)
    peak_ref = peak_refs[0]
    peak_ref[:row_count] = fresh_score.reshape(row_count, row_height, LANES)
    peak_ref[row_count] = jnp.full((row_height, LANES), NEG_FILL, jnp.float32)
    for ref in peak_refs[1:]:
        ref[...] = jnp.full(ref.shape, NEG_FILL, jnp.float32)
    stride = chosen_ref.shape[0] // 3

    lane = lax.broadcasted_iota(jnp.int32, (row_height, LANES), 1)
    head_of = lax.broadcasted_iota(jnp.int32, (row_height, LANES), 0) % heads // (heads // kv_heads)
    for c in range(capacity):
        slot, row, valid = (chosen_ref[i * stride + c] for i in range(3))
        every = jnp.dot(
            query_ref[row],
            turned_ref[c],
            preferred_element_type=jnp.float32,
        )
        score = every[:, :LANES]
        for g in range(1, kv_heads):
            score = jnp.where(head_of == g, every[:, g * LANES : (g + 1) * LANES], score)
        score = jnp.where(lane < valid, score * scale, NEG_FILL)
        score_ref[c] = score
        ref = peak_refs[c % len(peak_refs)]
        ref[row] = jnp.maximum(ref[row], score)

    peak = functools.reduce(jnp.maximum, [ref[:row_count] for ref in peak_refs])
    peak = jnp.max(peak.reshape(height, LANES), axis=1, keepdims=True)
    peak = jnp.broadcast_to(peak, (height, LANES))
    peak_ref[:row_count] = peak.reshape(row_count, row_height, LANES)
    weights = jnp.where(seen, jnp.exp(fresh_score - peak), 0.0)
    total_ref[:row_count] = weights.reshape(row_count, row_height, LANES)
    total_ref[row_count] = jnp.zeros((row_height, LANES), jnp.float32)
    accum = split_dot(weights, jnp.concatenate([fresh[count:], spare], axis=0))
    accum_ref[:row_count] = accum.reshape(row_count, row_height, head_dim)
    accum_ref[row_count] = jnp.zeros((row_height, head_dim), jnp.float32)

    for c in range(capacity):
        slot, row = chosen_ref[c], chosen_ref[stride + c]
        weights = jnp.exp(score_ref[c] - peak_ref[row])
        total_ref[row] += weights
        spread = [jnp.where(head_of == g, weights, 0.0) for g in range(kv_heads)]
        accum_ref[row] += split_dot(
            jnp.concatenate(spread, axis=1), value_ref[slot].reshape(kv_heads * LANES, head_dim)
        )

    total = jnp.sum(total_ref[:row_count].reshape(height, LANES), axis=1, keepdims=True)
    total = jnp.broadcast_to(total, (height, LANES))
    out_ref[:height] = accum_ref[:row_count].reshape(height, head_dim)
    packed = pack_columns(peak, query_count) + pack_columns(total, query_count)
    spare = out_ref.shape[0] - height - len(packed)
    packed.append(jnp.zeros((spare, LANES), jnp.float32))
    out_ref[height:] = jnp.concatenate(packed, axis=0)


def state_rows(groups, query_count):
    return -(-groups // (LANES // query_count))


def merge_states(query_count, groups, last, own_ref, other_ref):
    per_row = LANES // query_count
    height = groups * query_count
    rows = state_rows(groups, query_count)
    own_peak, own_total = (own_ref[height + i * rows : height + (i + 1) * rows] for i in range(2))
    if other_ref.dtype == jnp.bfloat16:
        tail = other_ref[height:]
        pieces = [tail[i * rows : (i + 1) * rows] for i in range(6)]
        other_peak, other_total = from_pieces(pieces[:3]), from_pieces(pieces[3:])
    else:
        other_peak, other_total = (
            other_ref[height + i * rows : height + (i + 1) * rows] for i in range(2)
        )
    peak = jnp.maximum(own_peak, other_peak)
    own_factor, other_factor = jnp.exp(own_peak - peak), jnp.exp(other_peak - peak)
    total = own_total * own_factor + other_total * other_factor
    if last:
        own_factor, other_factor = own_factor / total, other_factor / total
    values = []
    for group in range(groups):
        row, place = divmod(group, per_row)
        at = slice(group * query_count, (group + 1) * query_count)
        values.append(
            own_ref[at] * unpack_column(own_factor[row : row + 1], place, query_count)
            + other_ref[at].astype(jnp.float32)
            * unpack_column(other_factor[row : row + 1], place, query_count)
        )
    return peak, total, values


def combine_body(query_count, groups, own_ref, other_ref, *out_refs):
    height = groups * query_count
    peak, total, values = merge_states(query_count, groups, False, own_ref, other_ref)
    for ref in out_refs:
        tail = [peak, total]
        if ref.dtype == jnp.bfloat16:
            tail = to_pieces(peak) + to_pieces(total)
        spare = ref.shape[0] - height - len(tail) * peak.shape[0]
        tail.append(jnp.zeros((spare, LANES), ref.dtype))
        ref[height:] = jnp.concatenate(tail, axis=0)
        for group, value in enumerate(values):
            ref[group * query_count : (group + 1) * query_count] = value.astype(ref.dtype)


def output_body(query_count, tile, own_ref, other_ref, weight_ref, *refs):
    out_refs, wide_ref = refs[:-1], refs[-1]
    heads = weight_ref.shape[0] // LANES
    tokens = wide_ref.shape[0] // heads
    groups = wide_ref.shape[0] // query_count
    _, _, values = merge_states(query_count, groups, True, own_ref, other_ref)
    for group, value in enumerate(values):
        wide_ref[group * query_count : (group + 1) * query_count] = value
    rows = [wide_ref[pl.ds(head, tokens, stride=heads)] for head in range(heads)]
    rows = jnp.concatenate(rows, axis=1).astype(jnp.bfloat16)
    chunk = out_refs[0].shape[0]
    for col in range(0, weight_ref.shape[1], tile):
        product = jnp.dot(
            rows, weight_ref[:, col : col + tile], preferred_element_type=jnp.float32
        )
        for i, out_ref in enumerate(out_refs):
            out_ref[:, col : col + tile] = product[i * chunk : (i + 1) * chunk].astype(out_ref.dtype)


def shards(
    hidden,
    norm_gain,
    q_weight,
    k_weight,
    v_weight,
    o_weight,
    k_cache,
    v_cache,
    page_table,
    attend_list,
    lengths,
):
    mem_count, head_count = lax.axis_size("mem"), lax.axis_size("heads")
    chunk = hidden.shape[0]
    feature_cols = norm_gain.shape[0]
    query_cols, value_cols = q_weight.shape[1], k_weight.shape[1]
    pool, kv_heads, block, head_dim = k_cache.shape
    row_count, selected = attend_list.shape
    token_count = chunk * head_count
    steps = token_count // row_count
    per_kv = query_cols // head_dim // kv_heads
    query_count = steps * per_kv
    capacity = 2 * row_count * selected // mem_count
    groups = row_count * kv_heads
    height = groups * query_count
    f32, bf16 = jnp.float32, jnp.bfloat16

    own, mate = kernel_call(
        norm_body,
        "norm",
        [jax.ShapeDtypeStruct((chunk, feature_cols + 3 * LANES), bf16)] * 2,
        [pl.BlockSpec(memory_space=pltpu.HBM)],
        2,
        1,
        [pltpu.VMEM(hidden.shape, bf16), pltpu.SemaphoreType.DMA],
    )(pltpu.with_memory_space_constraint(hidden, pltpu.HBM))
    mate = kernel_call(
        pass_body,
        "pass",
        jax.ShapeDtypeStruct(mate.shape, bf16),
        [IN_VMEM],
        1,
        1e10,
    )(mate)
    distances = [*range(2, head_count), 1]
    gathered = distances[::-1]
    pieces = [own] + [swap_across(mate, d) for d in gathered]

    chosen, seen, turned = kernel_call(
        functools.partial(select_body, chunk, steps, per_kv),
        "select",
        [
            pltpu.SMEM((3 * (capacity + 1),), jnp.int32),
            jax.ShapeDtypeStruct((height, LANES), f32),
            jax.ShapeDtypeStruct((capacity, head_dim, kv_heads * block), bf16),
        ],
        [IN_SMEM] * 3 + [IN_VMEM],
        4,
        1e10,
        out_space=[IN_SMEM, IN_VMEM, IN_VMEM],
    )(page_table, attend_list, lengths, k_cache)

    width = query_cols + 2 * value_cols
    summed = kernel_call(
        functools.partial(project_body, (0, *gathered), 512),
        "project",
        jax.ShapeDtypeStruct((width // LANES * token_count, LANES), f32),
        [IN_VMEM] * (head_count + 4),
        4,
        2 * token_count * feature_cols * width,
    )(*pieces, norm_gain, q_weight, k_weight, v_weight)
    sent = summed
    distance = 1
    while 2 * distance < mem_count:
        outs = [jax.ShapeDtypeStruct(summed.shape, f32)]
        if 4 * distance == mem_count:
            outs.append(jax.ShapeDtypeStruct((summed.shape[0] - kv_heads * token_count + 16, LANES), f32))
        added = kernel_call(
            functools.partial(add_body, kv_heads * token_count, token_count),
            "add",
            outs,
            [IN_VMEM] * 2,
            2,
            1e10,
        )(summed, swap(sent, "mem", crossing(distance)))
        summed, sent = added[0], added[-1]
        distance *= 2

    state = (kv_heads * query_count, LANES)
    partial = kernel_call(
        functools.partial(attend_body, head_dim ** (-0.5), kv_heads * per_kv, query_count),
        "attend",
        jax.ShapeDtypeStruct((height + 8, LANES), f32),
        [IN_SMEM] + [IN_VMEM] * 5,
        4,
        1e10,
        [pltpu.VMEM((row_count + 1, *state), bf16), pltpu.VMEM((capacity, *state), f32)]
        + [pltpu.VMEM((row_count + 1, *state), f32)] * 4,
    )(
        pltpu.with_memory_space_constraint(chosen, pltpu.SMEM),
        seen,
        summed,
        swap(sent.astype(jnp.float16), "mem", crossing(distance)).astype(f32),
        turned,
        v_cache,
    )

    sent = partial
    distance = 1
    while 2 * distance < mem_count:
        outs = [jax.ShapeDtypeStruct(partial.shape, f32)]
        if 4 * distance == mem_count:
            pad = -(-6 * state_rows(groups, query_count) // 16) * 16
            outs.append(jax.ShapeDtypeStruct((height + pad, LANES), bf16))
        merged = kernel_call(
            functools.partial(combine_body, query_count, groups),
            "combine",
            outs,
            [IN_VMEM] * 2,
            2,
            1e10,
        )(partial, swap(sent, "mem", crossing(distance)))
        partial, sent = merged[0], merged[-1]
        distance *= 2

    out_cols = o_weight.shape[1]
    projected = kernel_call(
        functools.partial(output_body, query_count, min(512, out_cols)),
        "output",
        [jax.ShapeDtypeStruct((chunk, out_cols), bf16 if i else f32) for i in range(head_count)],
        [IN_VMEM] * 3,
        4,
        2 * token_count * query_cols * out_cols,
        [pltpu.VMEM((query_cols // LANES * token_count, LANES), f32)],
    )(partial, swap(sent, "mem", crossing(distance)), o_weight)
    total = projected[0]
    for d in distances:
        total = total + swap(projected[d], "heads", d).astype(f32)
    return total.astype(bf16)


def solution(mesh):
    in_specs = (
        P(("groups", "heads"), None),
        P("mem"),
        P("mem", "heads"),
        P("mem", "heads"),
        P("mem", "heads"),
        P("heads", "mem"),
        P(("groups", "mem"), "heads", None, None),
        P(("groups", "mem"), "heads", None, None),
        P("groups", None),
        P("groups", None),
        P("groups"),
    )
    out_specs = P(("groups", "heads"), "mem")
    return jax.shard_map(shards, mesh=mesh, in_specs=in_specs, out_specs=out_specs, check_vma=False)
```

```python
import functools
import math

import jax
import jax.numpy as jnp
from jax import lax
from jax.experimental import pallas as pl
from jax.experimental.pallas import tpu as pltpu
from jax.sharding import PartitionSpec as P

NEG_FILL = -1e30
EPSILON = 1e-05
LANES = 128
MIB = 1 << 20
IN_VMEM = pl.BlockSpec(memory_space=pltpu.VMEM)
IN_SMEM = pl.BlockSpec(memory_space=pltpu.SMEM)


def swap(array, axis, distance):
    count = lax.axis_size(axis)
    return lax.ppermute(array, axis, [(i, i ^ distance) for i in range(count)])


def crossing(distance):
    return distance if distance == 1 else distance + 1


def swap_across(array, distance):
    heads = lax.axis_size("heads")
    count = lax.axis_size("mem") * heads
    pairs = [(i, i ^ heads ^ distance) for i in range(count)]
    return lax.ppermute(array, ("mem", "heads"), pairs)


def kernel_call(body, name, outs, ins, vmem_mib, flops, scratch=(), out_space=IN_VMEM):
    return pl.pallas_call(
        body,
        out_shape=outs,
        in_specs=ins,
        out_specs=out_space if isinstance(out_space, list) else jax.tree.map(lambda _: out_space, outs),
        scratch_shapes=list(scratch),
        name=name,
        compiler_params=pltpu.CompilerParams(vmem_limit_bytes=vmem_mib * MIB),
        cost_estimate=pl.CostEstimate(flops=int(flops), bytes_accessed=1024, transcendentals=0),
    )


def norm_body(hidden_hbm, own_ref, mate_ref, hidden_ref, sem):
    copy = pltpu.make_async_copy(hidden_hbm, hidden_ref, sem)
    copy.start()
    copy.wait()
    cols = own_ref.shape[1] - 3 * LANES
    mem = lax.axis_index("mem")
    hidden = hidden_ref[...].astype(jnp.float32)
    factor = lax.rsqrt(jnp.mean(hidden * hidden, axis=-1, keepdims=True) + EPSILON)
    wide = jnp.broadcast_to(factor, (hidden.shape[0], LANES))
    tail = jnp.concatenate(to_pieces(wide), axis=1)
    for ref, index in ((own_ref, mem), (mate_ref, lax.bitwise_xor(mem, 1))):
        start = pl.multiple_of(index * cols, cols)
        ref[:, :cols] = hidden_ref[:, pl.ds(start, cols)]
        ref[:, cols:] = tail


def select_body(
    chunk, steps, per_kv, table_ref, list_ref, lengths_ref, key_ref, chosen_ref, seen_ref, turned_ref
):
    pool, kv_heads, block, head_dim = key_ref.shape
    mem = lax.axis_index("mem")
    head_shard = lax.axis_index("heads")
    row_count, selected = list_ref.shape
    stride = chosen_ref.shape[0] // 3
    count = jnp.int32(0)
    for row in range(row_count):
        first = row * steps
        place = (lax.bitwise_xor(first // chunk, head_shard) * chunk + first % chunk) // steps
        length = lengths_ref[row]
        for i in range(selected):
            index = list_ref[row, i]
            slot = table_ref[row, index] - mem * pool
            chosen_ref[count] = slot
            chosen_ref[stride + count] = place
            chosen_ref[2 * stride + count] = length - index * block
            count += ((slot >= 0) & (slot < pool)).astype(jnp.int32)
    for c in range(stride - 1):
        live = c < count
        for at, blank in ((c, 0), (stride + c, row_count), (2 * stride + c, 0)):
            chosen_ref[at] = jnp.where(live, chosen_ref[at], blank)
        keys = key_ref[chosen_ref[c]]
        for g in range(kv_heads):
            turned_ref[c, :, g * block : (g + 1) * block] = keys[g].T

    def token_of(place):
        return lax.bitwise_xor(place // chunk, head_shard) * chunk + place % chunk

    tokens = row_count * steps
    heads = kv_heads * per_kv
    at = lax.broadcasted_iota(jnp.int32, seen_ref.shape, 0)
    query_token = token_of(at // heads)
    query_head = at % heads // per_kv
    place = at // heads // steps
    half = lax.axis_size("mem") // 2
    owner = place // (row_count // 2) * half + place % half
    lane = lax.broadcasted_iota(jnp.int32, seen_ref.shape, 1)
    key_head, key = lane // tokens, lane % tokens
    key_token = token_of(key)
    seen = (
        (query_head == key_head)
        & (query_token // steps == key_token // steps)
        & (key_token <= query_token)
        & (owner == mem)
    )
    seen_ref[...] = seen.astype(jnp.float32)


def pass_body(in_ref, out_ref):
    out_ref[...] = in_ref[...]


def project_body(places, tile, *refs):
    gain_ref, q_ref, k_ref, v_ref, out_ref = refs[len(places) :]
    chunks = [refs[places.index(i)][...].astype(jnp.float32) for i in range(len(places))]
    rows = jnp.concatenate(chunks, axis=0)
    cols = gain_ref.shape[0]
    gain = gain_ref[...].astype(jnp.float32).reshape(1, cols)
    tail = [rows[:, cols + i * LANES : cols + (i + 1) * LANES] for i in range(3)]
    factor = jnp.concatenate([from_pieces(tail)] * (cols // LANES), axis=1)
    rows = (rows[:, :cols] * factor * gain).astype(jnp.bfloat16)
    tokens = rows.shape[0]
    heads = q_ref.shape[1] // LANES
    head = 0
    for weight in (q_ref, k_ref, v_ref):
        width = min(tile, weight.shape[1])
        for col in range(0, weight.shape[1], width):
            product = jnp.dot(
                rows, weight[:, col : col + width], preferred_element_type=jnp.float32
            )
            for lane in range(0, width, LANES):
                columns = product[:, lane : lane + LANES]
                if head < heads:
                    out_ref[pl.ds(head, tokens, stride=heads)] = columns
                else:
                    out_ref[head * tokens : (head + 1) * tokens] = columns
                head += 1


def add_body(values, tokens, own_ref, other_ref, out_ref, *sent_refs):
    total = own_ref[...] + other_ref[...]
    out_ref[...] = total
    for ref in sent_refs:
        height = total.shape[0]
        top = jnp.max(jnp.abs(total[height - values :]), axis=0, keepdims=True)
        top = jnp.maximum(top, 1e-30)
        exponent = jnp.ceil(jnp.log(top) * (1 / math.log(2)))
        mem, half = lax.axis_index("mem"), lax.axis_size("mem") // 2
        theirs = pl.multiple_of((1 - mem // half) * (tokens // 2), tokens // 2)
        first = height - 2 * values
        ref[:first] = total[:first]
        at = first
        for block in range(first, height, tokens):
            rows = out_ref[pl.ds(block + theirs, tokens // 2)]
            if block >= height - values:
                rows = rows * jnp.exp2(-exponent)
            ref[at : at + tokens // 2] = rows
            at += tokens // 2
        ref[at:] = jnp.broadcast_to(exponent, (ref.shape[0] - at, LANES))


def add_sent(own_ref, sent_ref, values, tokens):
    height = own_ref.shape[0]
    first = height - 2 * values
    parts = [sent_ref[:first]]
    scale = jnp.exp2(sent_ref[first + values : first + values + 1])
    for at in range(first, first + values, tokens // 2):
        rows = sent_ref[at : at + tokens // 2]
        if at >= first + values // 2:
            rows = rows * scale
        parts += [rows, rows]
    return own_ref[...] + jnp.concatenate(parts, axis=0)


def split_dot(weights, values):
    high = weights.astype(jnp.bfloat16)
    low = (weights - high.astype(jnp.float32)).astype(jnp.bfloat16)
    both = jnp.dot(
        jnp.concatenate([high, low], axis=0), values, preferred_element_type=jnp.float32
    )
    return both[: weights.shape[0]] + both[weights.shape[0] :]


def to_pieces(rows):
    pieces = []
    for _ in range(3):
        pieces.append(rows.astype(jnp.bfloat16))
        rows = rows - pieces[-1].astype(jnp.float32)
    return pieces


def from_pieces(pieces):
    high, middle, low = [piece.astype(jnp.float32) for piece in pieces]
    return low + middle + high


def group_lanes(query_count):
    lane = lax.broadcasted_iota(jnp.int32, (query_count, LANES), 1)
    row = lax.broadcasted_iota(jnp.int32, (query_count, LANES), 0)
    return lane - row


def pack_columns(column, query_count):
    per_row = LANES // query_count
    offset = group_lanes(query_count)
    groups = column.shape[0] // query_count
    rows = []
    for first in range(0, groups, per_row):
        row = jnp.zeros((query_count, LANES), jnp.float32)
        for i in range(min(per_row, groups - first)):
            at = (first + i) * query_count
            row = jnp.where(offset == i * query_count, column[at : at + query_count], row)
        rows.append(jnp.sum(row, axis=0, keepdims=True))
    return rows


def unpack_column(row, place, query_count):
    spread = jnp.broadcast_to(row, (query_count, LANES))
    picked = jnp.where(group_lanes(query_count) == place * query_count, spread, 0.0)
    return jnp.sum(picked, axis=1, keepdims=True)


def attend_body(
    scale,
    heads,
    query_count,
    chosen_ref,
    seen_ref,
    own_ref,
    other_ref,
    turned_ref,
    value_ref,
    out_ref,
    query_ref,
    score_ref,
    total_ref,
    accum_ref,
    *peak_refs,
):
    row_count, row_height, head_dim = query_ref.shape
    row_count -= 1
    kv_heads = value_ref.shape[1]
    capacity = score_ref.shape[0]
    height = row_count * row_height
    contract_last = (((1,), (1,)), ((), ()))

    values = (own_ref.shape[0] - height) // 2
    projected = add_sent(own_ref, other_ref, values, values // kv_heads).astype(jnp.bfloat16)
    queries = projected[:height]
    query_ref[:row_count] = queries.reshape(row_count, row_height, head_dim)
    query_ref[row_count] = jnp.zeros((row_height, head_dim), jnp.bfloat16)
    fresh = projected[height:]
    count = fresh.shape[0] // 2
    spare = jnp.zeros((LANES - count, head_dim), jnp.bfloat16)
    seen = seen_ref[...] > 0
    fresh_score = lax.dot_general(
        queries,
        jnp.concatenate([fresh[:count], spare], axis=0),
        contract_last,
        preferred_element_type=jnp.float32,
    )
    fresh_score = jnp.where(seen, fresh_score * scale, NEG_FILL)
    peak_ref = peak_refs[0]
    peak_ref[:row_count] = fresh_score.reshape(row_count, row_height, LANES)
    peak_ref[row_count] = jnp.full((row_height, LANES), NEG_FILL, jnp.float32)
    for ref in peak_refs[1:]:
        ref[...] = jnp.full(ref.shape, NEG_FILL, jnp.float32)
    stride = chosen_ref.shape[0] // 3

    lane = lax.broadcasted_iota(jnp.int32, (row_height, LANES), 1)
    head_of = lax.broadcasted_iota(jnp.int32, (row_height, LANES), 0) % heads // (heads // kv_heads)
    for c in range(capacity):
        slot, row, valid = (chosen_ref[i * stride + c] for i in range(3))
        every = jnp.dot(
            query_ref[row],
            turned_ref[c],
            preferred_element_type=jnp.float32,
        )
        score = every[:, :LANES]
        for g in range(1, kv_heads):
            score = jnp.where(head_of == g, every[:, g * LANES : (g + 1) * LANES], score)
        score = jnp.where(lane < valid, score * scale, NEG_FILL)
        score_ref[c] = score
        ref = peak_refs[c % len(peak_refs)]
        ref[row] = jnp.maximum(ref[row], score)

    peak = functools.reduce(jnp.maximum, [ref[:row_count] for ref in peak_refs])
    peak = jnp.max(peak.reshape(height, LANES), axis=1, keepdims=True)
    peak = jnp.broadcast_to(peak, (height, LANES))
    peak_ref[:row_count] = peak.reshape(row_count, row_height, LANES)
    weights = jnp.where(seen, jnp.exp(fresh_score - peak), 0.0)
    total_ref[:row_count] = weights.reshape(row_count, row_height, LANES)
    total_ref[row_count] = jnp.zeros((row_height, LANES), jnp.float32)
    accum = split_dot(weights, jnp.concatenate([fresh[count:], spare], axis=0))
    accum_ref[:row_count] = accum.reshape(row_count, row_height, head_dim)
    accum_ref[row_count] = jnp.zeros((row_height, head_dim), jnp.float32)

    for c in range(capacity):
        slot, row = chosen_ref[c], chosen_ref[stride + c]
        weights = jnp.exp(score_ref[c] - peak_ref[row])
        total_ref[row] += weights
        spread = [jnp.where(head_of == g, weights, 0.0) for g in range(kv_heads)]
        accum_ref[row] += split_dot(
            jnp.concatenate(spread, axis=1), value_ref[slot].reshape(kv_heads * LANES, head_dim)
        )

    total = jnp.sum(total_ref[:row_count].reshape(height, LANES), axis=1, keepdims=True)
    total = jnp.broadcast_to(total, (height, LANES))
    out_ref[:height] = accum_ref[:row_count].reshape(height, head_dim)
    packed = pack_columns(peak, query_count) + pack_columns(total, query_count)
    spare = out_ref.shape[0] - height - len(packed)
    packed.append(jnp.zeros((spare, LANES), jnp.float32))
    out_ref[height:] = jnp.concatenate(packed, axis=0)


def state_rows(groups, query_count):
    return -(-groups // (LANES // query_count))


def merge_states(query_count, groups, last, own_ref, other_ref):
    per_row = LANES // query_count
    height = groups * query_count
    rows = state_rows(groups, query_count)
    own_peak, own_total = (own_ref[height + i * rows : height + (i + 1) * rows] for i in range(2))
    if other_ref.dtype == jnp.bfloat16:
        tail = other_ref[height:]
        pieces = [tail[i * rows : (i + 1) * rows] for i in range(6)]
        other_peak, other_total = from_pieces(pieces[:3]), from_pieces(pieces[3:])
    else:
        other_peak, other_total = (
            other_ref[height + i * rows : height + (i + 1) * rows] for i in range(2)
        )
    peak = jnp.maximum(own_peak, other_peak)
    own_factor, other_factor = jnp.exp(own_peak - peak), jnp.exp(other_peak - peak)
    total = own_total * own_factor + other_total * other_factor
    if last:
        own_factor, other_factor = own_factor / total, other_factor / total
    values = []
    for group in range(groups):
        row, place = divmod(group, per_row)
        at = slice(group * query_count, (group + 1) * query_count)
        values.append(
            own_ref[at] * unpack_column(own_factor[row : row + 1], place, query_count)
            + other_ref[at].astype(jnp.float32)
            * unpack_column(other_factor[row : row + 1], place, query_count)
        )
    return peak, total, values


def combine_body(query_count, groups, own_ref, other_ref, *out_refs):
    height = groups * query_count
    peak, total, values = merge_states(query_count, groups, False, own_ref, other_ref)
    for ref in out_refs:
        tail = [peak, total]
        if ref.dtype == jnp.bfloat16:
            tail = to_pieces(peak) + to_pieces(total)
        spare = ref.shape[0] - height - len(tail) * peak.shape[0]
        tail.append(jnp.zeros((spare, LANES), ref.dtype))
        ref[height:] = jnp.concatenate(tail, axis=0)
        for group, value in enumerate(values):
            ref[group * query_count : (group + 1) * query_count] = value.astype(ref.dtype)


def output_body(query_count, tile, own_ref, other_ref, weight_ref, *refs):
    out_refs, wide_ref = refs[:-1], refs[-1]
    heads = weight_ref.shape[0] // LANES
    tokens = wide_ref.shape[0] // heads
    groups = wide_ref.shape[0] // query_count
    _, _, values = merge_states(query_count, groups, True, own_ref, other_ref)
    for group, value in enumerate(values):
        wide_ref[group * query_count : (group + 1) * query_count] = value
    rows = [wide_ref[pl.ds(head, tokens, stride=heads)] for head in range(heads)]
    rows = jnp.concatenate(rows, axis=1).astype(jnp.bfloat16)
    chunk = out_refs[0].shape[0]
    for col in range(0, weight_ref.shape[1], tile):
        product = jnp.dot(
            rows, weight_ref[:, col : col + tile], preferred_element_type=jnp.float32
        )
        for i, out_ref in enumerate(out_refs):
            out_ref[:, col : col + tile] = product[i * chunk : (i + 1) * chunk].astype(out_ref.dtype)


def shards(
    hidden,
    norm_gain,
    q_weight,
    k_weight,
    v_weight,
    o_weight,
    k_cache,
    v_cache,
    page_table,
    attend_list,
    lengths,
):
    mem_count, head_count = lax.axis_size("mem"), lax.axis_size("heads")
    chunk = hidden.shape[0]
    feature_cols = norm_gain.shape[0]
    query_cols, value_cols = q_weight.shape[1], k_weight.shape[1]
    pool, kv_heads, block, head_dim = k_cache.shape
    row_count, selected = attend_list.shape
    token_count = chunk * head_count
    steps = token_count // row_count
    per_kv = query_cols // head_dim // kv_heads
    query_count = steps * per_kv
    capacity = 2 * row_count * selected // mem_count
    groups = row_count * kv_heads
    height = groups * query_count
    f32, bf16 = jnp.float32, jnp.bfloat16

    own, mate = kernel_call(
        norm_body,
        "norm",
        [jax.ShapeDtypeStruct((chunk, feature_cols + 3 * LANES), bf16)] * 2,
        [pl.BlockSpec(memory_space=pltpu.HBM)],
        2,
        1,
        [pltpu.VMEM(hidden.shape, bf16), pltpu.SemaphoreType.DMA],
    )(pltpu.with_memory_space_constraint(hidden, pltpu.HBM))
    mate = kernel_call(
        pass_body,
        "pass",
        jax.ShapeDtypeStruct(mate.shape, bf16),
        [IN_VMEM],
        1,
        1e10,
    )(mate)
    distances = [*range(2, head_count), 1]
    gathered = distances[::-1]
    pieces = [own] + [swap_across(mate, d) for d in gathered]

    chosen, seen, turned = kernel_call(
        functools.partial(select_body, chunk, steps, per_kv),
        "select",
        [
            pltpu.SMEM((3 * (capacity + 1),), jnp.int32),
            jax.ShapeDtypeStruct((height, LANES), f32),
            jax.ShapeDtypeStruct((capacity, head_dim, kv_heads * block), bf16),
        ],
        [IN_SMEM] * 3 + [IN_VMEM],
        4,
        1e10,
        out_space=[IN_SMEM, IN_VMEM, IN_VMEM],
    )(page_table, attend_list, lengths, k_cache)

    width = query_cols + 2 * value_cols
    summed = kernel_call(
        functools.partial(project_body, (0, *gathered), 512),
        "project",
        jax.ShapeDtypeStruct((width // LANES * token_count, LANES), f32),
        [IN_VMEM] * (head_count + 4),
        4,
        2 * token_count * feature_cols * width,
    )(*pieces, norm_gain, q_weight, k_weight, v_weight)
    sent = summed
    distance = 1
    while 2 * distance < mem_count:
        outs = [jax.ShapeDtypeStruct(summed.shape, f32)]
        if 4 * distance == mem_count:
            outs.append(jax.ShapeDtypeStruct((summed.shape[0] - kv_heads * token_count + 16, LANES), f32))
        added = kernel_call(
            functools.partial(add_body, kv_heads * token_count, token_count),
            "add",
            outs,
            [IN_VMEM] * 2,
            2,
            1e10,
        )(summed, swap(sent, "mem", crossing(distance)))
        summed, sent = added[0], added[-1]
        distance *= 2

    state = (kv_heads * query_count, LANES)
    partial = kernel_call(
        functools.partial(attend_body, head_dim ** (-0.5), kv_heads * per_kv, query_count),
        "attend",
        jax.ShapeDtypeStruct((height + 8, LANES), f32),
        [IN_SMEM] + [IN_VMEM] * 5,
        4,
        1e10,
        [pltpu.VMEM((row_count + 1, *state), bf16), pltpu.VMEM((capacity, *state), f32)]
        + [pltpu.VMEM((row_count + 1, *state), f32)] * 4,
    )(
        pltpu.with_memory_space_constraint(chosen, pltpu.SMEM),
        seen,
        summed,
        swap(sent.astype(jnp.float16), "mem", crossing(distance)).astype(f32),
        turned,
        v_cache,
    )

    sent = partial
    distance = 1
    while 2 * distance < mem_count:
        outs = [jax.ShapeDtypeStruct(partial.shape, f32)]
        if 4 * distance == mem_count:
            pad = -(-6 * state_rows(groups, query_count) // 16) * 16
            outs.append(jax.ShapeDtypeStruct((height + pad, LANES), bf16))
        merged = kernel_call(
            functools.partial(combine_body, query_count, groups),
            "combine",
            outs,
            [IN_VMEM] * 2,
            2,
            1e10,
        )(partial, swap(sent, "mem", crossing(distance)))
        partial, sent = merged[0], merged[-1]
        distance *= 2

    out_cols = o_weight.shape[1]
    projected = kernel_call(
        functools.partial(output_body, query_count, min(512, out_cols)),
        "output",
        [jax.ShapeDtypeStruct((chunk, out_cols), bf16 if i else f32) for i in range(head_count)],
        [IN_VMEM] * 3,
        4,
        2 * token_count * query_cols * out_cols,
        [pltpu.VMEM((query_cols // LANES * token_count, LANES), f32)],
    )(partial, swap(sent, "mem", crossing(distance)), o_weight)
    total = projected[0]
    for d in range(head_count - 1, 0, -1):
        total = total + swap(projected[d], "heads", d).astype(f32)
    return total.astype(bf16)


def solution(mesh):
    in_specs = (
        P(("groups", "heads"), None),
        P("mem"),
        P("mem", "heads"),
        P("mem", "heads"),
        P("mem", "heads"),
        P("heads", "mem"),
        P(("groups", "mem"), "heads", None, None),
        P(("groups", "mem"), "heads", None, None),
        P("groups", None),
        P("groups", None),
        P("groups"),
    )
    out_specs = P(("groups", "heads"), "mem")
    return jax.shard_map(shards, mesh=mesh, in_specs=in_specs, out_specs=out_specs, check_vma=False)
```
